32 devices in a mesh: replica: 8 (over y, x, core), table: 4 (over z).
Axes of the slice: x: 2, y: 2, z: 4, core: 2. Of those that a mesh axis runs over, the one named last changes fastest.
Arguments:
- emb_table: float32 [4096, 128], P('table'), may hold values from -3 to 3
- row_accum: float32 [4096], P('table'), may hold values from 0.001 to 1
- look_rows: int32 [8, 4, 4, 4, 1248], P('replica', 'table'), may hold values from 0 to 1023
- live_counts: int32 [8, 4, 4], P('replica'), may hold values from 1 to 1248, 3328 in all within a row
- bag_order: int32 [8, 4, 3328], P('replica', 'table'), may hold values from 0 to 3327, each once within a row
- dense_emb: bfloat16 [4096, 128], P(('replica', 'table')), may hold values from -6 to 6
- labels: int32 [4096], P(('replica', 'table')), may hold values 0 or 1
- cross_in: bfloat16 [3456, 512], P('table'), may hold values from -0.109375 to 0.109375
- cross_out: bfloat16 [3456, 512], P('table'), may hold values from -0.25 to 0.25
- cross_bias: float32 [3456], replicated, may hold values from -3 to 3
- head_weight: float32 [3456], replicated, may hold values from -0.109375 to 0.109375
Outputs:
- logits: float32 [4096], P(('replica', 'table'))
- row_update: float32 [4096, 128], P('table')
- new_accum: float32 [4096], P('table')
The draws below stay inside these ranges and needn't reach their ends.
Inputs may be any that keep to these rules, and one draw needn't show every extreme that they name: `look_rows`: local row numbers within shard s; entries in unused slots are ignored. `live_counts`: for each replica and owner the counts over shards sum to 3328; for each of them some shard sends exactly 1248. `bag_order`: each of an owner's 3328 bags appears once.
All inputs are finite; a program needn't handle non-finite values. No bound on the sum of `labels` on one device may be relied on, other than what follows from the above.
Results may differ from the reference program's by a relative error of at most 0.0045.
Values may be sent and summed in bfloat16 or wider, within the bound.
No kernel may reach another device: no remote copies, remote signals or barrier semaphores. Data moves between devices by JAX's collectives and lax.ppermute only.
A program may use at most 64 MiB of HBM per device.

```python
import math
import jax
import jax.numpy as jnp
import numpy as np
from jax import lax

E = 128
RANK = 512
HOT = 4
ROWS_DEV = 1024
D = 3456
K = 3328
CAP = 1248
SAMPLES = 4096
VOCAB = 4096
N_REPLICA = 8
N_TABLE = 4


def touch_ends(array, rng, smallest, largest):
    longest = array.shape.index(max(array.shape))
    spots = []
    for shift in (0, 1):
        where = [jax.random.randint(jax.random.fold_in(rng, axis), (), 0, length) for axis, length in enumerate(array.shape)]
        where[longest] = (where[longest] + shift) % array.shape[longest]
        spots.append(tuple(where))
    return array.at[spots[0]].set(smallest).at[spots[1]].set(largest)


def shard_levels(rng, extent, cuts, least, high):
    def one(dim, parts):
        draws = jax.random.uniform(jax.random.fold_in(jax.random.fold_in(rng, 6), dim), (parts,), jnp.float32, least / len(cuts), high / len(cuts))
        return jnp.repeat(jnp.exp(draws), extent[dim] // parts).reshape((-1,) + (1,) * (len(extent) - dim - 1))

    factor_of = one(*cuts[0])
    for cut in cuts[1:]:
        factor_of = factor_of * one(*cut)
    return factor_of


def rank_bounds(amount, lean):
    weights = [(1 << 20) // math.isqrt(standing ** lean) + 1 for standing in range(1, amount + 1)]
    width = 1 + sum(weights) // (1 << 30)
    return np.cumsum(np.array([max(1, weight // width) for weight in weights]))


def ranked(stream_key, extent, number_of, slope):
    grid = rank_bounds(number_of, slope)
    pick = jax.random.randint(jax.random.fold_in(stream_key, 1), extent, 0, int(grid[number_of - 1]))
    standing = jnp.searchsorted(jnp.asarray(grid, jnp.int32), pick, side="right")
    return jax.random.permutation(jax.random.fold_in(stream_key, 2), number_of)[standing].astype(jnp.int32)


def profile(number_of, total, limit, slope):
    weights = [(1 << 20) // math.isqrt(grade ** slope) + 1 for grade in range(2, number_of + 1)]
    surplus, counts = total - limit - (number_of - 1), [1] * (number_of - 1)
    while surplus > 0:
        candidates = [i for i in range(number_of - 1) if counts[i] < limit]
        pool, remaining = sum([weights[i] for i in candidates]), surplus
        for i in candidates:
            more = min(limit - counts[i], max(1, remaining * weights[i] // pool), surplus)
            counts[i] = counts[i] + more
            surplus = surplus - more
    return np.array([limit] + counts)


def ragged(own_key, number_of, total, reach, slope):
    if number_of == 2:
        one = jax.random.randint(own_key, (), max(1, total - reach), min(reach, total - 1) + 1)
        return jnp.stack([one, total - one])
    tallies = jnp.asarray(profile(number_of, total, reach, slope), jnp.int32)
    couples = (number_of - 1) // 2
    donor, sink = tallies[1:1 + 2 * couples:2], tallies[2:2 + 2 * couples:2]
    slack = jnp.minimum(donor - 1, reach - sink)
    moved = jax.random.randint(jax.random.fold_in(own_key, 1), (couples,), 0, 1 << 20) % (slack + 1)
    tallies = tallies.at[1:1 + 2 * couples:2].set(donor - moved).at[2:2 + 2 * couples:2].set(sink + moved)
    return tallies[jax.random.permutation(jax.random.fold_in(own_key, 2), number_of)]


def centred(own_key, dims, width, bound, cuts=(), held_as=jnp.bfloat16):
    values = jax.random.normal(own_key, dims, jnp.float32) * width
    if len(cuts) > 0:
        values = shard_levels(own_key, dims, cuts, -0.22, 0.18) * values
    return jnp.clip(values, min=-bound, max=bound).astype(held_as)


def setup_inputs(seed: int = 0) -> dict:
    keys = jax.random.split(jax.random.key(seed), 12)
    emb_table = centred(keys[0], (VOCAB, E), 0.5, 3.0, ((0, 4),), jnp.float32)
    row_accum = jnp.clip(jnp.exp(math.log(1.0) - 6.9077552 * jax.random.uniform(keys[1], (VOCAB,), jnp.float32) ** shard_levels(keys[1], (VOCAB,), ((0, 4),), -0.2, 0.2)), 0.001, 1.0)
    look_rows = touch_ends(ranked(keys[2], (N_REPLICA, N_TABLE, N_TABLE, HOT, CAP), ROWS_DEV, 2), jax.random.fold_in(keys[2], 3), 0, ROWS_DEV - 1).astype(jnp.int32)
    live_counts = jax.vmap(lambda own: ragged(own, N_TABLE, K, CAP, 2))(jax.random.split(keys[3], N_REPLICA * N_TABLE)).reshape((N_REPLICA, N_TABLE, N_TABLE)).astype(jnp.int32)
    bag_order = jax.vmap(lambda own: jax.random.permutation(own, K))(jax.random.split(keys[4], N_REPLICA * N_TABLE)).reshape((N_REPLICA, N_TABLE, K)).astype(jnp.int32)
    dense_emb = centred(keys[5], (SAMPLES, E), 1.0, 6.0, ((0, 32),))
    labels = touch_ends((jax.random.randint(keys[6], (SAMPLES,), 0, 4) < 1).astype(jnp.int32), jax.random.fold_in(keys[6], 1), 0, 1)
    cross_in = centred(keys[7], (D, RANK), D ** -0.5, 0.109375, ((0, 4),))
    cross_out = centred(keys[8], (D, RANK), RANK ** -0.5, 0.25, ((0, 4),))
    cross_bias = centred(keys[9], (D,), 0.5, 3.0, (), jnp.float32)
    head_weight = centred(keys[10], (D,), D ** -0.5, 0.109375, (), jnp.float32)
    return {"emb_table": emb_table, "row_accum": row_accum, "look_rows": look_rows, "live_counts": live_counts, "bag_order": bag_order, "dense_emb": dense_emb, "labels": labels, "cross_in": cross_in, "cross_out": cross_out, "cross_bias": cross_bias, "head_weight": head_weight}


EPSILON = 1e-08

def bag_sources(live_row, permute, capacity):
    bag_count = permute.shape[0]
    slot_ends = jnp.cumsum(live_row).astype(jnp.int32)
    counter = jnp.arange(bag_count, dtype=jnp.int32)
    passed = (counter[:, None] >= slot_ends[None, :]).astype(jnp.int32)
    source = lax.optimization_barrier(jnp.sum(passed, axis=1)).astype(jnp.int32)
    before = lax.optimization_barrier(jnp.sum(passed * live_row[None, :], axis=1)).astype(jnp.int32)
    flat_slot = source * capacity + (counter - before)
    inverse = jnp.zeros((bag_count,), jnp.int32).at[permute].set(counter)
    return flat_slot[inverse].astype(jnp.int32)

def slot_bags(live_row, permute, capacity):
    bag_count = permute.shape[0]
    starts = (jnp.cumsum(live_row) - live_row).astype(jnp.int32)
    column = jnp.arange(capacity, dtype=jnp.int32)
    position = jnp.minimum(starts[:, None] + column[None, :], bag_count - 1).astype(jnp.int32)
    is_live = column[None, :] < live_row[:, None]
    return (permute[position], is_live)

def reference(emb_table, row_accum, look_rows, live_counts, bag_order, dense_emb, labels, cross_in, cross_out, cross_bias, head_weight):
    replicas = look_rows.shape[0]
    shards = look_rows.shape[1]
    capacity = look_rows.shape[4]
    feature_width = emb_table.shape[1]
    rows_dev = emb_table.shape[0] // shards
    batch_size = dense_emb.shape[0] // (replicas * shards)
    shard_tables = emb_table.reshape(shards, rows_dev, feature_width)
    dense_all = dense_emb.reshape(replicas, shards * batch_size, feature_width)
    label_all = labels.reshape(replicas, shards * batch_size).astype(jnp.float32)
    contract = (((1,), (1,)), ((), ()))

    def one_replica(grad_sum, inputs):
        row_ids, live_rep, order_rep, dense_rep, label_rep = inputs

        def pool_source(shard_rows, source_ids):
            picked = jnp.take(shard_rows, source_ids, axis=0)
            return lax.optimization_barrier(jnp.sum(picked, axis=1)).astype(jnp.bfloat16)
        slot_pool = jax.vmap(pool_source)(shard_tables, row_ids)

        def gather_dest(dest_slots, live_row, permute):
            bag_slot = bag_sources(live_row, permute, capacity)
            return jnp.take(dest_slots.reshape(-1, feature_width), bag_slot, axis=0)
        pooled = jax.vmap(gather_dest, in_axes=(1, 0, 0))(slot_pool, live_rep, order_rep)
        pooled = pooled.reshape(shards * batch_size, -1)
        cross_input = jnp.concatenate([dense_rep, pooled], axis=1)
        hidden = jnp.dot(cross_input, cross_in, preferred_element_type=jnp.float32).astype(jnp.bfloat16)
        mixed_rows = lax.dot_general(hidden, cross_out, contract, preferred_element_type=jnp.float32) + cross_bias
        crossed = cross_input * mixed_rows + cross_input
        logits = jnp.dot(crossed, head_weight, precision=lax.Precision.HIGHEST)
        logit_grad = jax.nn.sigmoid(logits) - label_rep
        cross_grad = logit_grad[:, None] * head_weight[None, :]
        mixed_grad = (cross_grad * cross_input).astype(jnp.bfloat16)
        hidden_grad = jnp.dot(mixed_grad, cross_out, preferred_element_type=jnp.float32).astype(jnp.bfloat16)
        input_grad = cross_grad * (mixed_rows + 1.0) + lax.dot_general(hidden_grad, cross_in, contract, preferred_element_type=jnp.float32)
        pooled_grad = input_grad[:, feature_width:].astype(jnp.bfloat16).reshape(shards, -1, feature_width)

        def back_dest(bag_grads, live_row, permute):
            bag_ids, is_live = slot_bags(live_row, permute, capacity)
            picked = jnp.take(bag_grads, bag_ids.reshape(-1), axis=0).reshape(shards, capacity, feature_width)
            return jnp.where(is_live[:, :, None], picked, jnp.zeros_like(picked))
        slot_grads = jax.vmap(back_dest)(pooled_grad, live_rep, order_rep)
        global_ids = row_ids + (jnp.arange(shards, dtype=jnp.int32) * rows_dev)[:, None, None, None]
        values = jnp.transpose(slot_grads, (1, 0, 2, 3))[:, :, None, :, :].astype(jnp.float32)
        values = jnp.broadcast_to(values, global_ids.shape + (feature_width,))
        grad_sum = grad_sum.at[global_ids.reshape(-1)].add(values.reshape(-1, feature_width))
        return (grad_sum, logits)
    start_grads = jnp.zeros(emb_table.shape, jnp.float32)
    row_grad, logits = lax.scan(one_replica, start_grads, (look_rows, live_counts, bag_order, dense_all, label_all))
    new_accum = row_accum + lax.optimization_barrier(jnp.mean(row_grad * row_grad, axis=1))
    row_update = -row_grad / (jnp.sqrt(new_accum)[:, None] + EPSILON)
    return (logits.reshape(-1), row_update, new_accum)
```

```python
import functools

import jax
import jax.numpy as jnp
from jax import lax
from jax.experimental import pallas as pl
from jax.experimental.pallas import tpu as pltpu
from jax.sharding import PartitionSpec as P

EPSILON = 1e-08
F32, BF16 = jnp.float32, jnp.bfloat16
LOW = 32
UNROLL = 8
VMEM_LIMIT = 48 * 1024 * 1024


def swap(array, mask):
    size = lax.axis_size("replica")
    return lax.ppermute(array, "replica", [(i, i ^ mask) for i in range(size)])


def shift(array, step):
    size = lax.axis_size("table")
    return lax.ppermute(array, "table", [(i, (i + step) % size) for i in range(size)])


def mask_stages(size):
    stages, bit = [(1,)], 1
    while (1 << bit) < size:
        if (2 << bit) < size:
            stages.append((1 << bit, 2 << bit, 3 << bit))
            bit += 2
        else:
            stages.append((1 << bit,))
            bit += 1
    return stages


def replica_gather(piece):
    out = {0: piece}
    for masks in reversed(mask_stages(lax.axis_size("replica"))):
        for held in list(out):
            for mask in masks:
                out[held ^ mask] = swap(out[held], mask)
    return [out[m] for m in sorted(out)]


def whole(space=pltpu.VMEM):
    return pl.BlockSpec(memory_space=space)


def pool_kernel(shards, replicas, scal, dest, *refs):
    ids, (own, *pieces), (out, table, pooled) = refs[:shards], refs[shards:-3], refs[-3:]
    hot = ids[0].shape[0]
    block = pieces[0].shape[1]
    mine = scal[2 * shards]
    table[0] = own[...]
    for m, piece in enumerate(pieces):
        rows = pl.ds(pl.multiple_of((mine ^ m) * block, block), block)
        for k in range(1, shards):
            table[k, rows, :] = piece[k - 1].astype(F32)
    for k in range(shards):
        start, live = scal[k], scal[shards + k]

        def one(c, k=k, start=start):
            total = table[k, pl.ds(ids[k][0, c], 1), :]
            for h in range(1, hot):
                total = total + table[k, pl.ds(ids[k][h, c], 1), :]
            pooled[pl.ds(dest[start + c], 1), :] = total

        def group(i, _, one=one):
            for u in range(UNROLL):
                one(i * UNROLL + u)
            return 0

        def single(c, _, one=one):
            one(c)
            return 0

        full = live // UNROLL
        lax.fori_loop(0, full, group, 0)
        lax.fori_loop(full * UNROLL, live, single, 0)
    out[...] = pooled[...].astype(BF16)


def pool(scal, dest, ids, own, pieces, bags):
    shards, replicas = len(ids), len(pieces)
    rows, width = own.shape
    smem = whole(pltpu.SMEM)
    return pl.pallas_call(
        functools.partial(pool_kernel, shards, replicas),
        out_shape=jax.ShapeDtypeStruct((bags, width), BF16),
        in_specs=[smem, smem] + [smem] * shards + [whole()] * (1 + replicas),
        out_specs=whole(),
        scratch_shapes=[pltpu.VMEM((shards, rows, width), F32), pltpu.VMEM((bags, width), F32)],
        compiler_params=pltpu.CompilerParams(vmem_limit_bytes=VMEM_LIMIT),
        cost_estimate=pl.CostEstimate(flops=10**6, bytes_accessed=30 * 10**6, transcendentals=0),
        name="pool",
    )(scal, dest, *ids, own, *pieces)


def column_of(row, size):
    eye = lax.broadcasted_iota(jnp.int32, (size, size), 0) == lax.broadcasted_iota(
        jnp.int32, (size, size), 1
    )
    return jnp.sum(jnp.where(eye, jnp.broadcast_to(row, (size, size)), 0.0), axis=1, keepdims=True)


def row_of(column, size):
    eye = lax.broadcasted_iota(jnp.int32, (size, size), 0) == lax.broadcasted_iota(
        jnp.int32, (size, size), 1
    )
    return jnp.sum(
        jnp.where(eye, jnp.broadcast_to(column, (size, size)), 0.0), axis=0, keepdims=True
    )


def dense_kernel(shards, replicas, spots, chunk, scal, dest, *refs):
    ids = refs[:shards]
    dense, rows_in, bias, head, labels = refs[shards : shards + 5]
    weights = refs[shards + 5 : shards + 5 + len(spots)]
    logits, even, odd = refs[shards + 5 + len(spots) : shards + 8 + len(spots)]
    full_in, full_out, cross, scaled, grads, slots, counts, total = refs[shards + 8 + len(spots) :]
    factor = (full_in, full_out)
    batch, width = dense.shape
    features = full_in.shape[0]
    hot, capacity = ids[0].shape
    table_rows = total.shape[0]
    mine = scal[2 * shards]
    across = (((1,), (1,)), ((), ()))

    for ref, placing in zip(weights, spots):
        placing(ref, factor, scal)

    cross[:, :width] = dense[...]
    for f in range(1, features // width):
        cross[:, f * width : (f + 1) * width] = rows_in[(f - 1) * batch : f * batch, :]
    for f in range(features // width):
        at = slice(f * width, (f + 1) * width)
        scaled[:, at] = (cross[:, at].astype(F32) * head[:, at]).astype(BF16)
    hidden = jnp.dot(cross[...], full_in[...], preferred_element_type=F32).astype(BF16)
    back = jnp.dot(scaled[...], full_out[...], preferred_element_type=F32).astype(BF16)

    step = 3 * width if (features // width) % 3 == 0 else width
    logit = jnp.zeros((batch, width), F32)
    for n in range(features // step):
        at = slice(n * step, (n + 1) * step)
        mixed = lax.dot_general(hidden, full_out[at, :], across, preferred_element_type=F32)
        gain = head[:, at] * (mixed + bias[:, at] + 1.0)
        term = cross[:, at].astype(F32) * gain
        grad = gain + lax.dot_general(back, full_in[at, :], across, preferred_element_type=F32)
        for p in range(step // width):
            part = slice(p * width, (p + 1) * width)
            logit = logit + term[:, part]
            f = n * (step // width) + p
            if f > 0:
                grads[(f - 1) * batch : f * batch, :] = grad[:, part]
    logit = jnp.sum(logit, axis=1, keepdims=True)
    logits[...] = row_of(logit, batch)
    lean = jax.nn.sigmoid(logit) - column_of(labels[...].astype(F32), batch)
    for f in range(features // width - 1):
        at = slice(f * batch, (f + 1) * batch)
        grads[at, :] = (grads[at, :] * lean).astype(BF16).astype(F32)

    slots[...] = jnp.zeros_like(slots)
    low = lax.broadcasted_iota(jnp.int32, (LOW, chunk), 0)
    block = table_rows // replicas
    for k in range(shards):
        start, live = scal[k], scal[shards + k]

        def group(i, _, start=start):
            for u in range(UNROLL):
                c = i * UNROLL + u
                slots[pl.ds(c, 1), :] = grads[pl.ds(dest[start + c], 1), :]
            return 0

        lax.fori_loop(0, (live + UNROLL - 1) // UNROLL, group, 0)
        total[...] = jnp.zeros_like(total)

        def piece(q, _, k=k, live=live):
            at = pl.ds(pl.multiple_of(q * chunk, chunk), chunk)
            place = q * chunk + lax.broadcasted_iota(jnp.int32, (1, chunk), 1)
            lows, highs = [], []
            for h in range(hot):
                row = ids[k][h : h + 1, at] ^ (mine * block)
                row = jnp.where(place < live, row, -1)
                high = lax.shift_right_arithmetic(row, LOW.bit_length() - 1)
                lows.append((low == (row & (LOW - 1))).astype(F32).astype(BF16))
                highs.append(high)
            for b in range(table_rows // LOW):
                count = None
                for h in range(hot):
                    hit = (highs[h] == b).astype(F32).astype(BF16)
                    term = lows[h] * hit
                    count = term if count is None else count + term
                counts[b * LOW : (b + 1) * LOW, :] = count
            total[...] += jnp.dot(
                counts[...], slots[at, :].astype(BF16), preferred_element_type=F32
            )
            return 0

        lax.fori_loop(0, (live + chunk - 1) // chunk, piece, 0)
        for m in range(replicas):
            half = even if m % 2 == 0 else odd
            half[m // 2, k] = total[m * block : (m + 1) * block, :].astype(BF16)


def dense_step(scal, dest, ids, dense, rows_in, bias, head, labels, weights, spots, replicas, rows):
    shards = len(ids)
    batch, width = dense.shape
    features = bias.shape[1]
    rank = sum_columns(weights, spots)
    capacity = ids[0].shape[1]
    chunk = 256 if capacity % 256 == 0 else 128
    half = jax.ShapeDtypeStruct((replicas // 2, shards, rows // replicas, width), BF16)
    smem = whole(pltpu.SMEM)
    return pl.pallas_call(
        functools.partial(dense_kernel, shards, replicas, spots, chunk),
        out_shape=(jax.ShapeDtypeStruct((1, batch), F32), half, half),
        in_specs=[smem, smem] + [whole()] * (shards + 5 + len(weights)),
        out_specs=(whole(), whole(), whole()),
        scratch_shapes=[
            pltpu.VMEM((features, rank), BF16),
            pltpu.VMEM((features, rank), BF16),
            pltpu.VMEM((batch, features), BF16),
            pltpu.VMEM((batch, features), BF16),
            pltpu.VMEM((features // width * batch - batch, width), F32),
            pltpu.VMEM((capacity, width), F32),
            pltpu.VMEM((rows, chunk), BF16),
            pltpu.VMEM((rows, width), F32),
        ],
        compiler_params=pltpu.CompilerParams(vmem_limit_bytes=VMEM_LIMIT),
        cost_estimate=pl.CostEstimate(
            flops=4 * 10**9, bytes_accessed=30 * 10**6, transcendentals=0
        ),
        name="dense",
    )(scal, dest, *ids, dense, rows_in, bias, head, labels, *weights)


def sum_columns(weights, spots):
    return max(spot.rank for spot in spots)


class Spot:
    def __init__(self, which, rank, copy):
        self.which, self.rank, self.copy = which, rank, copy

    def __call__(self, ref, factor, scal):
        self.copy(ref, factor[self.which], scal)


def gather_weights(cross_in, cross_out):
    shards, replicas = lax.axis_size("table"), lax.axis_size("replica")
    shard_rows, rank = cross_in.shape
    mine = lax.axis_index("replica")
    half, lanes = shard_rows // 2, 128
    if replicas != 8 or rank != 4 * lanes or half % 16 != 0:
        both = [lax.all_gather(w, "table", axis=0, tiled=True) for w in (cross_in, cross_out)]

        def whole_copy(ref, full, scal):
            full[...] = ref[...]

        return both, [Spot(i, rank, whole_copy) for i in range(2)]

    start = ((mine & 1) * half, (mine >> 1) * lanes)
    piece = jnp.stack([lax.dynamic_slice(w, start, (half, lanes)) for w in (cross_in, cross_out)])
    far = [shift(piece, k) for k in range(1, shards)]
    top = jnp.stack([f[0] for f in far])
    bottom = jnp.stack([f[1] for f in far])
    tops, bottoms = {0: top}, {0: bottom}
    tops[2], bottoms[2], tops[4], bottoms[4] = swap(top, 2), swap(bottom, 2), swap(top, 4), swap(bottom, 4)
    tops[6], bottoms[6] = swap(tops[2], 4), swap(bottoms[4], 2)
    arrays, spots = [], []
    for which, held in enumerate((tops, bottoms)):
        for m in (0, 2, 4, 6):
            for core in (0, 1):
                arrays.append(held[m] if core == 0 else swap(held[m], 1))

                def copy(ref, full, scal, m=m, core=core):
                    own, here = scal[2 * shards], scal[2 * shards + 1]
                    for k in range(1, shards):
                        source = lax.rem(here - k + shards, shards)
                        first = source * shard_rows + ((own & 1) ^ core) * half
                        at = pl.ds(pl.multiple_of(first, 16), half)
                        full[at, (m // 2) * lanes : (m // 2 + 1) * lanes] = ref[k - 1]

                spots.append(Spot(which, rank, copy))
    for which, own_rows in enumerate((cross_in, cross_out)):

        def copy_own(ref, full, scal):
            own, here = scal[2 * shards], scal[2 * shards + 1]
            at = pl.ds(pl.multiple_of(here * shard_rows, 16), shard_rows)
            for m in range(4):
                columns = pl.ds(pl.multiple_of(((own >> 1) ^ m) * lanes, lanes), lanes)
                full[at, m * lanes : (m + 1) * lanes] = ref[:, columns]

        arrays.append(own_rows)
        spots.append(Spot(which, rank, copy_own))
    return arrays, spots


def reduce_rows(even, odd):
    shards, replicas = lax.axis_size("table"), lax.axis_size("replica")
    kept = even.astype(F32) + swap(odd, 1).astype(F32)
    for masks in mask_stages(replicas)[1:]:
        split = kept.reshape((-1, len(masks) + 1) + kept.shape[1:])
        kept = split[:, 0]
        for i, mask in enumerate(masks):
            kept = kept + swap(split[:, i + 1].astype(BF16), mask).astype(F32)
    kept = kept[0]
    total = kept[0]
    for k in range(1, shards):
        total = total + shift(kept[k], -k)
    return total


def finish_kernel(replicas, scal, accum, *refs):
    pieces, (update, fresh) = refs[:-2], refs[-2:]
    block, width = pieces[0].shape
    mine = scal[0]
    for m, piece in enumerate(pieces):
        own = mine ^ m
        grad = piece[...]
        square = jnp.sum(grad * grad, axis=1, keepdims=True) * (1.0 / width)
        row = accum[pl.ds(own, 1), :] + row_of(square, block)
        fresh[pl.ds(own, 1), :] = row
        rows = pl.ds(pl.multiple_of(own * block, block), block)
        update[rows, :] = -grad / (jnp.sqrt(column_of(row, block)) + EPSILON)


def finish(mine, accum, pieces):
    block, width = pieces[0].shape
    replicas = len(pieces)
    return pl.pallas_call(
        functools.partial(finish_kernel, replicas),
        out_shape=(
            jax.ShapeDtypeStruct((replicas * block, width), F32),
            jax.ShapeDtypeStruct((replicas, block), F32),
        ),
        in_specs=[whole(pltpu.SMEM)] + [whole()] * (1 + replicas),
        out_specs=(whole(), whole()),
        name="finish",
    )(mine, accum, *pieces)


def local(
    emb_table,
    row_accum,
    look_rows,
    live_counts,
    bag_order,
    dense_emb,
    labels,
    cross_in,
    cross_out,
    cross_bias,
    head_weight,
):
    shards, replicas = lax.axis_size("table"), lax.axis_size("replica")
    here, mine = lax.axis_index("table"), lax.axis_index("replica")
    rows, width = emb_table.shape
    batch = dense_emb.shape[0]
    bags = bag_order.shape[2]
    per_sample = bags // batch
    capacity = look_rows.shape[4]
    padded = -(-capacity // 128) * 128

    sent = jnp.pad(look_rows[0, 0], ((0, 0), (0, 0), (0, padded - capacity)))
    around = [lax.rem(here + k, shards) for k in range(shards)]
    ids = [lax.dynamic_index_in_dim(sent, around[k], 0, keepdims=False) for k in range(shards)]
    ids = [ids[0]] + [shift(ids[k], k) for k in range(1, shards)]

    block = rows // replicas
    piece = lax.dynamic_slice_in_dim(emb_table, mine * block, block, 0).astype(BF16)
    near = jnp.stack([shift(piece, k) for k in range(1, shards)])
    pieces = replica_gather(near)

    weights, spots = gather_weights(cross_in, cross_out)

    live = lax.dynamic_index_in_dim(live_counts[0], here, 0, keepdims=False)
    starts = jnp.cumsum(live) - live
    back = lax.rem(here - jnp.arange(shards, dtype=jnp.int32) + shards, shards)
    scal = jnp.concatenate([starts[back], live[back], jnp.stack([mine, here])]).astype(jnp.int32)
    order = bag_order[0, 0]
    dest = (order % per_sample) * batch + order // per_sample
    dest = jnp.pad(dest, (0, 128))

    rows_in = pool(scal, dest, ids, emb_table, pieces, bags)
    logits, even, odd = dense_step(
        scal,
        dest,
        ids,
        dense_emb,
        rows_in,
        cross_bias.reshape(1, -1),
        head_weight.reshape(1, -1),
        labels.reshape(1, -1),
        weights,
        spots,
        replicas,
        rows,
    )
    grad = reduce_rows(even, odd)
    update, accum = finish(
        jnp.stack([mine]).astype(jnp.int32), row_accum.reshape(replicas, block), replica_gather(grad)
    )
    return (logits.reshape(-1), update, accum.reshape(-1))


def solution(mesh):
    placed = (
        P("table", None),
        P("table"),
        P("replica", "table", None, None, None),
        P("replica", None, None),
        P("replica", "table", None),
        P(("replica", "table"), None),
        P(("replica", "table")),
        P("table", None),
        P("table", None),
        P(),
        P(),
    )
    return jax.shard_map(
        local,
        mesh=mesh,
        in_specs=placed,
        out_specs=(P(("replica", "table")), P("table", None), P("table")),
        check_vma=False,
    )
```

```python
import functools

import jax
import jax.numpy as jnp
from jax import lax
from jax.experimental import pallas as pl
from jax.experimental.pallas import tpu as pltpu
from jax.sharding import PartitionSpec as P

EPSILON = 1e-08
F32, BF16 = jnp.float32, jnp.bfloat16
LOW = 32
UNROLL = 8
HOT = 4
CHUNK = 256
ID_BITS = 10
VMEM_LIMIT = 48 * 1024 * 1024


def swap(array, mask):
    size = lax.axis_size("replica")
    return lax.ppermute(array, "replica", [(i, i ^ mask) for i in range(size)])


def shift(array, step):
    size = lax.axis_size("table")
    return lax.ppermute(array, "table", [(i, (i + step) % size) for i in range(size)])


def mask_stages(size):
    stages, bit = [(1,)], 1
    while (1 << bit) < size:
        if (2 << bit) < size:
            stages.append((1 << bit, 2 << bit, 3 << bit))
            bit += 2
        else:
            stages.append((1 << bit,))
            bit += 1
    return stages


def replica_gather(piece):
    out = {0: piece}
    for masks in reversed(mask_stages(lax.axis_size("replica"))):
        for held in list(out):
            for mask in masks:
                out[held ^ mask] = swap(out[held], mask)
    return [out[m] for m in sorted(out)]


def whole(space=pltpu.VMEM):
    return pl.BlockSpec(memory_space=space)


def pool_kernel(shards, scal, first, second, *refs):
    (own, *pieces), (out, table, pooled) = refs[:-3], refs[-3:]
    rows_dev = own.shape[0]
    block = pieces[0].shape[1]
    mine = scal[2 * shards]
    table[:rows_dev, :] = own[...]
    for m, piece in enumerate(pieces):
        for k in range(1, shards):
            rows = pl.ds(pl.multiple_of((mine ^ m) * block + k * rows_dev, block), block)
            table[rows, :] = piece[k - 1]
    field = (1 << ID_BITS) - 1
    for j in range(shards):
        start, live = scal[j], scal[shards + j]
        base = j * rows_dev

        def several(k0, count, base=base):
            sums, places = [], []
            for u in range(count):
                one, two = first[k0 + u], second[k0 + u]
                spots = (
                    one & field,
                    lax.shift_right_logical(one, ID_BITS) & field,
                    two & field,
                    lax.shift_right_logical(two, ID_BITS),
                )
                read = [table[pl.ds(spot + base, 1), :] for spot in spots]
                sums.append((read[0] + read[1]) + (read[2] + read[3]))
                places.append(lax.shift_right_logical(one, 2 * ID_BITS))
            for total, place in zip(sums, places):
                pooled[pl.ds(place, 1), :] = total

        def group(i, _, start=start, several=several):
            several(start + i * UNROLL, UNROLL)
            return 0

        def single(i, _, start=start, several=several):
            several(start + i, 1)
            return 0

        full = live // UNROLL
        lax.fori_loop(0, full, group, 0)
        lax.fori_loop(full * UNROLL, live, single, 0)
    out[...] = pooled[...].astype(BF16)


def pool(scal, first, second, own, pieces, bags):
    rows, width = own.shape
    shards = pieces[0].shape[0] + 1
    smem = whole(pltpu.SMEM)
    return pl.pallas_call(
        functools.partial(pool_kernel, shards),
        out_shape=jax.ShapeDtypeStruct((bags, width), BF16),
        in_specs=[smem, smem, smem] + [whole()] * (1 + len(pieces)),
        out_specs=whole(),
        scratch_shapes=[pltpu.VMEM((shards * rows, width), F32), pltpu.VMEM((bags, width), F32)],
        compiler_params=pltpu.CompilerParams(vmem_limit_bytes=VMEM_LIMIT),
        cost_estimate=pl.CostEstimate(flops=10**6, bytes_accessed=30 * 10**6, transcendentals=0),
        name="pool",
    )(scal, first, second, own, *pieces)


def pair_range(scal, shards, j):
    start, live = scal[j], scal[shards + j]
    source = lax.rem(scal[2 * shards + 1] - j + shards, shards)
    return start, live, source, start // CHUNK, (start + live + CHUNK - 1) // CHUNK


def count_kernel(shards, replicas, scal, words, out):
    rows = out.shape[1]
    block = rows // replicas
    flip = scal[2 * shards] * block
    low = lax.broadcasted_iota(jnp.int32, (LOW, CHUNK), 0)
    field = (1 << ID_BITS) - 1
    for j in range(shards):
        start, live, source, begin, end = pair_range(scal, shards, j)

        def pair(q, _, start=start, live=live, source=source):
            at = pl.ds(pl.multiple_of(q * CHUNK, CHUNK), CHUNK)
            place = q * CHUNK + lax.broadcasted_iota(jnp.int32, (1, CHUNK), 1) - start
            inside = (place >= 0) & (place < live)
            lows, highs = [], []
            for h in range(HOT):
                word = words[h // 2 : h // 2 + 1, at]
                row = (lax.shift_right_logical(word, (h % 2) * ID_BITS) & field) ^ flip
                row = jnp.where(inside, row, -1)
                highs.append(lax.shift_right_arithmetic(row, LOW.bit_length() - 1))
                lows.append((low == (row & (LOW - 1))).astype(F32).astype(BF16))
            for b in range(rows // LOW):
                count = None
                for h in range(HOT):
                    hit = (highs[h] == b).astype(F32).astype(BF16)
                    term = lows[h] * hit
                    count = term if count is None else count + term
                out[q + source, b * LOW : (b + 1) * LOW, :] = count
            return 0

        lax.fori_loop(begin, end, pair, 0)


def count_rows(scal, words, shards, replicas, rows):
    pairs = words.shape[1] // CHUNK + shards - 1
    return pl.pallas_call(
        functools.partial(count_kernel, shards, replicas),
        out_shape=jax.ShapeDtypeStruct((pairs, rows, CHUNK), BF16),
        in_specs=[whole(pltpu.SMEM), whole()],
        out_specs=whole(),
        compiler_params=pltpu.CompilerParams(vmem_limit_bytes=VMEM_LIMIT),
        cost_estimate=pl.CostEstimate(flops=10**6, bytes_accessed=10 * 10**6, transcendentals=0),
        name="count_rows",
    )(scal, words)


def column_of(row, size):
    eye = lax.broadcasted_iota(jnp.int32, (size, size), 0) == lax.broadcasted_iota(
        jnp.int32, (size, size), 1
    )
    return jnp.sum(jnp.where(eye, jnp.broadcast_to(row, (size, size)), 0.0), axis=1, keepdims=True)


def row_of(column, size):
    eye = lax.broadcasted_iota(jnp.int32, (size, size), 0) == lax.broadcasted_iota(
        jnp.int32, (size, size), 1
    )
    return jnp.sum(
        jnp.where(eye, jnp.broadcast_to(column, (size, size)), 0.0), axis=0, keepdims=True
    )


def dense_kernel(shards, replicas, spots, scal, places, *refs):
    dense, rows_in, bias, head, labels, counted = refs[:6]
    weights = refs[6 : 6 + len(spots)]
    logits, even, odd = refs[6 + len(spots) : 9 + len(spots)]
    full_in, full_out, cross, scaled, grads, slots, narrow, counts, total, done = refs[9 + len(spots) :]
    batch, width = dense.shape
    features = full_in.shape[0]
    bags = grads.shape[0]
    table_rows = total.shape[0]
    across = (((1,), (1,)), ((), ()))

    fetch = pltpu.make_async_copy(counted, counts, done)
    fetch.start()
    for ref, spot in zip(weights, spots):
        spot.copy(ref, (full_in, full_out)[spot.which], scal)

    cross[:, :width] = dense[...]
    for f in range(1, features // width):
        cross[:, f * width : (f + 1) * width] = rows_in[(f - 1) * batch : f * batch, :]
    for f in range(features // width):
        at = slice(f * width, (f + 1) * width)
        scaled[:, at] = (cross[:, at].astype(F32) * head[:, at]).astype(BF16)
    hidden = jnp.dot(cross[...], full_in[...], preferred_element_type=F32).astype(BF16)
    back = jnp.dot(scaled[...], full_out[...], preferred_element_type=F32).astype(BF16)

    step = 3 * width if (features // width) % 3 == 0 else width
    logit = jnp.zeros((batch, width), F32)
    for n in range(features // step):
        at = slice(n * step, (n + 1) * step)
        mixed = lax.dot_general(hidden, full_out[at, :], across, preferred_element_type=F32)
        gain = head[:, at] * (mixed + bias[:, at] + 1.0)
        term = cross[:, at].astype(F32) * gain
        grad = gain + lax.dot_general(back, full_in[at, :], across, preferred_element_type=F32)
        for p in range(step // width):
            part = slice(p * width, (p + 1) * width)
            logit = logit + term[:, part]
            f = n * (step // width) + p
            if f > 0:
                grads[(f - 1) * batch : f * batch, :] = grad[:, part]
    logit = jnp.sum(logit, axis=1, keepdims=True)
    logits[...] = row_of(logit, batch)
    lean = jax.nn.sigmoid(logit) - column_of(labels[...].astype(F32), batch)
    for f in range(features // width - 1):
        at = slice(f * batch, (f + 1) * batch)
        grads[at, :] = (grads[at, :] * lean).astype(BF16).astype(F32)

    middle = bags // 2

    def group(i, _):
        for u in range(UNROLL):
            k = i * UNROLL + u
            word = places[k]
            slots[pl.ds(k, 1), :] = grads[pl.ds(word & 0xFFFF, 1), :]
            slots[pl.ds(k + middle, 1), :] = grads[pl.ds(lax.shift_right_logical(word, 16), 1), :]
        return 0

    lax.fori_loop(0, middle // UNROLL, group, 0)
    narrow[...] = slots[...].astype(BF16)
    fetch.wait()
    block = table_rows // replicas
    for j in range(shards):
        start, live, source, begin, end = pair_range(scal, shards, j)
        total[...] = jnp.zeros_like(total)

        def pair(q, _, source=source):
            at = pl.ds(pl.multiple_of(q * CHUNK, CHUNK), CHUNK)
            total[...] += jnp.dot(
                counts[q + source], narrow[at, :], preferred_element_type=F32
            )
            return 0

        lax.fori_loop(begin, end, pair, 0)
        for m in range(replicas):
            half = even if m % 2 == 0 else odd
            half[m // 2, j] = total[m * block : (m + 1) * block, :].astype(BF16)


def dense_step(scal, places, dense, rows_in, bias, head, labels, counted, weights, spots, shards, replicas):
    batch, width = dense.shape
    features = bias.shape[1]
    bags = rows_in.shape[0]
    rows = counted.shape[1]
    rank = spots[0].rank
    half = jax.ShapeDtypeStruct((replicas // 2, shards, rows // replicas, width), BF16)
    smem = whole(pltpu.SMEM)
    return pl.pallas_call(
        functools.partial(dense_kernel, shards, replicas, spots),
        out_shape=(jax.ShapeDtypeStruct((1, batch), F32), half, half),
        in_specs=[smem, smem] + [whole()] * 5 + [whole(pl.ANY)] + [whole()] * len(weights),
        out_specs=(whole(), whole(), whole()),
        scratch_shapes=[
            pltpu.VMEM((features, rank), BF16),
            pltpu.VMEM((features, rank), BF16),
            pltpu.VMEM((batch, features), BF16),
            pltpu.VMEM((batch, features), BF16),
            pltpu.VMEM((bags, width), F32),
            pltpu.VMEM((bags, width), F32),
            pltpu.VMEM((bags, width), BF16),
            pltpu.VMEM(counted.shape, BF16),
            pltpu.VMEM((rows, width), F32),
            pltpu.SemaphoreType.DMA(()),
        ],
        compiler_params=pltpu.CompilerParams(vmem_limit_bytes=VMEM_LIMIT),
        cost_estimate=pl.CostEstimate(
            flops=4 * 10**9, bytes_accessed=30 * 10**6, transcendentals=0
        ),
        name="dense",
    )(scal, places, dense, rows_in, bias, head, labels, counted, *weights)


class Spot:
    def __init__(self, which, rank, copy):
        self.which, self.rank, self.copy = which, rank, copy


def gather_weights(cross_in, cross_out, after):
    shards, replicas = lax.axis_size("table"), lax.axis_size("replica")
    shard_rows, rank = cross_in.shape
    mine = lax.axis_index("replica")
    half, lanes = shard_rows // 2, 128
    if replicas != 8 or rank != 4 * lanes or half % 16 != 0:
        both = [lax.all_gather(w, "table", axis=0, tiled=True) for w in (cross_in, cross_out)]

        def whole_copy(ref, full, scal):
            full[...] = ref[...]

        return both, [Spot(i, rank, whole_copy) for i in range(2)], after

    start = ((mine & 1) * half, (mine >> 1) * lanes)
    top, bottom = (
        jnp.stack([shift(lax.dynamic_slice(w, start, (half, lanes)), k) for k in range(1, shards)])
        for w in (cross_in, cross_out)
    )
    tops, bottoms = {0: top}, {0: bottom}
    tops[2], bottoms[2], tops[4], bottoms[4] = swap(top, 2), swap(bottom, 2), swap(top, 4), swap(bottom, 4)
    (near_top, near_bottom), after = lax.optimization_barrier(((tops[2], bottoms[4]), after))
    tops[6], bottoms[6] = swap(near_top, 4), swap(near_bottom, 2)
    arrays, spots = [], []
    for which, held in enumerate((tops, bottoms)):
        for m in (0, 2, 4, 6):
            for core in (0, 1):
                arrays.append(held[m] if core == 0 else swap(held[m], 1))

                def copy(ref, full, scal, m=m, core=core):
                    own, here = scal[2 * shards], scal[2 * shards + 1]
                    for k in range(1, shards):
                        source = lax.rem(here - k + shards, shards)
                        first = source * shard_rows + ((own & 1) ^ core) * half
                        at = pl.ds(pl.multiple_of(first, 16), half)
                        full[at, (m // 2) * lanes : (m // 2 + 1) * lanes] = ref[k - 1]

                spots.append(Spot(which, rank, copy))
    for which, own_rows in enumerate((cross_in, cross_out)):

        def copy_own(ref, full, scal):
            own, here = scal[2 * shards], scal[2 * shards + 1]
            at = pl.ds(pl.multiple_of(here * shard_rows, 16), shard_rows)
            for m in range(4):
                columns = pl.ds(pl.multiple_of(((own >> 1) ^ m) * lanes, lanes), lanes)
                full[at, m * lanes : (m + 1) * lanes] = ref[:, columns]

        arrays.append(own_rows)
        spots.append(Spot(which, rank, copy_own))
    return arrays, spots, after


def reduce_rows(even, odd):
    shards, replicas = lax.axis_size("table"), lax.axis_size("replica")
    kept = even.astype(F32) + swap(odd, 1).astype(F32)
    for masks in mask_stages(replicas)[1:]:
        split = kept.reshape((-1, len(masks) + 1) + kept.shape[1:])
        kept = split[:, 0]
        for i, mask in enumerate(masks):
            kept = kept + swap(split[:, i + 1].astype(BF16), mask).astype(F32)
    kept = kept[0]
    total = kept[0]
    for k in range(1, shards):
        total = total + shift(kept[k], -k)
    return total


def finish_kernel(replicas, scal, accum, *refs):
    pieces, (update, fresh) = refs[:-2], refs[-2:]
    block, width = pieces[0].shape
    mine = scal[0]
    for m, piece in enumerate(pieces):
        own = mine ^ m
        grad = piece[...]
        square = jnp.sum(grad * grad, axis=1, keepdims=True) * (1.0 / width)
        row = accum[pl.ds(own, 1), :] + row_of(square, block)
        fresh[pl.ds(own, 1), :] = row
        rows = pl.ds(pl.multiple_of(own * block, block), block)
        update[rows, :] = -grad / (jnp.sqrt(column_of(row, block)) + EPSILON)


def finish(mine, accum, pieces):
    block, width = pieces[0].shape
    replicas = len(pieces)
    return pl.pallas_call(
        functools.partial(finish_kernel, replicas),
        out_shape=(
            jax.ShapeDtypeStruct((replicas * block, width), F32),
            jax.ShapeDtypeStruct((replicas, block), F32),
        ),
        in_specs=[whole(pltpu.SMEM)] + [whole()] * (1 + replicas),
        out_specs=(whole(), whole()),
        compiler_params=pltpu.CompilerParams(vmem_limit_bytes=VMEM_LIMIT),
        name="finish",
    )(mine, accum, *pieces)


def local(
    emb_table,
    row_accum,
    look_rows,
    live_counts,
    bag_order,
    dense_emb,
    labels,
    cross_in,
    cross_out,
    cross_bias,
    head_weight,
):
    shards, replicas = lax.axis_size("table"), lax.axis_size("replica")
    here, mine = lax.axis_index("table"), lax.axis_index("replica")
    rows, width = emb_table.shape
    batch = dense_emb.shape[0]
    bags = bag_order.shape[2]
    per_sample = bags // batch
    capacity = look_rows.shape[4]
    padded = -(-capacity // width) * width
    block = rows // replicas

    live = lax.dynamic_index_in_dim(live_counts[0], here, 0, keepdims=False)
    starts = jnp.cumsum(live) - live
    back = [lax.rem(here - k + shards, shards) for k in range(shards)]
    starts = [lax.dynamic_index_in_dim(starts, b, 0, keepdims=False) for b in back]
    lives = [lax.dynamic_index_in_dim(live, b, 0, keepdims=False) for b in back]
    scal = jnp.stack(starts + lives + [mine, here]).astype(jnp.int32)
    order = bag_order[0, 0]
    dest = (order % per_sample) * batch + order // per_sample
    places = dest[: bags // 2] | (dest[bags // 2 :] << 16)

    piece = lax.dynamic_slice_in_dim(emb_table, mine * block, block, 0)
    sent = jnp.pad(look_rows[0, 0], ((0, 0), (0, 0), (0, padded - capacity))).astype(F32)
    sent = sent.reshape(shards, -1, width)
    parcels = []
    for k in range(shards):
        to = lax.rem(here + k, shards)
        parcel = jnp.concatenate([piece, lax.dynamic_index_in_dim(sent, to, 0, keepdims=False)])
        parcels.append(parcel if k == 0 else shift(parcel, k))

    slot = jnp.arange(bags, dtype=jnp.int32)
    words = jnp.zeros((2, bags), jnp.int32)
    for k in range(shards):
        ids = parcels[k][block:].reshape(HOT, padded).astype(jnp.int32)
        word = ids[0::2] | (ids[1::2] << ID_BITS)
        word = jnp.pad(word, ((0, 0), (bags, bags)))
        moved = lax.dynamic_slice_in_dim(word, bags - starts[k], bags, 1)
        words = jnp.where((slot >= starts[k]) & (slot < starts[k] + lives[k]), moved, words)
    counted = count_rows(scal, words, shards, replicas, rows)

    near = jnp.stack([parcels[k][:block] for k in range(1, shards)])
    pieces = replica_gather(near)
    scal, counted = lax.optimization_barrier((scal, counted))
    rows_in = pool(scal, words[0] | (dest << (2 * ID_BITS)), words[1], emb_table, pieces, bags)
    weights, spots, rows_in = gather_weights(cross_in, cross_out, rows_in)
    logits, even, odd = dense_step(
        scal,
        places,
        dense_emb,
        rows_in,
        cross_bias.reshape(1, -1),
        head_weight.reshape(1, -1),
        labels.reshape(1, -1),
        counted,
        weights,
        spots,
        shards,
        replicas,
    )
    grad = reduce_rows(even, odd)
    update, accum = finish(
        jnp.stack([mine]).astype(jnp.int32), row_accum.reshape(replicas, block), replica_gather(grad)
    )
    return (logits.reshape(-1), update, accum.reshape(-1))


def solution(mesh):
    placed = (
        P("table", None),
        P("table"),
        P("replica", "table", None, None, None),
        P("replica", None, None),
        P("replica", "table", None),
        P(("replica", "table"), None),
        P(("replica", "table")),
        P("table", None),
        P("table", None),
        P(),
        P(),
    )
    return jax.shard_map(
        local,
        mesh=mesh,
        in_specs=placed,
        out_specs=(P(("replica", "table")), P("table", None), P("table")),
        check_vma=False,
    )
```

```python
import functools

import jax
import jax.numpy as jnp
from jax import lax
from jax.experimental import pallas as pl
from jax.experimental.pallas import tpu as pltpu
from jax.sharding import PartitionSpec as P

EPSILON = 1e-08
F32, BF16 = jnp.float32, jnp.bfloat16
LOW = 32
UNROLL = 8
HOT = 4
CHUNK = 256
ID_BITS = 10
VMEM_LIMIT = 28 * 1024 * 1024
PACK_LIMIT = 60 * 1024 * 1024


def swap(array, mask):
    size = lax.axis_size("replica")
    return lax.ppermute(array, "replica", [(i, i ^ mask) for i in range(size)])


def shift(array, step):
    size = lax.axis_size("table")
    return lax.ppermute(array, "table", [(i, (i + step) % size) for i in range(size)])


def mask_stages(size):
    stages, bit = [(1,)], 1
    while (1 << bit) < size:
        if (2 << bit) < size:
            stages.append((1 << bit, 2 << bit, 3 << bit))
            bit += 2
        else:
            stages.append((1 << bit,))
            bit += 1
    return stages


def replica_gather(piece, *beside):
    held = [piece]
    for masks in reversed(mask_stages(lax.axis_size("replica"))[1:]):
        held = [held] + [[swap(h, mask) for h in held] for mask in masks]
        held = [h for group in held for h in group]
    order = sorted(range(len(held)), key=lambda i: gather_masks(lax.axis_size("replica"))[i])
    even = jnp.stack([held[i] for i in order])
    even, *beside = lax.optimization_barrier((even, *beside))
    return (even, swap(even, 1)), *beside


def gather_masks(size):
    masks = [0]
    for group in reversed(mask_stages(size)[1:]):
        masks = masks + [m ^ mask for mask in group for m in masks]
    return masks


def whole(space=pltpu.VMEM):
    return pl.BlockSpec(memory_space=space)


def slot_range(live_counts, shards, j):
    here = lax.axis_index("table")
    source = lax.rem(here - j + shards, shards)
    start = jnp.int32(0)
    for s in range(shards):
        start = start + jnp.where(s < source, live_counts[0, here, s], 0)
    return source, start, live_counts[0, here, source]


def pack_kernel(shards, wanted, look_rows, table, *refs):
    factors, refs = refs[: len(wanted)], refs[len(wanted) :]
    parcels, blocks, done = refs[: shards - 1], refs[shards - 1 : -1], refs[-1]
    width = table.shape[1]
    capacity = look_rows.shape[4]
    lines = -(-capacity // width)
    block = parcels[0].shape[0] - HOT * lines
    mine, here = lax.axis_index("replica"), lax.axis_index("table")
    rows = table.at[pl.ds(pl.multiple_of(mine * block, block), block), :]
    copies = [
        pltpu.make_async_copy(rows, parcel.at[:block, :], done.at[i])
        for i, parcel in enumerate(parcels)
    ]
    for i, factor in enumerate(factors):
        both = blocks[0]
        half, lanes = both.shape[0] // 2, both.shape[1]
        at = (
            pl.ds(pl.multiple_of((mine & 1) * half, 16), half),
            pl.ds(pl.multiple_of((mine >> 1) * lanes, lanes), lanes),
        )
        into = both.at[i * half : (i + 1) * half, :]
        copies.append(pltpu.make_async_copy(factor.at[at], into, done.at[shards - 1 + i]))
    for copy in copies:
        copy.start()
    for i, parcel in enumerate(parcels):
        owner = lax.rem(here + i + 1, shards)
        for h in range(HOT):
            for q in range(lines):
                line = block + h * lines + q
                size = min(width, capacity - q * width)
                if size < width:
                    parcel[line : line + 1, :] = jnp.zeros((1, width), F32)
                parcel[line : line + 1, :size] = look_rows[
                    0, 0, owner, h : h + 1, q * width : q * width + size
                ].astype(F32)
    for copy in copies:
        copy.wait()


def pack(look_rows, table, factors, shards, replicas):
    rows, width = table.shape
    capacity = look_rows.shape[4]
    lines = -(-capacity // width)
    parcel = jax.ShapeDtypeStruct((rows // replicas + HOT * lines, width), F32)
    blocks = [jax.ShapeDtypeStruct((f.shape[0], width), BF16) for f in factors[:1]]
    count = shards - 1 + len(factors)
    return pl.pallas_call(
        functools.partial(pack_kernel, shards, factors),
        out_shape=[parcel] * (shards - 1) + blocks,
        in_specs=[whole()] + [whole(pltpu.HBM)] * (1 + len(factors)),
        out_specs=[whole()] * (shards - 1 + len(blocks)),
        scratch_shapes=[pltpu.SemaphoreType.DMA((count,))],
        compiler_params=pltpu.CompilerParams(vmem_limit_bytes=PACK_LIMIT),
        name="pack",
    )(look_rows, table, *factors)


def quotient(value, divisor, below):
    shift = 19
    factor = (1 << shift) // divisor + 1
    assert below * factor < 1 << 31
    assert all((v * factor) >> shift == v // divisor for v in range(below))
    return lax.shift_right_logical(value * factor, shift)


def slots_kernel(shards, replicas, batch, live_counts, look_rows, bag_order, *refs):
    parcels, (places, counted, shifted, words) = refs[: shards - 1], refs[shards - 1 :]
    width = parcels[0].shape[1]
    capacity = look_rows.shape[4]
    lines = -(-capacity // width)
    bags = bag_order.shape[2]
    rows = counted.shape[1]
    block = rows // replicas
    field = (1 << ID_BITS) - 1
    slot = lax.broadcasted_iota(jnp.int32, (8, bags), 1)
    ranges = [slot_range(live_counts, shards, j) for j in range(shards)]
    here = lax.axis_index("table")
    shifted[...] = jnp.zeros_like(shifted)
    for j, (source, start, live) in enumerate(ranges):
        for pair in range(HOT // 2):
            for q in range(lines):
                size = min(width, capacity - q * width)

                def line(h, j=j, q=q, size=size):
                    if j == 0:
                        return look_rows[0, 0, here, h : h + 1, q * width : q * width + size]
                    at = block + h * lines + q
                    return parcels[j - 1][at : at + 1, :size].astype(jnp.int32)

                shifted[pair : pair + 1, q * width : q * width + size] = line(2 * pair) | (
                    line(2 * pair + 1) << ID_BITS
                )
        moved = pltpu.roll(shifted[...], start, 1)[:, :bags]
        inside = (slot >= start) & (slot < start + live)
        words[...] = jnp.where(inside, moved, words[...] if j else 0)
    order = bag_order[0]
    sample = quotient(order, bags // batch, bags)
    dest = (order - sample * (bags // batch)) * batch + sample
    places[...] = dest[:, : bags // 2] | (dest[:, bags // 2 :] << 16)

    flip = lax.axis_index("replica") * block
    low = lax.broadcasted_iota(jnp.int32, (LOW, CHUNK), 0)
    for source, start, live in ranges:

        def pair(q, _, start=start, live=live, source=source):
            at = pl.ds(pl.multiple_of(q * CHUNK, CHUNK), CHUNK)
            place = q * CHUNK + lax.broadcasted_iota(jnp.int32, (1, CHUNK), 1) - start
            inside = (place >= 0) & (place < live)
            lows, highs = [], []
            for h in range(HOT):
                word = words[h // 2 : h // 2 + 1, at]
                row = (lax.shift_right_logical(word, (h % 2) * ID_BITS) & field) ^ flip
                row = jnp.where(inside, row, -1)
                highs.append(lax.shift_right_arithmetic(row, LOW.bit_length() - 1))
                lows.append((low == (row & (LOW - 1))).astype(F32).astype(BF16))
            for b in range(rows // LOW):
                count = None
                for h in range(HOT):
                    hit = (highs[h] == b).astype(F32).astype(BF16)
                    term = lows[h] * hit
                    count = term if count is None else count + term
                counted[q + source, b * LOW : (b + 1) * LOW, :] = count
            return 0

        lax.fori_loop(start // CHUNK, (start + live + CHUNK - 1) // CHUNK, pair, 0)


def slots(live_counts, look_rows, bag_order, parcels, rows, shards, replicas, batch):
    bags = bag_order.shape[2]
    capacity = -(-look_rows.shape[4] // 128) * 128
    pairs = bags // CHUNK + shards - 1
    return pl.pallas_call(
        functools.partial(slots_kernel, shards, replicas, batch),
        out_shape=[
            jax.ShapeDtypeStruct((1, bags // 2), jnp.int32),
            jax.ShapeDtypeStruct((pairs, rows, CHUNK), BF16),
        ],
        in_specs=[whole(pltpu.SMEM)] + [whole()] * (2 + len(parcels)),
        out_specs=[whole()] * 2,
        scratch_shapes=[
            pltpu.VMEM((8, bags + capacity), jnp.int32),
            pltpu.VMEM((8, bags), jnp.int32),
        ],
        compiler_params=pltpu.CompilerParams(vmem_limit_bytes=VMEM_LIMIT),
        cost_estimate=pl.CostEstimate(flops=1000, bytes_accessed=1000, transcendentals=0),
        name="slots",
    )(live_counts, look_rows, bag_order, *parcels)


def pool_kernel(shards, live_counts, places, counted, own, even, odd, out, table, sums, pooled):
    rows_dev, width = own.shape
    block = even.shape[2]
    middle = sums.shape[0] // 2
    mine = lax.axis_index("replica")

    def put(shard, rows, value):
        high = value.astype(BF16)
        table[shard, rows, :width] = high
        table[shard, rows, width:] = (value - high.astype(F32)).astype(BF16)

    for m in range(2 * even.shape[0]):
        there = pl.ds(pl.multiple_of((mine ^ m) * block, block), block)
        rows = slice(m * block, (m + 1) * block)
        put(0, rows, own[there, :])
        for k in range(1, shards):
            put(k, rows, (odd if m % 2 else even)[m // 2, k - 1])
    sums[...] = jnp.zeros_like(sums)
    for j in range(shards):
        source, start, live = slot_range(live_counts, shards, j)

        def pair(q, _, j=j, source=source):
            at = pl.ds(pl.multiple_of(q * CHUNK, CHUNK), CHUNK)
            found = lax.dot_general(
                counted[q + source], table[j], (((0,), (0,)), ((), ())), preferred_element_type=F32
            )
            sums[at, :] += found[:, :width] + found[:, width:]
            return 0

        lax.fori_loop(start // CHUNK, (start + live + CHUNK - 1) // CHUNK, pair, 0)

    def group(i, _):
        for u in range(UNROLL):
            k = i * UNROLL + u
            word = places[0, k]
            pooled[pl.ds(word & 0xFFFF, 1), :] = sums[pl.ds(k, 1), :]
            pooled[pl.ds(lax.shift_right_logical(word, 16), 1), :] = sums[pl.ds(k + middle, 1), :]
        return 0

    lax.fori_loop(0, middle // UNROLL, group, 0)
    out[...] = pooled[...].astype(BF16)


def pool(live_counts, places, counted, own, pieces):
    rows, width = own.shape
    bags = 2 * places.shape[1]
    shards = pieces[0].shape[1] + 1
    smem = whole(pltpu.SMEM)
    return pl.pallas_call(
        functools.partial(pool_kernel, shards),
        out_shape=jax.ShapeDtypeStruct((bags, width), BF16),
        in_specs=[smem, smem] + [whole()] * 4,
        out_specs=whole(),
        scratch_shapes=[
            pltpu.VMEM((shards, rows, 2 * width), BF16),
            pltpu.VMEM((bags, width), F32),
            pltpu.VMEM((bags, width), F32),
        ],
        compiler_params=pltpu.CompilerParams(vmem_limit_bytes=VMEM_LIMIT),
        cost_estimate=pl.CostEstimate(flops=1000, bytes_accessed=1000, transcendentals=0),
        name="pool",
    )(live_counts, places, counted, own, *pieces)


def column_of(row, size):
    eye = lax.broadcasted_iota(jnp.int32, (size, size), 0) == lax.broadcasted_iota(
        jnp.int32, (size, size), 1
    )
    return jnp.sum(jnp.where(eye, jnp.broadcast_to(row, (size, size)), 0.0), axis=1, keepdims=True)


def row_of(column, size):
    eye = lax.broadcasted_iota(jnp.int32, (size, size), 0) == lax.broadcasted_iota(
        jnp.int32, (size, size), 1
    )
    return jnp.sum(
        jnp.where(eye, jnp.broadcast_to(column, (size, size)), 0.0), axis=0, keepdims=True
    )


def dense_kernel(shards, replicas, copies, live_counts, places, *refs):
    dense, rows_in, bias, head, labels, counted = refs[:6]
    weights = refs[6 : 6 + len(copies)]
    logits, even, odd = refs[6 + len(copies) : 9 + len(copies)]
    full_in, full_out, cross, scaled, grads, slots, narrow, total = refs[9 + len(copies) :]
    batch, width = dense.shape
    features = full_in.shape[0]
    bags = grads.shape[0]
    table_rows = total.shape[0]
    across = (((1,), (1,)), ((), ()))

    factor = (full_in, full_out)
    for ref, copy in zip(weights, copies):
        copy(ref, factor)

    cross[:, :width] = dense[...]
    for f in range(1, features // width):
        cross[:, f * width : (f + 1) * width] = rows_in[(f - 1) * batch : f * batch, :]
    for f in range(features // width):
        at = slice(f * width, (f + 1) * width)
        scaled[:, at] = (cross[:, at].astype(F32) * head[:, at]).astype(BF16)
    hidden = jnp.dot(cross[...], full_in[...], preferred_element_type=F32).astype(BF16)
    back = jnp.dot(scaled[...], full_out[...], preferred_element_type=F32).astype(BF16)

    step = 3 * width if (features // width) % 3 == 0 else width
    logit = jnp.zeros((batch, width), F32)
    for n in range(features // step):
        at = slice(n * step, (n + 1) * step)
        mixed = lax.dot_general(hidden, full_out[at, :], across, preferred_element_type=F32)
        gain = head[:, at] * (mixed + bias[:, at] + 1.0)
        term = cross[:, at].astype(F32) * gain
        grad = gain + lax.dot_general(back, full_in[at, :], across, preferred_element_type=F32)
        for p in range(step // width):
            part = slice(p * width, (p + 1) * width)
            logit = logit + term[:, part]
            f = n * (step // width) + p
            if f > 0:
                grads[(f - 1) * batch : f * batch, :] = grad[:, part]
    logit = jnp.sum(logit, axis=1, keepdims=True)
    logits[...] = row_of(logit, batch)
    lean = jax.nn.sigmoid(logit) - column_of(labels[...].astype(F32), batch)
    for f in range(features // width - 1):
        at = slice(f * batch, (f + 1) * batch)
        grads[at, :] = (grads[at, :] * lean).astype(BF16).astype(F32)

    middle = bags // 2

    def group(i, _):
        for u in range(UNROLL):
            k = i * UNROLL + u
            word = places[0, k]
            slots[pl.ds(k, 1), :] = grads[pl.ds(word & 0xFFFF, 1), :]
            slots[pl.ds(k + middle, 1), :] = grads[pl.ds(lax.shift_right_logical(word, 16), 1), :]
        return 0

    lax.fori_loop(0, middle // UNROLL, group, 0)
    narrow[...] = slots[...].astype(BF16)
    block = table_rows // replicas
    for j in range(shards):
        source, start, live = slot_range(live_counts, shards, j)
        total[...] = jnp.zeros_like(total)

        def pair(q, _, source=source):
            at = pl.ds(pl.multiple_of(q * CHUNK, CHUNK), CHUNK)
            total[...] += jnp.dot(
                counted[q + source], narrow[at, :], preferred_element_type=F32
            )
            return 0

        lax.fori_loop(start // CHUNK, (start + live + CHUNK - 1) // CHUNK, pair, 0)
        for m in range(replicas):
            half = even if m % 2 == 0 else odd
            half[m // 2, j] = total[m * block : (m + 1) * block, :].astype(BF16)


def dense_step(live_counts, places, dense, rows_in, bias, head, labels, counted, weights, copies, rank, shards, replicas):
    batch, width = dense.shape
    features = bias.shape[1]
    bags = rows_in.shape[0]
    rows = counted.shape[1]
    half = jax.ShapeDtypeStruct((replicas // 2, shards, rows // replicas, width), BF16)
    smem = whole(pltpu.SMEM)
    return pl.pallas_call(
        functools.partial(dense_kernel, shards, replicas, copies),
        out_shape=(jax.ShapeDtypeStruct((1, batch), F32), half, half),
        in_specs=[smem, smem] + [whole()] * 6 + [whole()] * len(weights),
        out_specs=(whole(), whole(), whole()),
        scratch_shapes=[
            pltpu.VMEM((features, rank), BF16),
            pltpu.VMEM((features, rank), BF16),
            pltpu.VMEM((batch, features), BF16),
            pltpu.VMEM((batch, features), BF16),
            pltpu.VMEM((bags, width), F32),
            pltpu.VMEM((bags, width), F32),
            pltpu.VMEM((bags, width), BF16),
            pltpu.VMEM((rows, width), F32),
        ],
        compiler_params=pltpu.CompilerParams(vmem_limit_bytes=VMEM_LIMIT),
        cost_estimate=pl.CostEstimate(
            flops=4 * 10**9, bytes_accessed=30 * 10**6, transcendentals=0
        ),
        name="dense",
    )(live_counts, places, dense, rows_in, bias, head, labels, counted, *weights)


def splits_evenly(factor, replicas):
    return replicas == 8 and factor.shape[1] == 4 * 128 and factor.shape[0] % 32 == 0


def gather_whole(factors):
    def spot(which):
        def copy(ref, full):
            full[which][...] = ref[...]

        return copy

    return [lax.all_gather(w, "table", axis=0, tiled=True) for w in factors], [spot(0), spot(1)]


def gather_blocks(factors, near, after):
    shards = lax.axis_size("table")
    shard_rows = factors[0].shape[0]
    half, lanes = shard_rows // 2, near.shape[2]
    first, second = swap(near, 2), swap(near, 4)
    first, second, after = lax.optimization_barrier((first, second, after))
    blocks = [(0, near, 0, 2), (2, first, 0, 2), (4, second, 0, 2)]
    blocks += [(6, swap(first[:, :half], 4), 0, 1), (6, swap(second[:, half:], 2), 1, 2)]
    arrays, copies = [], []
    for m, block, begin, end in blocks:
        for core in (0, 1):
            arrays.append(block if core == 0 else swap(block, 1))

            def copy(ref, full, m=m, core=core, begin=begin, end=end):
                own, here = lax.axis_index("replica"), lax.axis_index("table")
                for k in range(1, shards):
                    source = lax.rem(here - k + shards, shards)
                    first = source * shard_rows + ((own & 1) ^ core) * half
                    at = pl.ds(pl.multiple_of(first, 16), half)
                    for which in range(begin, end):
                        full[which][at, (m // 2) * lanes : (m // 2 + 1) * lanes] = ref[
                            k - 1, (which - begin) * half : (which - begin + 1) * half, :
                        ]

            copies.append(copy)
    for which, own_rows in enumerate(factors):

        def copy_own(ref, full, which=which):
            own, here = lax.axis_index("replica"), lax.axis_index("table")
            at = pl.ds(pl.multiple_of(here * shard_rows, 16), shard_rows)
            for m in range(4):
                columns = pl.ds(pl.multiple_of(((own >> 1) ^ m) * lanes, lanes), lanes)
                full[which][at, m * lanes : (m + 1) * lanes] = ref[:, columns]

        arrays.append(own_rows)
        copies.append(copy_own)
    return arrays, copies, after


def reduce_rows(even, odd):
    shards, replicas = lax.axis_size("table"), lax.axis_size("replica")
    kept = even.astype(F32) + swap(odd, 1).astype(F32)
    for masks in mask_stages(replicas)[1:]:
        split = kept.reshape((-1, len(masks) + 1) + kept.shape[1:])
        kept = split[:, 0]
        for i, mask in enumerate(masks):
            kept = kept + swap(split[:, i + 1].astype(BF16), mask).astype(F32)
    kept = kept[0]
    total = kept[0]
    for k in range(1, shards):
        total = total + shift(kept[k], -k)
    return total


def finish_kernel(accum, even, odd, update, fresh):
    count, block, width = even.shape
    mine = lax.axis_index("replica")
    for m in range(2 * count):
        own = mine ^ m
        grad = (odd if m % 2 else even)[m // 2]
        square = jnp.sum(grad * grad, axis=1, keepdims=True) * (1.0 / width)
        row = accum[pl.ds(own, 1), :] + row_of(square, block)
        fresh[pl.ds(own, 1), :] = row
        rows = pl.ds(pl.multiple_of(own * block, block), block)
        update[rows, :] = -grad / (jnp.sqrt(column_of(row, block)) + EPSILON)


def finish(accum, even, odd):
    replicas, block = accum.shape
    width = even.shape[2]
    return pl.pallas_call(
        finish_kernel,
        out_shape=(
            jax.ShapeDtypeStruct((replicas * block, width), F32),
            jax.ShapeDtypeStruct((replicas, block), F32),
        ),
        in_specs=[whole()] * 3,
        out_specs=(whole(), whole()),
        compiler_params=pltpu.CompilerParams(vmem_limit_bytes=VMEM_LIMIT),
        name="finish",
    )(accum, even, odd)


def local(
    emb_table,
    row_accum,
    look_rows,
    live_counts,
    bag_order,
    dense_emb,
    labels,
    cross_in,
    cross_out,
    cross_bias,
    head_weight,
):
    shards, replicas = lax.axis_size("table"), lax.axis_size("replica")
    rows = emb_table.shape[0]
    block = rows // replicas
    batch = dense_emb.shape[0]
    factors = (cross_in, cross_out)
    even_split = splits_evenly(cross_in, replicas)

    packed = pack(look_rows, emb_table, factors if even_split else (), shards, replicas)
    parcels = [shift(p, k + 1) for k, p in enumerate(packed[: shards - 1])]
    far = [shift(packed[shards - 1], k) for k in range(1, shards)] if even_split else []
    places, counted = slots(
        live_counts, look_rows, bag_order, parcels, rows, shards, replicas, batch
    )
    pieces, far, counted = replica_gather(
        jnp.stack([p[:block] for p in parcels]), far, counted
    )
    rows_in = pool(live_counts, places, counted, emb_table, pieces)
    if even_split:
        near = jnp.stack(far)
    if even_split:
        weights, copies, rows_in = gather_blocks(factors, near, rows_in)
    else:
        weights, copies = gather_whole(factors)
    logits, even, odd = dense_step(
        live_counts,
        places,
        dense_emb,
        rows_in,
        cross_bias.reshape(1, -1),
        head_weight.reshape(1, -1),
        labels.reshape(1, -1),
        counted,
        weights,
        copies,
        cross_in.shape[1],
        shards,
        replicas,
    )
    grad = reduce_rows(even, odd)
    update, accum = finish(row_accum.reshape(replicas, block), *replica_gather(grad)[0])
    return (logits.reshape(-1), update, accum.reshape(-1))


def solution(mesh):
    placed = (
        P("table", None),
        P("table"),
        P("replica", "table", None, None, None),
        P("replica", None, None),
        P("replica", "table", None),
        P(("replica", "table"), None),
        P(("replica", "table")),
        P("table", None),
        P("table", None),
        P(),
        P(),
    )
    return jax.shard_map(
        local,
        mesh=mesh,
        in_specs=placed,
        out_specs=(P(("replica", "table")), P("table", None), P("table")),
        check_vma=False,
    )
```

```python
import functools

import jax
import jax.numpy as jnp
from jax import lax
from jax.experimental import pallas as pl
from jax.experimental.pallas import tpu as pltpu
from jax.sharding import PartitionSpec as P

EPSILON = 1e-08
F32, BF16 = jnp.float32, jnp.bfloat16
LOW = 32
UNROLL = 8
HOT = 4
CHUNK = 256
ID_BITS = 10
VMEM_LIMIT = 28 * 1024 * 1024
PACK_LIMIT = 60 * 1024 * 1024


def swap(array, mask):
    size = lax.axis_size("replica")
    return lax.ppermute(array, "replica", [(i, i ^ mask) for i in range(size)])


def cross_over(array, mask):
    size = lax.axis_size("table")
    return lax.ppermute(array, "table", [(i, i ^ mask) for i in range(size)])


def mask_stages(size):
    stages, bit = [(1,)], 1
    while (1 << bit) < size:
        if (2 << bit) < size:
            stages.append((1 << bit, 2 << bit, 3 << bit))
            bit += 2
        else:
            stages.append((1 << bit,))
            bit += 1
    return stages


def replica_gather(piece, *beside):
    held = [piece]
    for masks in reversed(mask_stages(lax.axis_size("replica"))[1:]):
        held = [held] + [[swap(h, mask) for h in held] for mask in masks]
        held = [h for group in held for h in group]
    order = sorted(range(len(held)), key=lambda i: gather_masks(lax.axis_size("replica"))[i])
    even = jnp.stack([held[i] for i in order])
    even, *beside = lax.optimization_barrier((even, *beside))
    return (even, swap(even, 1)), *beside


def gather_masks(size):
    masks = [0]
    for group in reversed(mask_stages(size)[1:]):
        masks = masks + [m ^ mask for mask in group for m in masks]
    return masks


def whole(space=pltpu.VMEM):
    return pl.BlockSpec(memory_space=space)


def slot_range(live_counts, shards, j):
    here = lax.axis_index("table")
    source = here ^ j
    start = jnp.int32(0)
    for s in range(shards):
        start = start + jnp.where(s < source, live_counts[0, here, s], 0)
    return source, start, live_counts[0, here, source]


def pack_kernel(shards, wanted, look_rows, table, *refs):
    factors, refs = refs[: len(wanted)], refs[len(wanted) :]
    parcels, blocks, done = refs[: shards - 1], refs[shards - 1 : -1], refs[-1]
    width = table.shape[1]
    capacity = look_rows.shape[4]
    lines = -(-capacity // width)
    paired = HOT // 2 * lines
    block = parcels[0].shape[0] - paired
    mine, here = lax.axis_index("replica"), lax.axis_index("table")
    rows = table.at[pl.ds(pl.multiple_of(mine * block, block), block), :]
    copies = [
        pltpu.make_async_copy(rows, parcel.at[:block, :], done.at[i])
        for i, parcel in enumerate(parcels)
    ]
    for i, factor in enumerate(factors):
        both = blocks[0]
        half, lanes = both.shape[0] // 2, both.shape[1]
        at = (
            pl.ds(pl.multiple_of((mine & 1) * half, 16), half),
            pl.ds(pl.multiple_of((mine >> 1) * lanes, lanes), lanes),
        )
        into = both.at[i * half : (i + 1) * half, :]
        copies.append(pltpu.make_async_copy(factor.at[at], into, done.at[shards - 1 + i]))
    for copy in copies:
        copy.start()
    for i, parcel in enumerate(parcels):
        owner = here ^ (i + 1)
        for pair in range(HOT // 2):
            for q in range(lines):
                line = block + pair * lines + q
                size = min(width, capacity - q * width)
                if size < width:
                    parcel[line : line + 1, :] = jnp.zeros((1, width), F32)
                at = slice(q * width, q * width + size)
                value = (look_rows[0, 0, owner, 2 * pair : 2 * pair + 1, at] << ID_BITS) | (
                    look_rows[0, 0, owner, 2 * pair + 1 : 2 * pair + 2, at]
                )
                parcel[line : line + 1, :size] = value.astype(F32)
    for copy in copies:
        copy.wait()


def pack(look_rows, table, factors, shards, replicas):
    rows, width = table.shape
    capacity = look_rows.shape[4]
    lines = HOT // 2 * -(-capacity // width)
    parcel = jax.ShapeDtypeStruct((rows // replicas + lines, width), F32)
    blocks = [jax.ShapeDtypeStruct((f.shape[0], width), BF16) for f in factors[:1]]
    return pl.pallas_call(
        functools.partial(pack_kernel, shards, factors),
        out_shape=[parcel] * (shards - 1) + blocks,
        in_specs=[whole()] + [whole(pltpu.HBM)] * (1 + len(factors)),
        out_specs=[whole()] * (shards - 1 + len(blocks)),
        scratch_shapes=[pltpu.SemaphoreType.DMA((shards - 1 + len(factors),))],
        compiler_params=pltpu.CompilerParams(vmem_limit_bytes=PACK_LIMIT),
        name="pack",
    )(look_rows, table, *factors)


def quotient(value, divisor, below):
    shift = 19
    factor = (1 << shift) // divisor + 1
    assert below * factor < 1 << 31
    assert all((v * factor) >> shift == v // divisor for v in range(below))
    return lax.shift_right_logical(value * factor, shift)


def slots_kernel(shards, replicas, batch, live_counts, look_rows, bag_order, *refs):
    parcels, (places, counted, shifted, words) = refs[: shards - 1], refs[shards - 1 :]
    width = parcels[0].shape[1]
    capacity = look_rows.shape[4]
    lines = -(-capacity // width)
    bags = bag_order.shape[2]
    rows = counted.shape[1]
    block = rows // replicas
    field = (1 << ID_BITS) - 1
    slot = lax.broadcasted_iota(jnp.int32, (8, bags), 1)
    ranges = [slot_range(live_counts, shards, j) for j in range(shards)]
    here = lax.axis_index("table")
    shifted[...] = jnp.zeros_like(shifted)
    for j, (source, start, live) in enumerate(ranges):
        for pair in range(HOT // 2):
            for q in range(lines):
                size = min(width, capacity - q * width)

                at = slice(q * width, q * width + size)
                if j == 0:
                    own = [look_rows[0, 0, here, 2 * pair + h : 2 * pair + h + 1, at] for h in (0, 1)]
                    value = (own[0] << ID_BITS) | own[1]
                else:
                    line = block + pair * lines + q
                    value = parcels[j - 1][line : line + 1, :size].astype(jnp.int32)
                shifted[pair : pair + 1, at] = value
        moved = pltpu.roll(shifted[...], start, 1)[:, :bags]
        inside = (slot >= start) & (slot < start + live)
        words[...] = jnp.where(inside, moved, words[...] if j else 0)
    order = bag_order[0]
    sample = quotient(order, bags // batch, bags)
    dest = (order - sample * (bags // batch)) * batch + sample
    for q in range(bags // CHUNK):
        one = dest[:, q * CHUNK : q * CHUNK + CHUNK // 2]
        two = dest[:, q * CHUNK + CHUNK // 2 : (q + 1) * CHUNK]
        places[:, q * CHUNK // 2 : (q + 1) * CHUNK // 2] = one | (two << 16)

    flip = lax.axis_index("replica") * block
    low = lax.broadcasted_iota(jnp.int32, (LOW, CHUNK), 0)
    for source, start, live in ranges:

        def pair(q, _, start=start, live=live, source=source):
            at = pl.ds(pl.multiple_of(q * CHUNK, CHUNK), CHUNK)
            place = q * CHUNK + lax.broadcasted_iota(jnp.int32, (1, CHUNK), 1) - start
            inside = (place >= 0) & (place < live)
            lows, highs = [], []
            for h in range(HOT):
                word = words[h // 2 : h // 2 + 1, at]
                row = (lax.shift_right_logical(word, (h % 2) * ID_BITS) & field) ^ flip
                row = jnp.where(inside, row, -1)
                highs.append(lax.shift_right_arithmetic(row, LOW.bit_length() - 1))
                lows.append((low == (row & (LOW - 1))).astype(F32).astype(BF16))
            for b in range(rows // LOW):
                count = None
                for h in range(HOT):
                    hit = (highs[h] == b).astype(F32).astype(BF16)
                    term = lows[h] * hit
                    count = term if count is None else count + term
                counted[q + source, b * LOW : (b + 1) * LOW, :] = count
            return 0

        lax.fori_loop(start // CHUNK, (start + live + CHUNK - 1) // CHUNK, pair, 0)


def slots(live_counts, look_rows, bag_order, parcels, rows, shards, replicas, batch):
    bags = bag_order.shape[2]
    capacity = -(-look_rows.shape[4] // 128) * 128
    pairs = bags // CHUNK + shards - 1
    return pl.pallas_call(
        functools.partial(slots_kernel, shards, replicas, batch),
        out_shape=[
            jax.ShapeDtypeStruct((1, bags // 2), jnp.int32),
            jax.ShapeDtypeStruct((pairs, rows, CHUNK), BF16),
        ],
        in_specs=[whole(pltpu.SMEM)] + [whole()] * (2 + len(parcels)),
        out_specs=[whole()] * 2,
        scratch_shapes=[
            pltpu.VMEM((8, bags + capacity), jnp.int32),
            pltpu.VMEM((8, bags), jnp.int32),
        ],
        compiler_params=pltpu.CompilerParams(vmem_limit_bytes=VMEM_LIMIT),
        cost_estimate=pl.CostEstimate(flops=1000, bytes_accessed=1000, transcendentals=0),
        name="slots",
    )(live_counts, look_rows, bag_order, *parcels)


def pool_kernel(
    shards, live_counts, places, counted, own, even, odd, dense, head, cross, scaled, table, sums, pooled
):
    rows_dev, width = own.shape
    block = even.shape[2]
    batch = dense.shape[0]
    half = CHUNK // 2
    mine = lax.axis_index("replica")

    def put(shard, rows, value):
        high = value.astype(BF16)
        table[shard, rows, :width] = high
        table[shard, rows, width:] = (value - high.astype(F32)).astype(BF16)

    for m in range(2 * even.shape[0]):
        there = pl.ds(pl.multiple_of((mine ^ m) * block, block), block)
        rows = slice(m * block, (m + 1) * block)
        put(0, rows, own[there, :])
        for k in range(1, shards):
            put(k, rows, (odd if m % 2 else even)[m // 2, k - 1])
    sums[...] = jnp.zeros_like(sums)
    for j in range(shards):
        source, start, live = slot_range(live_counts, shards, j)

        def pair(q, _, j=j, source=source):
            at = pl.ds(pl.multiple_of(q * CHUNK, CHUNK), CHUNK)
            found = lax.dot_general(
                counted[q + source], table[j], (((0,), (0,)), ((), ())), preferred_element_type=F32
            )
            sums[at, :] += found[:, :width] + found[:, width:]
            return 0

        lax.fori_loop(start // CHUNK, (start + live + CHUNK - 1) // CHUNK, pair, 0)

    def group(i, _):
        k0 = i * UNROLL
        k0 = k0 + lax.div(k0, half) * half
        for u in range(UNROLL):
            word = places[0, i * UNROLL + u]
            pooled[pl.ds(word & 0xFFFF, 1), :] = sums[pl.ds(k0 + u, 1), :]
            pooled[pl.ds(lax.shift_right_logical(word, 16), 1), :] = sums[pl.ds(k0 + u + half, 1), :]
        return 0

    lax.fori_loop(0, sums.shape[0] // (2 * UNROLL), group, 0)
    for f in range(cross.shape[1] // width):
        at = slice(f * width, (f + 1) * width)
        block = dense[...] if f == 0 else pooled[(f - 1) * batch : f * batch, :].astype(BF16)
        cross[:, at] = block
        scaled[:, at] = (block.astype(F32) * head[:, at]).astype(BF16)


def pool(live_counts, places, counted, own, pieces, dense, head):
    rows, width = own.shape
    bags = 2 * places.shape[1]
    shards = pieces[0].shape[1] + 1
    smem = whole(pltpu.SMEM)
    return pl.pallas_call(
        functools.partial(pool_kernel, shards),
        out_shape=[jax.ShapeDtypeStruct((dense.shape[0], head.shape[1]), BF16)] * 2,
        in_specs=[smem, smem] + [whole()] * 6,
        out_specs=[whole()] * 2,
        scratch_shapes=[
            pltpu.VMEM((shards, rows, 2 * width), BF16),
            pltpu.VMEM((bags, width), F32),
            pltpu.VMEM((bags, width), F32),
        ],
        compiler_params=pltpu.CompilerParams(vmem_limit_bytes=VMEM_LIMIT),
        cost_estimate=pl.CostEstimate(flops=1000, bytes_accessed=1000, transcendentals=0),
        name="pool",
    )(live_counts, places, counted, own, *pieces, dense, head)


def column_of(row, size):
    eye = lax.broadcasted_iota(jnp.int32, (size, size), 0) == lax.broadcasted_iota(
        jnp.int32, (size, size), 1
    )
    return jnp.sum(jnp.where(eye, jnp.broadcast_to(row, (size, size)), 0.0), axis=1, keepdims=True)


def row_of(column, size):
    eye = lax.broadcasted_iota(jnp.int32, (size, size), 0) == lax.broadcasted_iota(
        jnp.int32, (size, size), 1
    )
    return jnp.sum(
        jnp.where(eye, jnp.broadcast_to(column, (size, size)), 0.0), axis=0, keepdims=True
    )


def first_kernel(copies, cross, scaled, bias, head, *refs):
    weights, (grads, logit, full_in, full_out) = refs[: len(copies)], refs[len(copies) :]
    for ref, copy in zip(weights, copies):
        copy(ref, (full_in, full_out))
    add_rank(cross, scaled, head, full_in, full_out, bias, None, grads, logit)


def add_rank(cross, scaled, head, full_in, full_out, bias, before, grads, logit):
    batch, features = cross.shape
    width = logit.shape[1]
    across = (((1,), (1,)), ((), ()))
    hidden = jnp.dot(cross[...], full_in[...], preferred_element_type=F32).astype(BF16)
    back = jnp.dot(scaled[...], full_out[...], preferred_element_type=F32).astype(BF16)
    step = 3 * width if (features // width) % 3 == 0 else width
    total = jnp.zeros((batch, width), F32) if before is None else before[1][...]
    for n in range(features // step):
        at = slice(n * step, (n + 1) * step)
        mixed = lax.dot_general(hidden, full_out[at, :], across, preferred_element_type=F32)
        if bias is not None:
            mixed = mixed + bias[:, at] + 1.0
        gain = head[:, at] * mixed
        term = cross[:, at].astype(F32) * gain
        grad = gain + lax.dot_general(back, full_in[at, :], across, preferred_element_type=F32)
        for p in range(step // width):
            part = slice(p * width, (p + 1) * width)
            total = total + term[:, part]
            f = n * (step // width) + p
            if f > 0:
                rows = slice((f - 1) * batch, f * batch)
                grads[rows, :] = grad[:, part] + (0.0 if before is None else before[0][rows, :])
    logit[...] = total


def first_step(cross, scaled, bias, head, weights, copies, rank):
    batch, features = cross.shape
    width = 128
    return pl.pallas_call(
        functools.partial(first_kernel, copies),
        out_shape=(
            jax.ShapeDtypeStruct((features // width * batch - batch, width), F32),
            jax.ShapeDtypeStruct((batch, width), F32),
        ),
        in_specs=[whole()] * (4 + len(weights)),
        out_specs=(whole(), whole()),
        scratch_shapes=[pltpu.VMEM((features, rank), BF16)] * 2,
        compiler_params=pltpu.CompilerParams(vmem_limit_bytes=VMEM_LIMIT),
        cost_estimate=pl.CostEstimate(
            flops=2 * 10**9, bytes_accessed=20 * 10**6, transcendentals=0
        ),
        name="first",
    )(cross, scaled, bias, head, *weights)


def dense_kernel(shards, replicas, copies, live_counts, places, cross, scaled, head, labels, counted, *refs):
    begun, partial = refs[:2]
    weights = refs[2 : 2 + len(copies)]
    logits, even, odd, full_in, full_out, grads, logit, slots, narrow, total, spots, done = refs[
        2 + len(copies) :
    ]
    batch = cross.shape[0]
    width = slots.shape[1]
    bags = grads.shape[0]
    rows = total.shape[2]
    here = lax.axis_index("table")
    fetch = pltpu.make_async_copy(places, spots, done)
    fetch.start()

    if copies:
        for ref, copy in zip(weights, copies):
            copy(ref, (full_in, full_out))
        add_rank(cross, scaled, head, full_in, full_out, None, (begun, partial), grads, logit)
    else:
        grads[...] = begun[...]
        logit[...] = partial[...]
    sums = jnp.sum(logit[...], axis=1, keepdims=True)
    logits[...] = row_of(sums, batch)
    lean = jax.nn.sigmoid(sums) - column_of(labels[...].astype(F32), batch)
    for f in range(bags // batch):
        at = slice(f * batch, (f + 1) * batch)
        grads[at, :] = (grads[at, :] * lean).astype(BF16).astype(F32)

    half = CHUNK // 2
    chunks = bags // CHUNK
    total[...] = jnp.zeros_like(total)

    def gather(q):
        for i in range(half):
            word = spots[0, q * half + i]
            slots[i : i + 1, :] = grads[pl.ds(word & 0xFFFF, 1), :]
            slots[i + half : i + half + 1, :] = grads[pl.ds(lax.shift_right_logical(word, 16), 1), :]

    def shard_of(k):
        end, shard = jnp.int32(0), jnp.int32(0)
        for s in range(shards - 1):
            end = end + live_counts[0, here, s]
            shard = shard + jnp.where(k >= end, 1, 0)
        return shard

    def add(q, shard):
        place = here ^ shard
        total[place] += lax.dot_general(
            narrow[...], counted[q + shard], (((0,), (1,)), ((), ())), preferred_element_type=F32
        )

    fetch.wait()
    gather(0)

    def chunk(q, _):
        narrow[...] = slots[...].astype(BF16)
        shard = shard_of(q * CHUNK)
        add(q, shard)
        gather(jnp.minimum(q + 1, chunks - 1))

        def more(s, _):
            add(q, s)
            return 0

        lax.fori_loop(shard + 1, shard_of((q + 1) * CHUNK - 1) + 1, more, 0)
        return 0

    lax.fori_loop(0, chunks, chunk, 0)
    block = rows // replicas
    for j in range(shards):
        for m in range(replicas):
            sums = total[j, :, m * block : (m + 1) * block].T
            (odd if m % 2 else even)[m // 2, j] = sums.astype(BF16)


def dense_step(
    live_counts, places, cross, scaled, head, labels, counted, begun, weights, copies, shards, replicas
):
    batch, features = cross.shape
    width = 128
    bags = begun[0].shape[0]
    rows = counted.shape[1]
    half = jax.ShapeDtypeStruct((replicas // 2, shards, rows // replicas, width), BF16)
    smem = whole(pltpu.SMEM)
    part = pltpu.VMEM((features, width) if copies else (16, width), BF16)
    return pl.pallas_call(
        functools.partial(dense_kernel, shards, replicas, copies),
        out_shape=(jax.ShapeDtypeStruct((1, batch), F32), half, half),
        in_specs=[smem] + [whole()] * (8 + len(weights)),
        out_specs=(whole(), whole(), whole()),
        scratch_shapes=[
            part,
            part,
            pltpu.VMEM((bags, width), F32),
            pltpu.VMEM((batch, width), F32),
            pltpu.VMEM((CHUNK, width), F32),
            pltpu.VMEM((CHUNK, width), BF16),
            pltpu.VMEM((shards, width, rows), F32),
            pltpu.SMEM(places.shape, jnp.int32),
            pltpu.SemaphoreType.DMA(()),
        ],
        compiler_params=pltpu.CompilerParams(vmem_limit_bytes=VMEM_LIMIT),
        cost_estimate=pl.CostEstimate(
            flops=2 * 10**9, bytes_accessed=20 * 10**6, transcendentals=0
        ),
        name="dense",
    )(live_counts, places, cross, scaled, head, labels, counted, *begun, *weights)


def splits_evenly(factor, replicas):
    return replicas == 8 and factor.shape[1] == 4 * 128 and factor.shape[0] % 32 == 0


def gather_whole(factors):
    def spot(which):
        def copy(ref, full):
            full[which][...] = ref[...]

        return copy

    return [
        (lax.all_gather(w, "table", axis=0, tiled=True), spot(i)) for i, w in enumerate(factors)
    ]


def gather_blocks(factors, near, after):
    shards = lax.axis_size("table")
    shard_rows = factors[0].shape[0]
    half, lanes = shard_rows // 2, near.shape[2]
    first, second = swap(near, 2), swap(near, 4)
    first, second, after = lax.optimization_barrier((first, second, after))
    corners = [(swap(first[:, :half], 4), 0), (swap(second[:, half:], 2), 1)]

    def put(block, core, column, begin, end):
        def copy(ref, full):
            own, here = lax.axis_index("replica"), lax.axis_index("table")
            for k in range(1, shards):
                source = here ^ k
                start = source * shard_rows + ((own & 1) ^ core) * half
                at = pl.ds(pl.multiple_of(start, 16), half)
                for which in range(begin, end):
                    full[which][at, column * lanes : (column + 1) * lanes] = ref[
                        k - 1, (which - begin) * half : (which - begin + 1) * half, :
                    ]

        return block, copy

    def put_own(which, masks):
        def copy(ref, full):
            own, here = lax.axis_index("replica"), lax.axis_index("table")
            at = pl.ds(pl.multiple_of(here * shard_rows, 16), shard_rows)
            for column, mask in enumerate(masks):
                columns = pl.ds(pl.multiple_of(((own >> 1) ^ mask) * lanes, lanes), lanes)
                full[which][at, column * lanes : (column + 1) * lanes] = ref[:, columns]

        return factors[which], copy

    early = [put_own(which, (0, 1, 2)) for which in range(2)]
    for column, block in enumerate((near, first, second)):
        early += [put(block, 0, column, 0, 2), put(swap(block, 1), 1, column, 0, 2)]

    def late(after):
        blocks, after = lax.optimization_barrier(([c[0] for c in corners], after))
        out = [put_own(which, (3,)) for which in range(2)]
        for block, (_, which) in zip(blocks, corners):
            out += [put(block, 0, 0, which, which + 1), put(swap(block, 1), 1, 0, which, which + 1)]
        return out, after

    return early, late, after


def reduce_rows(even, odd):
    shards, replicas = lax.axis_size("table"), lax.axis_size("replica")
    kept = even.astype(F32) + swap(odd, 1).astype(F32)
    for masks in mask_stages(replicas)[1:]:
        split = kept.reshape((-1, len(masks) + 1) + kept.shape[1:])
        kept = split[:, 0]
        for i, mask in enumerate(masks):
            kept = kept + swap(split[:, i + 1].astype(BF16), mask).astype(F32)
    kept = kept[0]
    total = kept[0]
    for k in range(1, shards):
        total = total + cross_over(kept[k].astype(BF16), k).astype(F32)
    return total


def finish_kernel(accum, even, odd, update, fresh):
    count, block, width = even.shape
    mine = lax.axis_index("replica")
    for m in range(2 * count):
        own = mine ^ m
        grad = (odd if m % 2 else even)[m // 2]
        square = jnp.sum(grad * grad, axis=1, keepdims=True) * (1.0 / width)
        row = accum[pl.ds(own, 1), :] + row_of(square, block)
        fresh[pl.ds(own, 1), :] = row
        rows = pl.ds(pl.multiple_of(own * block, block), block)
        update[rows, :] = -grad / (jnp.sqrt(column_of(row, block)) + EPSILON)


def finish(accum, even, odd):
    replicas, block = accum.shape
    width = even.shape[2]
    return pl.pallas_call(
        finish_kernel,
        out_shape=(
            jax.ShapeDtypeStruct((replicas * block, width), F32),
            jax.ShapeDtypeStruct((replicas, block), F32),
        ),
        in_specs=[whole()] * 3,
        out_specs=(whole(), whole()),
        compiler_params=pltpu.CompilerParams(vmem_limit_bytes=VMEM_LIMIT),
        name="finish",
    )(accum, even, odd)


def local(
    emb_table,
    row_accum,
    look_rows,
    live_counts,
    bag_order,
    dense_emb,
    labels,
    cross_in,
    cross_out,
    cross_bias,
    head_weight,
):
    shards, replicas = lax.axis_size("table"), lax.axis_size("replica")
    rows = emb_table.shape[0]
    block = rows // replicas
    batch = dense_emb.shape[0]
    factors = (cross_in, cross_out)
    even_split = splits_evenly(cross_in, replicas)

    packed = pack(look_rows, emb_table, factors if even_split else (), shards, replicas)
    parcels = [cross_over(p, k + 1) for k, p in enumerate(packed[: shards - 1])]
    far = [cross_over(packed[shards - 1], k) for k in range(1, shards)] if even_split else []
    places, counted = slots(
        live_counts, look_rows, bag_order, parcels, rows, shards, replicas, batch
    )
    pieces, far, counted = replica_gather(
        jnp.stack([p[:block] for p in parcels]), far, counted
    )
    bias, head = cross_bias.reshape(1, -1), head_weight.reshape(1, -1)
    crossed = pool(live_counts, places, counted, emb_table, pieces, dense_emb, head)
    rank = cross_in.shape[1]
    if even_split:
        early, late, crossed = gather_blocks(factors, jnp.stack(far), crossed)
        rank = rank - 128
    else:
        early, late = gather_whole(factors), None
    begun = first_step(*crossed, bias, head, *zip(*early), rank)
    last = []
    if late:
        last, begun = late(begun)
    logits, even, odd = dense_step(
        live_counts,
        places,
        *crossed,
        head,
        labels.reshape(1, -1),
        counted,
        begun,
        [block for block, _ in last],
        [copy for _, copy in last],
        shards,
        replicas,
    )
    grad = reduce_rows(even, odd)
    update, accum = finish(row_accum.reshape(replicas, block), *replica_gather(grad)[0])
    return (logits.reshape(-1), update, accum.reshape(-1))


def solution(mesh):
    placed = (
        P("table", None),
        P("table"),
        P("replica", "table", None, None, None),
        P("replica", None, None),
        P("replica", "table", None),
        P(("replica", "table"), None),
        P(("replica", "table")),
        P("table", None),
        P("table", None),
        P(),
        P(),
    )
    return jax.shard_map(
        local,
        mesh=mesh,
        in_specs=placed,
        out_specs=(P(("replica", "table")), P("table", None), P("table")),
        check_vma=False,
    )
```

```python
import functools

import jax
import jax.numpy as jnp
from jax import lax
from jax.experimental import pallas as pl
from jax.experimental.pallas import tpu as pltpu
from jax.sharding import PartitionSpec as P

EPSILON = 1e-08
F32, BF16 = jnp.float32, jnp.bfloat16
LOW = 32
UNROLL = 8
HOT = 4
CHUNK = 256
ID_BITS = 10
VMEM_LIMIT = 28 * 1024 * 1024
PACK_LIMIT = 60 * 1024 * 1024


def swap(array, mask):
    size = lax.axis_size("replica")
    return lax.ppermute(array, "replica", [(i, i ^ mask) for i in range(size)])


def cross_over(array, mask):
    size = lax.axis_size("table")
    return lax.ppermute(array, "table", [(i, i ^ mask) for i in range(size)])


def mask_stages(size):
    stages, bit = [(1,)], 1
    while (1 << bit) < size:
        if (2 << bit) < size:
            stages.append((1 << bit, 2 << bit, 3 << bit))
            bit += 2
        else:
            stages.append((1 << bit,))
            bit += 1
    return stages


def replica_gather(piece, *beside):
    held = [piece]
    for masks in reversed(mask_stages(lax.axis_size("replica"))[1:]):
        held = [held] + [[swap(h, mask) for h in held] for mask in masks]
        held = [h for group in held for h in group]
    held, *beside = lax.optimization_barrier((held, *beside))
    order = sorted(range(len(held)), key=lambda i: gather_masks(lax.axis_size("replica"))[i])
    even = jnp.stack([held[i] for i in order])
    return (even, swap(even, 1)), *beside


def gather_masks(size):
    masks = [0]
    for group in reversed(mask_stages(size)[1:]):
        masks = masks + [m ^ mask for mask in group for m in masks]
    return masks


def whole(space=pltpu.VMEM):
    return pl.BlockSpec(memory_space=space)


def slot_range(live_counts, shards, j):
    here = lax.axis_index("table")
    source = here ^ j
    start = jnp.int32(0)
    for s in range(shards):
        start = start + jnp.where(s < source, live_counts[0, here, s], 0)
    return source, start, live_counts[0, here, source]


def pack_kernel(shards, look_rows, table, *refs):
    parcels, done = refs[:-1], refs[-1]
    width = table.shape[1]
    capacity = look_rows.shape[4]
    lines = -(-capacity // width)
    block = parcels[0].shape[0] - HOT // 2 * lines
    mine, here = lax.axis_index("replica"), lax.axis_index("table")
    rows = table.at[pl.ds(pl.multiple_of(mine * block, block), block), :]
    copies = [
        pltpu.make_async_copy(rows, parcel.at[:block, :], done.at[i])
        for i, parcel in enumerate(parcels)
    ]
    for copy in copies:
        copy.start()
    for i, parcel in enumerate(parcels):
        owner = here ^ (i + 1)
        for pair in range(HOT // 2):
            for q in range(lines):
                line = block + pair * lines + q
                size = min(width, capacity - q * width)
                if size < width:
                    parcel[line : line + 1, :] = jnp.zeros((1, width), F32)
                at = slice(q * width, q * width + size)
                value = (look_rows[0, 0, owner, 2 * pair : 2 * pair + 1, at] << ID_BITS) | (
                    look_rows[0, 0, owner, 2 * pair + 1 : 2 * pair + 2, at]
                )
                parcel[line : line + 1, :size] = value.astype(F32)
    for copy in copies:
        copy.wait()


def pack(look_rows, table, shards, replicas):
    rows, width = table.shape
    capacity = look_rows.shape[4]
    lines = HOT // 2 * -(-capacity // width)
    parcel = jax.ShapeDtypeStruct((rows // replicas + lines, width), F32)
    return pl.pallas_call(
        functools.partial(pack_kernel, shards),
        out_shape=[parcel] * (shards - 1),
        in_specs=[whole(), whole(pltpu.HBM)],
        out_specs=[whole()] * (shards - 1),
        scratch_shapes=[pltpu.SemaphoreType.DMA((shards - 1,))],
        compiler_params=pltpu.CompilerParams(vmem_limit_bytes=PACK_LIMIT),
        name="pack",
    )(look_rows, table)


def cut_kernel(first, second, near, corner, done):
    half, lanes = near.shape[0] // 2, near.shape[1]
    mine = lax.axis_index("replica")
    copies = []
    for out, mask in ((near, 0), (corner, 3)):
        for i, factor in enumerate((first, second)):
            at = (
                pl.ds(pl.multiple_of((mine & 1) * half, 16), half),
                pl.ds(pl.multiple_of(((mine >> 1) ^ mask) * lanes, lanes), lanes),
            )
            into = out.at[i * half : (i + 1) * half, :]
            copies.append(pltpu.make_async_copy(factor.at[at], into, done.at[len(copies)]))
    for copy in copies:
        copy.start()
    for copy in copies:
        copy.wait()


def cut(factors):
    rows = factors[0].shape[0]
    return pl.pallas_call(
        cut_kernel,
        out_shape=[jax.ShapeDtypeStruct((r, 128), BF16) for r in (rows, rows)],
        in_specs=[whole(pltpu.HBM)] * 2,
        out_specs=[whole()] * 2,
        scratch_shapes=[pltpu.SemaphoreType.DMA((4,))],
        compiler_params=pltpu.CompilerParams(vmem_limit_bytes=PACK_LIMIT),
        name="cut",
    )(*factors)


def quotient(value, divisor, below):
    shift = 19
    factor = (1 << shift) // divisor + 1
    assert below * factor < 1 << 31
    assert all((v * factor) >> shift == v // divisor for v in range(below))
    return lax.shift_right_logical(value * factor, shift)


def slots_kernel(shards, replicas, batch, live_counts, look_rows, bag_order, *refs):
    parcels, (places, counted, shifted, words) = refs[: shards - 1], refs[shards - 1 :]
    width = parcels[0].shape[1]
    capacity = look_rows.shape[4]
    lines = -(-capacity // width)
    bags = bag_order.shape[2]
    rows = counted.shape[1]
    block = rows // replicas
    field = (1 << ID_BITS) - 1
    slot = lax.broadcasted_iota(jnp.int32, (8, bags), 1)
    ranges = [slot_range(live_counts, shards, j) for j in range(shards)]
    here = lax.axis_index("table")
    shifted[...] = jnp.zeros_like(shifted)
    for j, (source, start, live) in enumerate(ranges):
        for pair in range(HOT // 2):
            for q in range(lines):
                size = min(width, capacity - q * width)

                at = slice(q * width, q * width + size)
                if j == 0:
                    own = [look_rows[0, 0, here, 2 * pair + h : 2 * pair + h + 1, at] for h in (0, 1)]
                    value = (own[0] << ID_BITS) | own[1]
                else:
                    line = block + pair * lines + q
                    value = parcels[j - 1][line : line + 1, :size].astype(jnp.int32)
                shifted[pair : pair + 1, at] = value
        moved = pltpu.roll(shifted[...], start, 1)[:, :bags]
        inside = (slot >= start) & (slot < start + live)
        words[...] = jnp.where(inside, moved, words[...] if j else 0)
    order = bag_order[0]
    sample = quotient(order, bags // batch, bags)
    dest = (order - sample * (bags // batch)) * batch + sample
    for q in range(bags // CHUNK):
        one = dest[:, q * CHUNK : q * CHUNK + CHUNK // 2]
        two = dest[:, q * CHUNK + CHUNK // 2 : (q + 1) * CHUNK]
        places[:, q * CHUNK // 2 : (q + 1) * CHUNK // 2] = one | (two << 16)

    flip = lax.axis_index("replica") * block
    low = lax.broadcasted_iota(jnp.int32, (LOW, CHUNK), 0)
    for source, start, live in ranges:

        def pair(q, _, start=start, live=live, source=source):
            at = pl.ds(pl.multiple_of(q * CHUNK, CHUNK), CHUNK)
            place = q * CHUNK + lax.broadcasted_iota(jnp.int32, (1, CHUNK), 1) - start
            inside = (place >= 0) & (place < live)
            lows, highs = [], []
            for h in range(HOT):
                word = words[h // 2 : h // 2 + 1, at]
                row = (lax.shift_right_logical(word, (h % 2) * ID_BITS) & field) ^ flip
                row = jnp.where(inside, row, -1)
                highs.append(lax.shift_right_arithmetic(row, LOW.bit_length() - 1))
                lows.append((low == (row & (LOW - 1))).astype(F32).astype(BF16))
            for b in range(rows // LOW):
                count = None
                for h in range(HOT):
                    hit = (highs[h] == b).astype(F32).astype(BF16)
                    term = lows[h] * hit
                    count = term if count is None else count + term
                counted[q + source, b * LOW : (b + 1) * LOW, :] = count
            return 0

        lax.fori_loop(start // CHUNK, (start + live + CHUNK - 1) // CHUNK, pair, 0)


def slots(live_counts, look_rows, bag_order, parcels, rows, shards, replicas, batch):
    bags = bag_order.shape[2]
    capacity = -(-look_rows.shape[4] // 128) * 128
    pairs = bags // CHUNK + shards - 1
    return pl.pallas_call(
        functools.partial(slots_kernel, shards, replicas, batch),
        out_shape=[
            jax.ShapeDtypeStruct((1, bags // 2), jnp.int32),
            jax.ShapeDtypeStruct((pairs, rows, CHUNK), BF16),
        ],
        in_specs=[whole(pltpu.SMEM)] + [whole()] * (2 + len(parcels)),
        out_specs=[whole()] * 2,
        scratch_shapes=[
            pltpu.VMEM((8, bags + capacity), jnp.int32),
            pltpu.VMEM((8, bags), jnp.int32),
        ],
        compiler_params=pltpu.CompilerParams(vmem_limit_bytes=VMEM_LIMIT),
        cost_estimate=pl.CostEstimate(flops=1000, bytes_accessed=1000, transcendentals=0),
        name="slots",
    )(live_counts, look_rows, bag_order, *parcels)


def pool_kernel(
    shards, live_counts, places, counted, own, even, odd, dense, head, cross, scaled, table, sums, pooled
):
    rows_dev, width = own.shape
    block = even.shape[2]
    batch = dense.shape[0]
    half = CHUNK // 2
    mine = lax.axis_index("replica")

    def put(shard, rows, value):
        high = value.astype(BF16)
        table[shard, rows, :width] = high
        table[shard, rows, width:] = (value - high.astype(F32)).astype(BF16)

    for m in range(2 * even.shape[0]):
        there = pl.ds(pl.multiple_of((mine ^ m) * block, block), block)
        rows = slice(m * block, (m + 1) * block)
        put(0, rows, own[there, :])
        for k in range(1, shards):
            put(k, rows, (odd if m % 2 else even)[m // 2, k - 1])
    sums[...] = jnp.zeros_like(sums)
    for j in range(shards):
        source, start, live = slot_range(live_counts, shards, j)

        def pair(q, _, j=j, source=source):
            at = pl.ds(pl.multiple_of(q * CHUNK, CHUNK), CHUNK)
            found = lax.dot_general(
                counted[q + source], table[j], (((0,), (0,)), ((), ())), preferred_element_type=F32
            )
            sums[at, :] += found[:, :width] + found[:, width:]
            return 0

        lax.fori_loop(start // CHUNK, (start + live + CHUNK - 1) // CHUNK, pair, 0)

    def group(i, _):
        k0 = i * UNROLL
        k0 = k0 + lax.div(k0, half) * half
        for u in range(UNROLL):
            word = places[0, i * UNROLL + u]
            pooled[pl.ds(word & 0xFFFF, 1), :] = sums[pl.ds(k0 + u, 1), :]
            pooled[pl.ds(lax.shift_right_logical(word, 16), 1), :] = sums[pl.ds(k0 + u + half, 1), :]
        return 0

    lax.fori_loop(0, sums.shape[0] // (2 * UNROLL), group, 0)
    for f in range(cross.shape[1] // width):
        at = slice(f * width, (f + 1) * width)
        block = dense[...] if f == 0 else pooled[(f - 1) * batch : f * batch, :].astype(BF16)
        cross[:, at] = block
        scaled[:, at] = (block.astype(F32) * head[:, at]).astype(BF16)


def pool(live_counts, places, counted, own, pieces, dense, head):
    rows, width = own.shape
    bags = 2 * places.shape[1]
    shards = pieces[0].shape[1] + 1
    smem = whole(pltpu.SMEM)
    return pl.pallas_call(
        functools.partial(pool_kernel, shards),
        out_shape=[jax.ShapeDtypeStruct((dense.shape[0], head.shape[1]), BF16)] * 2,
        in_specs=[smem, smem] + [whole()] * 6,
        out_specs=[whole()] * 2,
        scratch_shapes=[
            pltpu.VMEM((shards, rows, 2 * width), BF16),
            pltpu.VMEM((bags, width), F32),
            pltpu.VMEM((bags, width), F32),
        ],
        compiler_params=pltpu.CompilerParams(vmem_limit_bytes=VMEM_LIMIT),
        cost_estimate=pl.CostEstimate(flops=1000, bytes_accessed=1000, transcendentals=0),
        name="pool",
    )(live_counts, places, counted, own, *pieces, dense, head)


def column_of(row, size):
    eye = lax.broadcasted_iota(jnp.int32, (size, size), 0) == lax.broadcasted_iota(
        jnp.int32, (size, size), 1
    )
    return jnp.sum(jnp.where(eye, jnp.broadcast_to(row, (size, size)), 0.0), axis=1, keepdims=True)


def row_of(column, size):
    eye = lax.broadcasted_iota(jnp.int32, (size, size), 0) == lax.broadcasted_iota(
        jnp.int32, (size, size), 1
    )
    return jnp.sum(
        jnp.where(eye, jnp.broadcast_to(column, (size, size)), 0.0), axis=0, keepdims=True
    )


def first_kernel(copies, cross, scaled, bias, head, *refs):
    weights, (grads, logit, full_in, full_out) = refs[: len(copies)], refs[len(copies) :]
    for ref, copy in zip(weights, copies):
        copy(ref, (full_in, full_out))
    add_rank(cross, scaled, head, full_in, full_out, bias, None, grads, logit)


def add_rank(cross, scaled, head, full_in, full_out, bias, before, grads, logit):
    batch, features = cross.shape
    width = logit.shape[1]
    across = (((1,), (1,)), ((), ()))
    hidden = jnp.dot(cross[...], full_in[...], preferred_element_type=F32).astype(BF16)
    back = jnp.dot(scaled[...], full_out[...], preferred_element_type=F32).astype(BF16)
    step = 3 * width if (features // width) % 3 == 0 else width
    total = jnp.zeros((batch, width), F32) if before is None else before[1][...]
    for n in range(features // step):
        at = slice(n * step, (n + 1) * step)
        mixed = lax.dot_general(hidden, full_out[at, :], across, preferred_element_type=F32)
        if bias is not None:
            mixed = mixed + bias[:, at] + 1.0
        gain = head[:, at] * mixed
        term = cross[:, at].astype(F32) * gain
        grad = gain + lax.dot_general(back, full_in[at, :], across, preferred_element_type=F32)
        for p in range(step // width):
            part = slice(p * width, (p + 1) * width)
            total = total + term[:, part]
            f = n * (step // width) + p
            if f > 0:
                rows = slice((f - 1) * batch, f * batch)
                grads[rows, :] = grad[:, part] + (0.0 if before is None else before[0][rows, :])
    logit[...] = total


def first_step(cross, scaled, bias, head, weights, copies, rank):
    batch, features = cross.shape
    width = 128
    return pl.pallas_call(
        functools.partial(first_kernel, copies),
        out_shape=(
            jax.ShapeDtypeStruct((features // width * batch - batch, width), F32),
            jax.ShapeDtypeStruct((batch, width), F32),
        ),
        in_specs=[whole()] * (4 + len(weights)),
        out_specs=(whole(), whole()),
        scratch_shapes=[pltpu.VMEM((features, rank), BF16)] * 2,
        compiler_params=pltpu.CompilerParams(vmem_limit_bytes=VMEM_LIMIT),
        cost_estimate=pl.CostEstimate(
            flops=2 * 10**9, bytes_accessed=20 * 10**6, transcendentals=0
        ),
        name="first",
    )(cross, scaled, bias, head, *weights)


def dense_kernel(shards, replicas, copies, live_counts, places, cross, scaled, head, labels, counted, *refs):
    begun, partial = refs[:2]
    weights = refs[2 : 2 + len(copies)]
    logits, even, odd, full_in, full_out, grads, logit, slots, narrow, total, spots, done = refs[
        2 + len(copies) :
    ]
    batch = cross.shape[0]
    width = slots.shape[1]
    bags = grads.shape[0]
    rows = total.shape[2]
    here = lax.axis_index("table")
    fetch = pltpu.make_async_copy(places, spots, done)
    fetch.start()

    if copies:
        for ref, copy in zip(weights, copies):
            copy(ref, (full_in, full_out))
        add_rank(cross, scaled, head, full_in, full_out, None, (begun, partial), grads, logit)
    else:
        grads[...] = begun[...]
        logit[...] = partial[...]
    sums = jnp.sum(logit[...], axis=1, keepdims=True)
    logits[...] = row_of(sums, batch)
    lean = jax.nn.sigmoid(sums) - column_of(labels[...].astype(F32), batch)
    for f in range(bags // batch):
        at = slice(f * batch, (f + 1) * batch)
        grads[at, :] = (grads[at, :] * lean).astype(BF16).astype(F32)

    half = CHUNK // 2
    chunks = bags // CHUNK
    total[...] = jnp.zeros_like(total)

    def gather(q):
        for i in range(half):
            word = spots[0, q * half + i]
            slots[i : i + 1, :] = grads[pl.ds(word & 0xFFFF, 1), :]
            slots[i + half : i + half + 1, :] = grads[pl.ds(lax.shift_right_logical(word, 16), 1), :]

    def shard_of(k):
        end, shard = jnp.int32(0), jnp.int32(0)
        for s in range(shards - 1):
            end = end + live_counts[0, here, s]
            shard = shard + jnp.where(k >= end, 1, 0)
        return shard

    def add(q, shard):
        place = here ^ shard
        total[place] += lax.dot_general(
            narrow[...], counted[q + shard], (((0,), (1,)), ((), ())), preferred_element_type=F32
        )

    fetch.wait()
    gather(0)

    def chunk(q, _):
        narrow[...] = slots[...].astype(BF16)
        shard = shard_of(q * CHUNK)
        add(q, shard)
        gather(jnp.minimum(q + 1, chunks - 1))

        def more(s, _):
            add(q, s)
            return 0

        lax.fori_loop(shard + 1, shard_of((q + 1) * CHUNK - 1) + 1, more, 0)
        return 0

    lax.fori_loop(0, chunks, chunk, 0)
    block = rows // replicas
    for j in range(shards):
        for m in range(replicas):
            sums = total[j, :, m * block : (m + 1) * block].T
            (odd if m % 2 else even)[m // 2, j] = sums.astype(BF16)


def dense_step(
    live_counts, places, cross, scaled, head, labels, counted, begun, weights, copies, shards, replicas
):
    batch, features = cross.shape
    width = 128
    bags = begun[0].shape[0]
    rows = counted.shape[1]
    half = jax.ShapeDtypeStruct((replicas // 2, shards, rows // replicas, width), BF16)
    smem = whole(pltpu.SMEM)
    part = pltpu.VMEM((features, width) if copies else (16, width), BF16)
    return pl.pallas_call(
        functools.partial(dense_kernel, shards, replicas, copies),
        out_shape=(jax.ShapeDtypeStruct((1, batch), F32), half, half),
        in_specs=[smem] + [whole()] * (8 + len(weights)),
        out_specs=(whole(), whole(), whole()),
        scratch_shapes=[
            part,
            part,
            pltpu.VMEM((bags, width), F32),
            pltpu.VMEM((batch, width), F32),
            pltpu.VMEM((CHUNK, width), F32),
            pltpu.VMEM((CHUNK, width), BF16),
            pltpu.VMEM((shards, width, rows), F32),
            pltpu.SMEM(places.shape, jnp.int32),
            pltpu.SemaphoreType.DMA(()),
        ],
        compiler_params=pltpu.CompilerParams(vmem_limit_bytes=VMEM_LIMIT),
        cost_estimate=pl.CostEstimate(
            flops=2 * 10**9, bytes_accessed=20 * 10**6, transcendentals=0
        ),
        name="dense",
    )(live_counts, places, cross, scaled, head, labels, counted, *begun, *weights)


def splits_evenly(factor, replicas):
    return replicas == 8 and factor.shape[1] == 4 * 128 and factor.shape[0] % 32 == 0


def gather_whole(factors):
    def spot(which):
        def copy(ref, full):
            full[which][...] = ref[...]

        return copy

    return [
        (lax.all_gather(w, "table", axis=0, tiled=True), spot(i)) for i, w in enumerate(factors)
    ]


def gather_blocks(factors, near, corner, after):
    shards = lax.axis_size("table")
    shard_rows = factors[0].shape[0]
    half, lanes = shard_rows // 2, near.shape[2]
    first, second = swap(near, 2), swap(near, 4)
    first, second, corner, after = lax.optimization_barrier((first, second, corner, after))
    corners = [(swap(first[1:, :half], 4), 0), (swap(second[1:, half:], 2), 1)]
    every = tuple(range(1, shards))

    def put(masks, block, core, column, begin, end):
        def copy(ref, full):
            own, here = lax.axis_index("replica"), lax.axis_index("table")
            for i, mask in enumerate(masks):
                start = (here ^ mask) * shard_rows + ((own & 1) ^ core) * half
                at = pl.ds(pl.multiple_of(start, 16), half)
                for which in range(begin, end):
                    full[which][at, column * lanes : (column + 1) * lanes] = ref[
                        i, (which - begin) * half : (which - begin + 1) * half, :
                    ]

        return block, copy

    def put_own(which, masks):
        def copy(ref, full):
            own, here = lax.axis_index("replica"), lax.axis_index("table")
            at = pl.ds(pl.multiple_of(here * shard_rows, 16), shard_rows)
            for column, mask in enumerate(masks):
                columns = pl.ds(pl.multiple_of(((own >> 1) ^ mask) * lanes, lanes), lanes)
                full[which][at, column * lanes : (column + 1) * lanes] = ref[:, columns]

        return factors[which], copy

    early = [put_own(which, (0, 1, 2)) for which in range(2)]
    for column, block in enumerate((near, first, second)):
        early += [put(every, block, 0, column, 0, 2), put(every, swap(block, 1), 1, column, 0, 2)]

    def late(after):
        blocks, after = lax.optimization_barrier(([c[0] for c in corners], after))
        out = [put_own(which, (3,)) for which in range(2)]
        out += [put((1,), corner, 0, 0, 0, 2), put((1,), swap(corner, 1), 1, 0, 0, 2)]
        for block, (_, which) in zip(blocks, corners):
            out.append(put(every[1:], block, 0, 0, which, which + 1))
            out.append(put(every[1:], swap(block, 1), 1, 0, which, which + 1))
        return out, after

    return early, late, after


def reduce_rows(even, odd):
    shards, replicas = lax.axis_size("table"), lax.axis_size("replica")
    kept = even.astype(F32) + swap(odd, 1).astype(F32)
    for masks in mask_stages(replicas)[1:]:
        split = kept.reshape((-1, len(masks) + 1) + kept.shape[1:])
        kept = split[:, 0]
        for i, mask in enumerate(masks):
            kept = kept + swap(split[:, i + 1].astype(BF16), mask).astype(F32)
    kept = kept[0]
    total = kept[0]
    for k in range(1, shards):
        total = total + cross_over(kept[k].astype(BF16), k).astype(F32)
    return total


def finish_kernel(accum, even, odd, update, fresh):
    count, block, width = even.shape
    mine = lax.axis_index("replica")
    for m in range(2 * count):
        own = mine ^ m
        grad = (odd if m % 2 else even)[m // 2]
        square = jnp.sum(grad * grad, axis=1, keepdims=True) * (1.0 / width)
        row = accum[pl.ds(own, 1), :] + row_of(square, block)
        fresh[pl.ds(own, 1), :] = row
        rows = pl.ds(pl.multiple_of(own * block, block), block)
        update[rows, :] = -grad / (jnp.sqrt(column_of(row, block)) + EPSILON)


def finish(accum, even, odd):
    replicas, block = accum.shape
    width = even.shape[2]
    return pl.pallas_call(
        finish_kernel,
        out_shape=(
            jax.ShapeDtypeStruct((replicas * block, width), F32),
            jax.ShapeDtypeStruct((replicas, block), F32),
        ),
        in_specs=[whole()] * 3,
        out_specs=(whole(), whole()),
        compiler_params=pltpu.CompilerParams(vmem_limit_bytes=VMEM_LIMIT),
        name="finish",
    )(accum, even, odd)


def local(
    emb_table,
    row_accum,
    look_rows,
    live_counts,
    bag_order,
    dense_emb,
    labels,
    cross_in,
    cross_out,
    cross_bias,
    head_weight,
):
    shards, replicas = lax.axis_size("table"), lax.axis_size("replica")
    rows = emb_table.shape[0]
    block = rows // replicas
    batch = dense_emb.shape[0]
    factors = (cross_in, cross_out)
    even_split = splits_evenly(cross_in, replicas)

    packed = pack(look_rows, emb_table, shards, replicas)
    parcels = [cross_over(p, k + 1) for k, p in enumerate(packed)]
    far = []
    if even_split:
        parcels, blocks = lax.optimization_barrier((parcels, cut(factors)))
        far = jnp.stack([cross_over(blocks[0], k) for k in range(1, shards)])
        corner = cross_over(blocks[1], 1)[None]
    places, counted = slots(
        live_counts, look_rows, bag_order, parcels, rows, shards, replicas, batch
    )
    pieces, far, counted = replica_gather(
        jnp.stack([p[:block] for p in parcels]), far, counted
    )
    bias, head = cross_bias.reshape(1, -1), head_weight.reshape(1, -1)
    crossed = pool(live_counts, places, counted, emb_table, pieces, dense_emb, head)
    rank = cross_in.shape[1]
    if even_split:
        early, late, crossed = gather_blocks(factors, far, corner, crossed)
        rank = rank - 128
    else:
        early, late = gather_whole(factors), None
    begun = first_step(*crossed, bias, head, *zip(*early), rank)
    last = []
    if late:
        last, begun = late(begun)
    logits, even, odd = dense_step(
        live_counts,
        places,
        *crossed,
        head,
        labels.reshape(1, -1),
        counted,
        begun,
        [block for block, _ in last],
        [copy for _, copy in last],
        shards,
        replicas,
    )
    grad = reduce_rows(even, odd)
    update, accum = finish(row_accum.reshape(replicas, block), *replica_gather(grad)[0])
    return (logits.reshape(-1), update, accum.reshape(-1))


def solution(mesh):
    placed = (
        P("table", None),
        P("table"),
        P("replica", "table", None, None, None),
        P("replica", None, None),
        P("replica", "table", None),
        P(("replica", "table"), None),
        P(("replica", "table")),
        P("table", None),
        P("table", None),
        P(),
        P(),
    )
    return jax.shard_map(
        local,
        mesh=mesh,
        in_specs=placed,
        out_specs=(P(("replica", "table")), P("table", None), P("table")),
        check_vma=False,
    )
```

```python
import functools

import jax
import jax.numpy as jnp
from jax import lax
from jax.experimental import pallas as pl
from jax.experimental.pallas import tpu as pltpu
from jax.sharding import PartitionSpec as P

EPSILON = 1e-08
F32, BF16 = jnp.float32, jnp.bfloat16
LOW = 32
UNROLL = 8
HOT = 4
CHUNK = 256
ID_BITS = 10
VMEM_LIMIT = 28 * 1024 * 1024
PACK_LIMIT = 60 * 1024 * 1024


def swap(array, mask):
    size = lax.axis_size("replica")
    return lax.ppermute(array, "replica", [(i, i ^ mask) for i in range(size)])


def cross_over(array, mask):
    size = lax.axis_size("table")
    return lax.ppermute(array, "table", [(i, i ^ mask) for i in range(size)])


def mask_stages(size):
    stages, bit = [(1,)], 1
    while (1 << bit) < size:
        if (2 << bit) < size:
            stages.append((1 << bit, 2 << bit, 3 << bit))
            bit += 2
        else:
            stages.append((1 << bit,))
            bit += 1
    return stages


def replica_gather(piece, *beside):
    held = [piece]
    for masks in reversed(mask_stages(lax.axis_size("replica"))[1:]):
        held = [held] + [[swap(h, mask) for h in held] for mask in masks]
        held = [h for group in held for h in group]
    held, *beside = lax.optimization_barrier((held, *beside))
    order = sorted(range(len(held)), key=lambda i: gather_masks(lax.axis_size("replica"))[i])
    even = jnp.stack([held[i] for i in order])
    return (even, swap(even, 1)), *beside


def gather_masks(size):
    masks = [0]
    for group in reversed(mask_stages(size)[1:]):
        masks = masks + [m ^ mask for mask in group for m in masks]
    return masks


def whole(space=pltpu.VMEM):
    return pl.BlockSpec(memory_space=space)


def slot_range(info, shards, j):
    source = lax.axis_index("table") ^ j
    start = jnp.int32(0)
    for s in range(shards):
        start = start + jnp.where(s < source, info[0, s], 0)
    return source, start, info[0, source]


def pack_kernel(shards, look_rows, table, *refs):
    parcels, done = refs[:-1], refs[-1]
    width = table.shape[1]
    capacity = look_rows.shape[4]
    lines = -(-capacity // width)
    block = parcels[0].shape[0] - HOT // 2 * lines
    mine, here = lax.axis_index("replica"), lax.axis_index("table")
    rows = table.at[pl.ds(pl.multiple_of(mine * block, block), block), :]
    copies = [
        pltpu.make_async_copy(rows, parcel.at[:block, :], done.at[i])
        for i, parcel in enumerate(parcels)
    ]
    for copy in copies:
        copy.start()
    for i, parcel in enumerate(parcels):
        owner = here ^ (i + 1)
        for pair in range(HOT // 2):
            for q in range(lines):
                line = block + pair * lines + q
                size = min(width, capacity - q * width)
                if size < width:
                    parcel[line : line + 1, :] = jnp.zeros((1, width), F32)
                at = slice(q * width, q * width + size)
                value = (look_rows[0, 0, owner, 2 * pair : 2 * pair + 1, at] << ID_BITS) | (
                    look_rows[0, 0, owner, 2 * pair + 1 : 2 * pair + 2, at]
                )
                parcel[line : line + 1, :size] = value.astype(F32)
    for copy in copies:
        copy.wait()


def pack(look_rows, table, shards, replicas):
    rows, width = table.shape
    capacity = look_rows.shape[4]
    lines = HOT // 2 * -(-capacity // width)
    parcel = jax.ShapeDtypeStruct((rows // replicas + lines, width), F32)
    return pl.pallas_call(
        functools.partial(pack_kernel, shards),
        out_shape=[parcel] * (shards - 1),
        in_specs=[whole(), whole(pltpu.HBM)],
        out_specs=[whole()] * (shards - 1),
        scratch_shapes=[pltpu.SemaphoreType.DMA((shards - 1,))],
        compiler_params=pltpu.CompilerParams(vmem_limit_bytes=PACK_LIMIT),
        name="pack",
    )(look_rows, table)


def cut_kernel(first, second, near, corner, done):
    half, lanes = near.shape[0] // 2, near.shape[1]
    mine = lax.axis_index("replica")
    copies = []
    for out, mask in ((near, 0), (corner, 3)):
        for i, factor in enumerate((first, second)):
            at = (
                pl.ds(pl.multiple_of((mine & 1) * half, 16), half),
                pl.ds(pl.multiple_of(((mine >> 1) ^ mask) * lanes, lanes), lanes),
            )
            into = out.at[i * half : (i + 1) * half, :]
            copies.append(pltpu.make_async_copy(factor.at[at], into, done.at[len(copies)]))
    for copy in copies:
        copy.start()
    for copy in copies:
        copy.wait()


def cut(factors):
    rows = factors[0].shape[0]
    return pl.pallas_call(
        cut_kernel,
        out_shape=[jax.ShapeDtypeStruct((r, 128), BF16) for r in (rows, rows)],
        in_specs=[whole(pltpu.HBM)] * 2,
        out_specs=[whole()] * 2,
        scratch_shapes=[pltpu.SemaphoreType.DMA((4,))],
        compiler_params=pltpu.CompilerParams(vmem_limit_bytes=PACK_LIMIT),
        name="cut",
    )(*factors)


def quotient(value, divisor, below):
    shift = 19
    factor = (1 << shift) // divisor + 1
    assert below * factor < 1 << 31
    assert all((v * factor) >> shift == v // divisor for v in range(below))
    return lax.shift_right_logical(value * factor, shift)


def split_rows(value):
    high = value.astype(BF16)
    return high, (value - high.astype(F32)).astype(BF16)


def ready_kernel(
    shards, live_counts, look_rows, bag_order, dense, head, places, info, words, lead
):
    batch, width = dense.shape
    capacity = look_rows.shape[4]
    bags = bag_order.shape[2]
    here = lax.axis_index("table")
    order = bag_order[0]
    sample = quotient(order, bags // batch, bags)
    dest = (order - sample * (bags // batch)) * batch + sample
    for q in range(bags // CHUNK):
        one = dest[:, q * CHUNK : q * CHUNK + CHUNK // 2]
        two = dest[:, q * CHUNK + CHUNK // 2 : (q + 1) * CHUNK]
        places[:, q * CHUNK // 2 : (q + 1) * CHUNK // 2] = one | (two << 16)
    lane = lax.broadcasted_iota(jnp.int32, info.shape, 1)
    counts = jnp.zeros(info.shape, jnp.int32)
    for s in range(shards):
        counts = jnp.where(lane == s, live_counts[0, here, s], counts)
    info[...] = counts
    words[...] = jnp.zeros_like(words)
    for pair in range(HOT // 2):
        words[pair : pair + 1, :capacity] = (
            look_rows[0, 0, here, 2 * pair : 2 * pair + 1, :] << ID_BITS
        ) | look_rows[0, 0, here, 2 * pair + 1 : 2 * pair + 2, :]
    lead[:, :width] = dense[...]
    lead[:, width:] = (dense[...].astype(F32) * head[:, :width]).astype(BF16)


def ready(live_counts, look_rows, bag_order, dense, head, shards):
    batch, width = dense.shape
    bags = bag_order.shape[2]
    padded = -(-look_rows.shape[4] // width) * width
    return pl.pallas_call(
        functools.partial(ready_kernel, shards),
        out_shape=[
            jax.ShapeDtypeStruct((1, bags // 2), jnp.int32),
            jax.ShapeDtypeStruct((1, 128), jnp.int32),
            jax.ShapeDtypeStruct((8, padded), jnp.int32),
            jax.ShapeDtypeStruct((batch, 2 * width), BF16),
        ],
        in_specs=[whole(pltpu.SMEM)] + [whole()] * 4,
        out_specs=[whole()] * 4,
        compiler_params=pltpu.CompilerParams(vmem_limit_bytes=VMEM_LIMIT),
        cost_estimate=pl.CostEstimate(flops=1000, bytes_accessed=1000, transcendentals=0),
        name="ready",
    )(live_counts, look_rows, bag_order, dense, head)


def own_kernel(replicas, table, own):
    rows, width = table.shape
    block = rows // replicas
    mine = lax.axis_index("replica")
    for m in range(replicas):
        there = pl.ds(pl.multiple_of((mine ^ m) * block, block), block)
        at = slice(m * block, (m + 1) * block)
        own[at, :width], own[at, width:] = split_rows(table[there, :])


def split_own(table, replicas):
    rows, width = table.shape
    return pl.pallas_call(
        functools.partial(own_kernel, replicas),
        out_shape=jax.ShapeDtypeStruct((rows, 2 * width), BF16),
        in_specs=[whole()],
        out_specs=whole(),
        compiler_params=pltpu.CompilerParams(vmem_limit_bytes=VMEM_LIMIT),
        cost_estimate=pl.CostEstimate(flops=1000, bytes_accessed=1000, transcendentals=0),
        name="split_own",
    )(table)


def slots_kernel(shards, replicas, bags, info, own, *refs):
    parcels, (counted, shifted, words) = refs[: shards - 1], refs[shards - 1 :]
    width = parcels[0].shape[1]
    padded = own.shape[1]
    rows = counted.shape[1]
    block = rows // replicas
    field = (1 << ID_BITS) - 1
    slot = lax.broadcasted_iota(jnp.int32, (8, bags), 1)
    ranges = [slot_range(info, shards, j) for j in range(shards)]
    shifted[...] = jnp.zeros_like(shifted)
    for j, (source, start, live) in enumerate(ranges):
        if j == 0:
            shifted[:, :padded] = own[...]
        else:
            for pair in range(HOT // 2):
                for q in range(padded // width):
                    line = block + pair * (padded // width) + q
                    shifted[pair : pair + 1, q * width : (q + 1) * width] = parcels[j - 1][
                        line : line + 1, :
                    ].astype(jnp.int32)
        moved = pltpu.roll(shifted[...], start, 1)[:, :bags]
        inside = (slot >= start) & (slot < start + live)
        words[...] = jnp.where(inside, moved, words[...] if j else 0)

    flip = lax.axis_index("replica") * block
    low = lax.broadcasted_iota(jnp.int32, (LOW, CHUNK), 0)
    for source, start, live in ranges:

        def pair(q, _, start=start, live=live, source=source):
            at = pl.ds(pl.multiple_of(q * CHUNK, CHUNK), CHUNK)
            place = q * CHUNK + lax.broadcasted_iota(jnp.int32, (1, CHUNK), 1) - start
            inside = (place >= 0) & (place < live)
            lows, highs = [], []
            for h in range(HOT):
                word = words[h // 2 : h // 2 + 1, at]
                row = (lax.shift_right_logical(word, (h % 2) * ID_BITS) & field) ^ flip
                row = jnp.where(inside, row, -1)
                highs.append(lax.shift_right_arithmetic(row, LOW.bit_length() - 1))
                lows.append((low == (row & (LOW - 1))).astype(F32).astype(BF16))
            for b in range(rows // LOW):
                count = None
                for h in range(HOT):
                    hit = (highs[h] == b).astype(F32).astype(BF16)
                    term = lows[h] * hit
                    count = term if count is None else count + term
                counted[q + source, b * LOW : (b + 1) * LOW, :] = count
            return 0

        lax.fori_loop(start // CHUNK, (start + live + CHUNK - 1) // CHUNK, pair, 0)


def slots(info, own, parcels, bags, rows, shards, replicas):
    pairs = bags // CHUNK + shards - 1
    return pl.pallas_call(
        functools.partial(slots_kernel, shards, replicas, bags),
        out_shape=jax.ShapeDtypeStruct((pairs, rows, CHUNK), BF16),
        in_specs=[whole(pltpu.SMEM)] + [whole()] * (1 + len(parcels)),
        out_specs=whole(),
        scratch_shapes=[
            pltpu.VMEM((8, bags + own.shape[1]), jnp.int32),
            pltpu.VMEM((8, bags), jnp.int32),
        ],
        compiler_params=pltpu.CompilerParams(vmem_limit_bytes=VMEM_LIMIT),
        cost_estimate=pl.CostEstimate(flops=1000, bytes_accessed=1000, transcendentals=0),
        name="slots",
    )(info, own, *parcels)


def pool_kernel(
    shards, info, places, counted, own, even, odd, lead, head, cross, scaled, table, sums, pooled
):
    width = lead.shape[1] // 2
    block = even.shape[2]
    batch = lead.shape[0]
    half = CHUNK // 2
    for m in range(2 * even.shape[0]):
        at = slice(m * block, (m + 1) * block)
        for k in range(1, shards):
            value = (odd if m % 2 else even)[m // 2, k - 1]
            table[k - 1, at, :width], table[k - 1, at, width:] = split_rows(value)
    sums[...] = jnp.zeros_like(sums)
    for j in range(shards):
        source, start, live = slot_range(info, shards, j)
        found_in = own if j == 0 else table.at[j - 1]

        def pair(q, _, found_in=found_in, source=source):
            at = pl.ds(pl.multiple_of(q * CHUNK, CHUNK), CHUNK)
            found = lax.dot_general(
                counted[q + source], found_in[...], (((0,), (0,)), ((), ())), preferred_element_type=F32
            )
            sums[at, :] += found[:, :width] + found[:, width:]
            return 0

        lax.fori_loop(start // CHUNK, (start + live + CHUNK - 1) // CHUNK, pair, 0)

    def group(i, _):
        k0 = i * UNROLL
        k0 = k0 + lax.div(k0, half) * half
        for u in range(UNROLL):
            word = places[0, i * UNROLL + u]
            pooled[pl.ds(word & 0xFFFF, 1), :] = sums[pl.ds(k0 + u, 1), :]
            pooled[pl.ds(lax.shift_right_logical(word, 16), 1), :] = sums[pl.ds(k0 + u + half, 1), :]
        return 0

    lax.fori_loop(0, sums.shape[0] // (2 * UNROLL), group, 0)
    cross[:, :width] = lead[:, :width]
    scaled[:, :width] = lead[:, width:]
    for f in range(1, cross.shape[1] // width):
        at = slice(f * width, (f + 1) * width)
        value = pooled[(f - 1) * batch : f * batch, :].astype(BF16)
        cross[:, at] = value
        scaled[:, at] = (value.astype(F32) * head[:, at]).astype(BF16)


def pool(info, places, counted, own, pieces, lead, head):
    rows, width = own.shape[0], own.shape[1] // 2
    bags = 2 * places.shape[1]
    shards = pieces[0].shape[1] + 1
    smem = whole(pltpu.SMEM)
    return pl.pallas_call(
        functools.partial(pool_kernel, shards),
        out_shape=[jax.ShapeDtypeStruct((lead.shape[0], head.shape[1]), BF16)] * 2,
        in_specs=[smem, smem] + [whole()] * 6,
        out_specs=[whole()] * 2,
        scratch_shapes=[
            pltpu.VMEM((shards - 1, rows, 2 * width), BF16),
            pltpu.VMEM((bags, width), F32),
            pltpu.VMEM((bags, width), F32),
        ],
        compiler_params=pltpu.CompilerParams(vmem_limit_bytes=VMEM_LIMIT),
        cost_estimate=pl.CostEstimate(flops=1000, bytes_accessed=1000, transcendentals=0),
        name="pool",
    )(info, places, counted, own, *pieces, lead, head)


def column_of(row, size):
    eye = lax.broadcasted_iota(jnp.int32, (size, size), 0) == lax.broadcasted_iota(
        jnp.int32, (size, size), 1
    )
    return jnp.sum(jnp.where(eye, jnp.broadcast_to(row, (size, size)), 0.0), axis=1, keepdims=True)


def row_of(column, size):
    eye = lax.broadcasted_iota(jnp.int32, (size, size), 0) == lax.broadcasted_iota(
        jnp.int32, (size, size), 1
    )
    return jnp.sum(
        jnp.where(eye, jnp.broadcast_to(column, (size, size)), 0.0), axis=0, keepdims=True
    )


def first_kernel(copies, cross, scaled, bias, head, *refs):
    weights, (grads, logit, full_in, full_out) = refs[: len(copies)], refs[len(copies) :]
    for ref, copy in zip(weights, copies):
        copy(ref, (full_in, full_out))
    add_rank(cross, scaled, head, full_in, full_out, bias, None, grads, logit)


def add_rank(cross, scaled, head, full_in, full_out, bias, before, grads, logit):
    batch, features = cross.shape
    width = logit.shape[1]
    across = (((1,), (1,)), ((), ()))
    hidden = jnp.dot(cross[...], full_in[...], preferred_element_type=F32).astype(BF16)
    back = jnp.dot(scaled[...], full_out[...], preferred_element_type=F32).astype(BF16)
    step = 3 * width if (features // width) % 3 == 0 else width
    total = jnp.zeros((batch, width), F32) if before is None else before[1][...]
    for n in range(features // step):
        at = slice(n * step, (n + 1) * step)
        mixed = lax.dot_general(hidden, full_out[at, :], across, preferred_element_type=F32)
        if bias is not None:
            mixed = mixed + bias[:, at] + 1.0
        gain = head[:, at] * mixed
        term = cross[:, at].astype(F32) * gain
        grad = gain + lax.dot_general(back, full_in[at, :], across, preferred_element_type=F32)
        for p in range(step // width):
            part = slice(p * width, (p + 1) * width)
            total = total + term[:, part]
            f = n * (step // width) + p
            if f > 0:
                rows = slice((f - 1) * batch, f * batch)
                grads[rows, :] = grad[:, part] + (0.0 if before is None else before[0][rows, :])
    logit[...] = total


def first_step(cross, scaled, bias, head, weights, copies, rank):
    batch, features = cross.shape
    width = 128
    return pl.pallas_call(
        functools.partial(first_kernel, copies),
        out_shape=(
            jax.ShapeDtypeStruct((features // width * batch - batch, width), F32),
            jax.ShapeDtypeStruct((batch, width), F32),
        ),
        in_specs=[whole()] * (4 + len(weights)),
        out_specs=(whole(), whole()),
        scratch_shapes=[pltpu.VMEM((features, rank), BF16)] * 2,
        compiler_params=pltpu.CompilerParams(vmem_limit_bytes=VMEM_LIMIT),
        cost_estimate=pl.CostEstimate(
            flops=2 * 10**9, bytes_accessed=20 * 10**6, transcendentals=0
        ),
        name="first",
    )(cross, scaled, bias, head, *weights)


def dense_kernel(shards, replicas, copies, info, places, cross, scaled, head, labels, counted, *refs):
    begun, partial = refs[:2]
    weights = refs[2 : 2 + len(copies)]
    logits, even, odd, full_in, full_out, grads, logit, slots, narrow, total, spots, done = refs[
        2 + len(copies) :
    ]
    batch = cross.shape[0]
    width = slots.shape[1]
    bags = grads.shape[0]
    rows = total.shape[2]
    here = lax.axis_index("table")
    fetch = pltpu.make_async_copy(places, spots, done)
    fetch.start()

    if copies:
        for ref, copy in zip(weights, copies):
            copy(ref, (full_in, full_out))
        add_rank(cross, scaled, head, full_in, full_out, None, (begun, partial), grads, logit)
    else:
        grads[...] = begun[...]
        logit[...] = partial[...]
    sums = jnp.sum(logit[...], axis=1, keepdims=True)
    logits[...] = row_of(sums, batch)
    lean = jax.nn.sigmoid(sums) - column_of(labels[...].astype(F32), batch)
    for f in range(bags // batch):
        at = slice(f * batch, (f + 1) * batch)
        grads[at, :] = (grads[at, :] * lean).astype(BF16).astype(F32)

    half = CHUNK // 2
    chunks = bags // CHUNK
    total[...] = jnp.zeros_like(total)

    def gather(q):
        for i in range(half):
            word = spots[0, q * half + i]
            slots[i : i + 1, :] = grads[pl.ds(word & 0xFFFF, 1), :]
            slots[i + half : i + half + 1, :] = grads[pl.ds(lax.shift_right_logical(word, 16), 1), :]

    def shard_of(k):
        end, shard = jnp.int32(0), jnp.int32(0)
        for s in range(shards - 1):
            end = end + info[0, s]
            shard = shard + jnp.where(k >= end, 1, 0)
        return shard

    def add(q, shard):
        place = here ^ shard
        total[place] += lax.dot_general(
            narrow[...], counted[q + shard], (((0,), (1,)), ((), ())), preferred_element_type=F32
        )

    fetch.wait()
    gather(0)

    def chunk(q, _):
        narrow[...] = slots[...].astype(BF16)
        shard = shard_of(q * CHUNK)
        add(q, shard)
        gather(jnp.minimum(q + 1, chunks - 1))

        def more(s, _):
            add(q, s)
            return 0

        lax.fori_loop(shard + 1, shard_of((q + 1) * CHUNK - 1) + 1, more, 0)
        return 0

    lax.fori_loop(0, chunks, chunk, 0)
    block = rows // replicas
    for j in range(shards):
        for m in range(replicas):
            sums = total[j, :, m * block : (m + 1) * block].T
            (odd if m % 2 else even)[m // 2, j] = sums.astype(BF16)


def dense_step(
    info, places, cross, scaled, head, labels, counted, begun, weights, copies, shards, replicas
):
    batch, features = cross.shape
    width = 128
    bags = begun[0].shape[0]
    rows = counted.shape[1]
    half = jax.ShapeDtypeStruct((replicas // 2, shards, rows // replicas, width), BF16)
    smem = whole(pltpu.SMEM)
    part = pltpu.VMEM((features, width) if copies else (16, width), BF16)
    return pl.pallas_call(
        functools.partial(dense_kernel, shards, replicas, copies),
        out_shape=(jax.ShapeDtypeStruct((1, batch), F32), half, half),
        in_specs=[smem] + [whole()] * (8 + len(weights)),
        out_specs=(whole(), whole(), whole()),
        scratch_shapes=[
            part,
            part,
            pltpu.VMEM((bags, width), F32),
            pltpu.VMEM((batch, width), F32),
            pltpu.VMEM((CHUNK, width), F32),
            pltpu.VMEM((CHUNK, width), BF16),
            pltpu.VMEM((shards, width, rows), F32),
            pltpu.SMEM(places.shape, jnp.int32),
            pltpu.SemaphoreType.DMA(()),
        ],
        compiler_params=pltpu.CompilerParams(vmem_limit_bytes=VMEM_LIMIT),
        cost_estimate=pl.CostEstimate(
            flops=2 * 10**9, bytes_accessed=20 * 10**6, transcendentals=0
        ),
        name="dense",
    )(info, places, cross, scaled, head, labels, counted, *begun, *weights)


def splits_evenly(factor, replicas):
    return replicas == 8 and factor.shape[1] == 4 * 128 and factor.shape[0] % 32 == 0


def gather_whole(factors):
    def spot(which):
        def copy(ref, full):
            full[which][...] = ref[...]

        return copy

    return [
        (lax.all_gather(w, "table", axis=0, tiled=True), spot(i)) for i, w in enumerate(factors)
    ]


def gather_blocks(factors, near, corner, after):
    shards = lax.axis_size("table")
    shard_rows = factors[0].shape[0]
    half, lanes = shard_rows // 2, near.shape[2]
    first, second = swap(near, 2), swap(near, 4)
    first, second, corner, after = lax.optimization_barrier((first, second, corner, after))
    corners = [(swap(first[1:, :half], 4), 0), (swap(second[1:, half:], 2), 1)]
    every = tuple(range(1, shards))

    def put(masks, block, core, column, begin, end):
        def copy(ref, full):
            own, here = lax.axis_index("replica"), lax.axis_index("table")
            for i, mask in enumerate(masks):
                start = (here ^ mask) * shard_rows + ((own & 1) ^ core) * half
                at = pl.ds(pl.multiple_of(start, 16), half)
                for which in range(begin, end):
                    full[which][at, column * lanes : (column + 1) * lanes] = ref[
                        i, (which - begin) * half : (which - begin + 1) * half, :
                    ]

        return block, copy

    def put_own(which, masks):
        def copy(ref, full):
            own, here = lax.axis_index("replica"), lax.axis_index("table")
            at = pl.ds(pl.multiple_of(here * shard_rows, 16), shard_rows)
            for column, mask in enumerate(masks):
                columns = pl.ds(pl.multiple_of(((own >> 1) ^ mask) * lanes, lanes), lanes)
                full[which][at, column * lanes : (column + 1) * lanes] = ref[:, columns]

        return factors[which], copy

    early = [put_own(which, (0, 1, 2)) for which in range(2)]
    for column, block in enumerate((near, first, second)):
        early += [put(every, block, 0, column, 0, 2), put(every, swap(block, 1), 1, column, 0, 2)]

    def late(after):
        blocks, after = lax.optimization_barrier(([c[0] for c in corners], after))
        out = [put_own(which, (3,)) for which in range(2)]
        out += [put((1,), corner, 0, 0, 0, 2), put((1,), swap(corner, 1), 1, 0, 0, 2)]
        for block, (_, which) in zip(blocks, corners):
            out.append(put(every[1:], block, 0, 0, which, which + 1))
            out.append(put(every[1:], swap(block, 1), 1, 0, which, which + 1))
        return out, after

    return early, late, after


def reduce_rows(even, odd):
    shards, replicas = lax.axis_size("table"), lax.axis_size("replica")
    kept = even.astype(F32) + swap(odd, 1).astype(F32)
    for masks in mask_stages(replicas)[1:]:
        split = kept.reshape((-1, len(masks) + 1) + kept.shape[1:])
        kept = split[:, 0]
        for i, mask in enumerate(masks):
            kept = kept + swap(split[:, i + 1].astype(BF16), mask).astype(F32)
    kept = kept[0]
    total = kept[0]
    for k in range(1, shards):
        total = total + cross_over(kept[k].astype(BF16), k).astype(F32)
    return total


def finish_kernel(accum, even, odd, update, fresh):
    count, block, width = even.shape
    mine = lax.axis_index("replica")
    for m in range(2 * count):
        own = mine ^ m
        grad = (odd if m % 2 else even)[m // 2]
        square = jnp.sum(grad * grad, axis=1, keepdims=True) * (1.0 / width)
        row = accum[pl.ds(own, 1), :] + row_of(square, block)
        fresh[pl.ds(own, 1), :] = row
        rows = pl.ds(pl.multiple_of(own * block, block), block)
        update[rows, :] = -grad / (jnp.sqrt(column_of(row, block)) + EPSILON)


def finish(accum, even, odd):
    replicas, block = accum.shape
    width = even.shape[2]
    return pl.pallas_call(
        finish_kernel,
        out_shape=(
            jax.ShapeDtypeStruct((replicas * block, width), F32),
            jax.ShapeDtypeStruct((replicas, block), F32),
        ),
        in_specs=[whole()] * 3,
        out_specs=(whole(), whole()),
        compiler_params=pltpu.CompilerParams(vmem_limit_bytes=VMEM_LIMIT),
        name="finish",
    )(accum, even, odd)


def local(
    emb_table,
    row_accum,
    look_rows,
    live_counts,
    bag_order,
    dense_emb,
    labels,
    cross_in,
    cross_out,
    cross_bias,
    head_weight,
):
    shards, replicas = lax.axis_size("table"), lax.axis_size("replica")
    rows = emb_table.shape[0]
    block = rows // replicas
    batch = dense_emb.shape[0]
    factors = (cross_in, cross_out)
    even_split = splits_evenly(cross_in, replicas)

    packed = pack(look_rows, emb_table, shards, replicas)
    parcels = [cross_over(p, k + 1) for k, p in enumerate(packed)]
    bias, head, label_row = (x.reshape(1, -1) for x in (cross_bias, head_weight, labels))
    prepared = ready(live_counts, look_rows, bag_order, dense_emb, head, shards)
    parcels, prepared, blocks = lax.optimization_barrier(
        (parcels, prepared, cut(factors) if even_split else [])
    )
    places, info, own_words, lead = prepared
    far, corner = [], []
    if even_split:
        far = jnp.stack([cross_over(blocks[0], k) for k in range(1, shards)])
        corner = cross_over(blocks[1], 1)[None]
    counted = slots(info, own_words, parcels, bag_order.shape[2], rows, shards, replicas)
    pieces, far, counted, own_rows = replica_gather(
        jnp.stack([p[:block] for p in parcels]), far, counted, split_own(emb_table, replicas)
    )
    crossed = pool(info, places, counted, own_rows, pieces, lead, head)
    rank = cross_in.shape[1]
    if even_split:
        early, late, crossed = gather_blocks(factors, far, corner, crossed)
        rank = rank - 128
    else:
        early, late = gather_whole(factors), None
    begun = first_step(*crossed, bias, head, *zip(*early), rank)
    last = []
    if late:
        last, begun = late(begun)
    logits, even, odd = dense_step(
        info,
        places,
        *crossed,
        head,
        label_row,
        counted,
        begun,
        [block for block, _ in last],
        [copy for _, copy in last],
        shards,
        replicas,
    )
    grad = reduce_rows(even, odd)
    update, accum = finish(row_accum.reshape(replicas, block), *replica_gather(grad)[0])
    return (logits.reshape(-1), update, accum.reshape(-1))


def solution(mesh):
    placed = (
        P("table", None),
        P("table"),
        P("replica", "table", None, None, None),
        P("replica", None, None),
        P("replica", "table", None),
        P(("replica", "table"), None),
        P(("replica", "table")),
        P("table", None),
        P("table", None),
        P(),
        P(),
    )
    return jax.shard_map(
        local,
        mesh=mesh,
        in_specs=placed,
        out_specs=(P(("replica", "table")), P("table", None), P("table")),
        check_vma=False,
    )
```

```python
import functools

import jax
import jax.numpy as jnp
from jax import lax
from jax.experimental import pallas as pl
from jax.experimental.pallas import tpu as pltpu
from jax.sharding import PartitionSpec as P

EPSILON = 1e-08
F32, BF16 = jnp.float32, jnp.bfloat16
LOW = 32
UNROLL = 8
HOT = 4
CHUNK = 256
ID_BITS = 10
VMEM_LIMIT = 28 * 1024 * 1024
PACK_LIMIT = 60 * 1024 * 1024


def swap(array, mask):
    size = lax.axis_size("replica")
    return lax.ppermute(array, "replica", [(i, i ^ mask) for i in range(size)])


def cross_over(array, mask):
    size = lax.axis_size("table")
    return lax.ppermute(array, "table", [(i, i ^ mask) for i in range(size)])


def mask_stages(size):
    stages, bit = [(1,)], 1
    while (1 << bit) < size:
        if (2 << bit) < size:
            stages.append((1 << bit, 2 << bit, 3 << bit))
            bit += 2
        else:
            stages.append((1 << bit,))
            bit += 1
    return stages


def replica_gather(piece, *beside):
    held = [piece]
    for masks in reversed(mask_stages(lax.axis_size("replica"))[1:]):
        held = [held] + [[swap(h, mask) for h in held] for mask in masks]
        held = [h for group in held for h in group]
    held, *beside = lax.optimization_barrier((held, *beside))
    order = sorted(range(len(held)), key=lambda i: gather_masks(lax.axis_size("replica"))[i])
    even = jnp.stack([held[i] for i in order])
    return (even, swap(even, 1)), *beside


def gather_masks(size):
    masks = [0]
    for group in reversed(mask_stages(size)[1:]):
        masks = masks + [m ^ mask for mask in group for m in masks]
    return masks


def whole(space=pltpu.VMEM):
    return pl.BlockSpec(memory_space=space)


def slot_range(info, shards, j):
    source = lax.axis_index("table") ^ j
    start = jnp.int32(0)
    for s in range(shards):
        start = start + jnp.where(s < source, info[0, s], 0)
    return source, start, info[0, source]


def pack_kernel(shards, look_rows, table, *refs):
    parcels, (ids, done) = refs[:-2], refs[-2:]
    width = table.shape[1]
    capacity = look_rows.shape[4]
    lines = -(-capacity // width)
    block = parcels[0].shape[0] - HOT // 2 * lines
    mine, here = lax.axis_index("replica"), lax.axis_index("table")
    rows = table.at[pl.ds(pl.multiple_of(mine * block, block), block), :]
    copies = [
        pltpu.make_async_copy(rows, parcel.at[:block, :], done.at[i])
        for i, parcel in enumerate(parcels)
    ]
    reads = [
        pltpu.make_async_copy(look_rows.at[0, 0, here ^ (i + 1)], ids.at[i], done.at[shards - 1 + i])
        for i in range(shards - 1)
    ]
    for copy in reads + copies:
        copy.start()
    for i, parcel in enumerate(parcels):
        reads[i].wait()
        for pair in range(HOT // 2):
            for q in range(lines):
                line = block + pair * lines + q
                size = min(width, capacity - q * width)
                if size < width:
                    parcel[line : line + 1, :] = jnp.zeros((1, width), F32)
                at = slice(q * width, q * width + size)
                value = (ids[i, 2 * pair : 2 * pair + 1, at] << ID_BITS) | (
                    ids[i, 2 * pair + 1 : 2 * pair + 2, at]
                )
                parcel[line : line + 1, :size] = value.astype(F32)
    for copy in copies:
        copy.wait()


def pack(look_rows, table, shards, replicas):
    rows, width = table.shape
    capacity = look_rows.shape[4]
    lines = HOT // 2 * -(-capacity // width)
    parcel = jax.ShapeDtypeStruct((rows // replicas + lines, width), F32)
    return pl.pallas_call(
        functools.partial(pack_kernel, shards),
        out_shape=[parcel] * (shards - 1),
        in_specs=[whole(pltpu.HBM)] * 2,
        out_specs=[whole()] * (shards - 1),
        scratch_shapes=[
            pltpu.VMEM((shards - 1,) + look_rows.shape[3:], jnp.int32),
            pltpu.SemaphoreType.DMA((2 * shards - 2,)),
        ],
        compiler_params=pltpu.CompilerParams(vmem_limit_bytes=PACK_LIMIT),
        name="pack",
    )(look_rows, table)


def cut_kernel(first, second, near, corner, done):
    half, lanes = near.shape[0] // 2, near.shape[1]
    mine = lax.axis_index("replica")
    copies = []
    for out, mask in ((near, 0), (corner, 3)):
        for i, factor in enumerate((first, second)):
            at = (
                pl.ds(pl.multiple_of((mine & 1) * half, 16), half),
                pl.ds(pl.multiple_of(((mine >> 1) ^ mask) * lanes, lanes), lanes),
            )
            into = out.at[i * half : (i + 1) * half, :]
            copies.append(pltpu.make_async_copy(factor.at[at], into, done.at[len(copies)]))
    for copy in copies:
        copy.start()
    for copy in copies:
        copy.wait()


def cut(factors):
    rows = factors[0].shape[0]
    return pl.pallas_call(
        cut_kernel,
        out_shape=[jax.ShapeDtypeStruct((r, 128), BF16) for r in (rows, rows)],
        in_specs=[whole(pltpu.HBM)] * 2,
        out_specs=[whole()] * 2,
        scratch_shapes=[pltpu.SemaphoreType.DMA((4,))],
        compiler_params=pltpu.CompilerParams(vmem_limit_bytes=PACK_LIMIT),
        name="cut",
    )(*factors)


def quotient(value, divisor, below):
    shift = 19
    factor = (1 << shift) // divisor + 1
    assert below * factor < 1 << 31
    assert all((v * factor) >> shift == v // divisor for v in range(below))
    return lax.shift_right_logical(value * factor, shift)


def split_rows(value):
    high = value.astype(BF16)
    return high, (value - high.astype(F32)).astype(BF16)


def ready_kernel(
    shards, live_counts, look_rows, bag_order, dense, head, places, info, words, lead
):
    batch, width = dense.shape
    capacity = look_rows.shape[4]
    bags = bag_order.shape[2]
    here = lax.axis_index("table")
    order = bag_order[0]
    sample = quotient(order, bags // batch, bags)
    dest = (order - sample * (bags // batch)) * batch + sample
    for q in range(bags // CHUNK):
        one = dest[:, q * CHUNK : q * CHUNK + CHUNK // 2]
        two = dest[:, q * CHUNK + CHUNK // 2 : (q + 1) * CHUNK]
        places[:, q * CHUNK // 2 : (q + 1) * CHUNK // 2] = one | (two << 16)
    lane = lax.broadcasted_iota(jnp.int32, info.shape, 1)
    counts = jnp.zeros(info.shape, jnp.int32)
    for s in range(shards):
        counts = jnp.where(lane == s, live_counts[0, here, s], counts)
    info[...] = counts
    words[...] = jnp.zeros_like(words)
    for pair in range(HOT // 2):
        words[pair : pair + 1, :capacity] = (
            look_rows[0, 0, here, 2 * pair : 2 * pair + 1, :] << ID_BITS
        ) | look_rows[0, 0, here, 2 * pair + 1 : 2 * pair + 2, :]
    lead[:, :width] = dense[...]
    lead[:, width:] = (dense[...].astype(F32) * head[:, :width]).astype(BF16)


def ready(live_counts, look_rows, bag_order, dense, head, shards):
    batch, width = dense.shape
    bags = bag_order.shape[2]
    padded = -(-look_rows.shape[4] // width) * width
    return pl.pallas_call(
        functools.partial(ready_kernel, shards),
        out_shape=[
            jax.ShapeDtypeStruct((1, bags // 2), jnp.int32),
            jax.ShapeDtypeStruct((1, 128), jnp.int32),
            jax.ShapeDtypeStruct((8, padded), jnp.int32),
            jax.ShapeDtypeStruct((batch, 2 * width), BF16),
        ],
        in_specs=[whole(pltpu.SMEM)] + [whole()] * 4,
        out_specs=[whole()] * 4,
        compiler_params=pltpu.CompilerParams(vmem_limit_bytes=VMEM_LIMIT),
        cost_estimate=pl.CostEstimate(flops=1000, bytes_accessed=1000, transcendentals=0),
        name="ready",
    )(live_counts, look_rows, bag_order, dense, head)


def own_kernel(replicas, table, own):
    rows, width = table.shape
    block = rows // replicas
    mine = lax.axis_index("replica")
    for m in range(replicas):
        there = pl.ds(pl.multiple_of((mine ^ m) * block, block), block)
        at = slice(m * block, (m + 1) * block)
        own[at, :width], own[at, width:] = split_rows(table[there, :])


def split_own(table, replicas):
    rows, width = table.shape
    return pl.pallas_call(
        functools.partial(own_kernel, replicas),
        out_shape=jax.ShapeDtypeStruct((rows, 2 * width), BF16),
        in_specs=[whole()],
        out_specs=whole(),
        compiler_params=pltpu.CompilerParams(vmem_limit_bytes=VMEM_LIMIT),
        cost_estimate=pl.CostEstimate(flops=1000, bytes_accessed=1000, transcendentals=0),
        name="split_own",
    )(table)


def slots_kernel(shards, replicas, bags, info, own, *refs):
    parcels, (counted, shifted, words) = refs[: shards - 1], refs[shards - 1 :]
    width = parcels[0].shape[1]
    padded = own.shape[1]
    rows = counted.shape[1]
    block = rows // replicas
    field = (1 << ID_BITS) - 1
    slot = lax.broadcasted_iota(jnp.int32, (8, bags), 1)
    ranges = [slot_range(info, shards, j) for j in range(shards)]
    shifted[...] = jnp.zeros_like(shifted)
    for j, (source, start, live) in enumerate(ranges):
        if j == 0:
            shifted[:, :padded] = own[...]
        else:
            for pair in range(HOT // 2):
                for q in range(padded // width):
                    line = block + pair * (padded // width) + q
                    shifted[pair : pair + 1, q * width : (q + 1) * width] = parcels[j - 1][
                        line : line + 1, :
                    ].astype(jnp.int32)
        moved = pltpu.roll(shifted[...], start, 1)[:, :bags]
        inside = (slot >= start) & (slot < start + live)
        words[...] = jnp.where(inside, moved, words[...] if j else 0)

    flip = lax.axis_index("replica") * block
    low = lax.broadcasted_iota(jnp.int32, (LOW, CHUNK), 0)
    for source, start, live in ranges:

        def pair(q, _, start=start, live=live, source=source):
            at = pl.ds(pl.multiple_of(q * CHUNK, CHUNK), CHUNK)
            place = q * CHUNK + lax.broadcasted_iota(jnp.int32, (1, CHUNK), 1) - start
            inside = (place >= 0) & (place < live)
            lows, highs = [], []
            for h in range(HOT):
                word = words[h // 2 : h // 2 + 1, at]
                row = (lax.shift_right_logical(word, (h % 2) * ID_BITS) & field) ^ flip
                row = jnp.where(inside, row, -1)
                highs.append(lax.shift_right_arithmetic(row, LOW.bit_length() - 1))
                lows.append((low == (row & (LOW - 1))).astype(F32).astype(BF16))
            for b in range(rows // LOW):
                count = None
                for h in range(HOT):
                    hit = (highs[h] == b).astype(F32).astype(BF16)
                    term = lows[h] * hit
                    count = term if count is None else count + term
                counted[q + source, b * LOW : (b + 1) * LOW, :] = count
            return 0

        lax.fori_loop(start // CHUNK, (start + live + CHUNK - 1) // CHUNK, pair, 0)


def slots(info, own, parcels, bags, rows, shards, replicas):
    pairs = bags // CHUNK + shards - 1
    return pl.pallas_call(
        functools.partial(slots_kernel, shards, replicas, bags),
        out_shape=jax.ShapeDtypeStruct((pairs, rows, CHUNK), BF16),
        in_specs=[whole(pltpu.SMEM)] + [whole()] * (1 + len(parcels)),
        out_specs=whole(),
        scratch_shapes=[
            pltpu.VMEM((8, bags + own.shape[1]), jnp.int32),
            pltpu.VMEM((8, bags), jnp.int32),
        ],
        compiler_params=pltpu.CompilerParams(vmem_limit_bytes=VMEM_LIMIT),
        cost_estimate=pl.CostEstimate(flops=1000, bytes_accessed=1000, transcendentals=0),
        name="slots",
    )(info, own, *parcels)


def pool_kernel(
    shards, info, places, counted, own, even, odd, lead, head, cross, scaled, table, sums, pooled
):
    width = lead.shape[1] // 2
    block = even.shape[2]
    batch = lead.shape[0]
    half = CHUNK // 2
    for m in range(2 * even.shape[0]):
        at = slice(m * block, (m + 1) * block)
        for k in range(1, shards):
            value = (odd if m % 2 else even)[m // 2, k - 1]
            table[k - 1, at, :width], table[k - 1, at, width:] = split_rows(value)
    sums[...] = jnp.zeros_like(sums)
    for j in range(shards):
        source, start, live = slot_range(info, shards, j)
        found_in = own if j == 0 else table.at[j - 1]

        def pair(q, _, found_in=found_in, source=source):
            at = pl.ds(pl.multiple_of(q * CHUNK, CHUNK), CHUNK)
            found = lax.dot_general(
                counted[q + source], found_in[...], (((0,), (0,)), ((), ())), preferred_element_type=F32
            )
            sums[at, :] += found[:, :width] + found[:, width:]
            return 0

        lax.fori_loop(start // CHUNK, (start + live + CHUNK - 1) // CHUNK, pair, 0)

    def group(i, _):
        k0 = i * UNROLL
        k0 = k0 + lax.div(k0, half) * half
        for u in range(UNROLL):
            word = places[0, i * UNROLL + u]
            pooled[pl.ds(word & 0xFFFF, 1), :] = sums[pl.ds(k0 + u, 1), :]
            pooled[pl.ds(lax.shift_right_logical(word, 16), 1), :] = sums[pl.ds(k0 + u + half, 1), :]
        return 0

    lax.fori_loop(0, sums.shape[0] // (2 * UNROLL), group, 0)
    cross[:, :width] = lead[:, :width]
    scaled[:, :width] = lead[:, width:]
    for f in range(1, cross.shape[1] // width):
        at = slice(f * width, (f + 1) * width)
        value = pooled[(f - 1) * batch : f * batch, :].astype(BF16)
        cross[:, at] = value
        scaled[:, at] = (value.astype(F32) * head[:, at]).astype(BF16)


def pool(info, places, counted, own, pieces, lead, head):
    rows, width = own.shape[0], own.shape[1] // 2
    bags = 2 * places.shape[1]
    shards = pieces[0].shape[1] + 1
    smem = whole(pltpu.SMEM)
    return pl.pallas_call(
        functools.partial(pool_kernel, shards),
        out_shape=[jax.ShapeDtypeStruct((lead.shape[0], head.shape[1]), BF16)] * 2,
        in_specs=[smem, smem] + [whole()] * 6,
        out_specs=[whole()] * 2,
        scratch_shapes=[
            pltpu.VMEM((shards - 1, rows, 2 * width), BF16),
            pltpu.VMEM((bags, width), F32),
            pltpu.VMEM((bags, width), F32),
        ],
        compiler_params=pltpu.CompilerParams(vmem_limit_bytes=VMEM_LIMIT),
        cost_estimate=pl.CostEstimate(flops=1000, bytes_accessed=1000, transcendentals=0),
        name="pool",
    )(info, places, counted, own, *pieces, lead, head)


def column_of(row, size):
    eye = lax.broadcasted_iota(jnp.int32, (size, size), 0) == lax.broadcasted_iota(
        jnp.int32, (size, size), 1
    )
    return jnp.sum(jnp.where(eye, jnp.broadcast_to(row, (size, size)), 0.0), axis=1, keepdims=True)


def row_of(column, size):
    eye = lax.broadcasted_iota(jnp.int32, (size, size), 0) == lax.broadcasted_iota(
        jnp.int32, (size, size), 1
    )
    return jnp.sum(
        jnp.where(eye, jnp.broadcast_to(column, (size, size)), 0.0), axis=0, keepdims=True
    )


def first_kernel(copies, cross, scaled, bias, head, *refs):
    weights, (grads, logit, full_in, full_out) = refs[: len(copies)], refs[len(copies) :]
    for ref, copy in zip(weights, copies):
        copy(ref, (full_in, full_out))
    add_rank(cross, scaled, head, full_in, full_out, bias, None, grads, logit)


def add_rank(cross, scaled, head, full_in, full_out, bias, before, grads, logit):
    batch, features = cross.shape
    width = logit.shape[1]
    across = (((1,), (1,)), ((), ()))
    hidden = jnp.dot(cross[...], full_in[...], preferred_element_type=F32).astype(BF16)
    back = jnp.dot(scaled[...], full_out[...], preferred_element_type=F32).astype(BF16)
    step = 3 * width if (features // width) % 3 == 0 else width
    total = jnp.zeros((batch, width), F32) if before is None else before[1][...]
    for n in range(features // step):
        at = slice(n * step, (n + 1) * step)
        mixed = lax.dot_general(hidden, full_out[at, :], across, preferred_element_type=F32)
        if bias is not None:
            mixed = mixed + bias[:, at] + 1.0
        gain = head[:, at] * mixed
        term = cross[:, at].astype(F32) * gain
        grad = gain + lax.dot_general(back, full_in[at, :], across, preferred_element_type=F32)
        for p in range(step // width):
            part = slice(p * width, (p + 1) * width)
            total = total + term[:, part]
            f = n * (step // width) + p
            if f > 0:
                rows = slice((f - 1) * batch, f * batch)
                grads[rows, :] = grad[:, part] + (0.0 if before is None else before[0][rows, :])
    logit[...] = total


def first_step(cross, scaled, bias, head, weights, copies, rank):
    batch, features = cross.shape
    width = 128
    return pl.pallas_call(
        functools.partial(first_kernel, copies),
        out_shape=(
            jax.ShapeDtypeStruct((features // width * batch - batch, width), F32),
            jax.ShapeDtypeStruct((batch, width), F32),
        ),
        in_specs=[whole()] * (4 + len(weights)),
        out_specs=(whole(), whole()),
        scratch_shapes=[pltpu.VMEM((features, rank), BF16)] * 2,
        compiler_params=pltpu.CompilerParams(vmem_limit_bytes=VMEM_LIMIT),
        cost_estimate=pl.CostEstimate(
            flops=2 * 10**9, bytes_accessed=20 * 10**6, transcendentals=0
        ),
        name="first",
    )(cross, scaled, bias, head, *weights)


def dense_kernel(shards, replicas, copies, info, places, cross, scaled, head, labels, counted, *refs):
    begun, partial = refs[:2]
    weights = refs[2 : 2 + len(copies)]
    logits, even, odd, full_in, full_out, grads, logit, slots, narrow, total, spots, done = refs[
        2 + len(copies) :
    ]
    batch = cross.shape[0]
    width = slots.shape[1]
    bags = grads.shape[0]
    rows = total.shape[2]
    here = lax.axis_index("table")
    fetch = pltpu.make_async_copy(places, spots, done)
    fetch.start()

    if copies:
        for ref, copy in zip(weights, copies):
            copy(ref, (full_in, full_out))
        add_rank(cross, scaled, head, full_in, full_out, None, (begun, partial), grads, logit)
    else:
        grads[...] = begun[...]
        logit[...] = partial[...]
    sums = jnp.sum(logit[...], axis=1, keepdims=True)
    logits[...] = row_of(sums, batch)
    lean = jax.nn.sigmoid(sums) - column_of(labels[...].astype(F32), batch)
    for f in range(bags // batch):
        at = slice(f * batch, (f + 1) * batch)
        grads[at, :] = (grads[at, :] * lean).astype(BF16).astype(F32)

    half = CHUNK // 2
    chunks = bags // CHUNK

    def gather(q):
        for i in range(half):
            word = spots[0, q * half + i]
            slots[i : i + 1, :] = grads[pl.ds(word & 0xFFFF, 1), :]
            slots[i + half : i + half + 1, :] = grads[pl.ds(lax.shift_right_logical(word, 16), 1), :]

    def shard_of(k):
        end, shard = jnp.int32(0), jnp.int32(0)
        for s in range(shards - 1):
            end = end + info[0, s]
            shard = shard + jnp.where(k >= end, 1, 0)
        return shard

    def add(q, shard):
        place = here ^ shard
        found = lax.dot_general(
            narrow[...], counted[q + shard], (((0,), (1,)), ((), ())), preferred_element_type=F32
        )
        start = slot_range(info, shards, place)[1]
        total[place] = found + jnp.where(start < q * CHUNK, total[place], 0.0)

    fetch.wait()
    gather(0)

    def chunk(q, _):
        narrow[...] = slots[...].astype(BF16)
        shard = shard_of(q * CHUNK)
        add(q, shard)
        gather(jnp.minimum(q + 1, chunks - 1))

        def more(s, _):
            add(q, s)
            return 0

        lax.fori_loop(shard + 1, shard_of((q + 1) * CHUNK - 1) + 1, more, 0)
        return 0

    lax.fori_loop(0, chunks, chunk, 0)
    block = rows // replicas
    for j in range(shards):
        for m in range(replicas):
            sums = total[j, :, m * block : (m + 1) * block].T
            (odd if m % 2 else even)[m // 2, j] = sums.astype(BF16)


def dense_step(
    info, places, cross, scaled, head, labels, counted, begun, weights, copies, shards, replicas
):
    batch, features = cross.shape
    width = 128
    bags = begun[0].shape[0]
    rows = counted.shape[1]
    half = jax.ShapeDtypeStruct((replicas // 2, shards, rows // replicas, width), BF16)
    smem = whole(pltpu.SMEM)
    part = pltpu.VMEM((features, width) if copies else (16, width), BF16)
    return pl.pallas_call(
        functools.partial(dense_kernel, shards, replicas, copies),
        out_shape=(jax.ShapeDtypeStruct((1, batch), F32), half, half),
        in_specs=[smem] + [whole()] * (8 + len(weights)),
        out_specs=(whole(), whole(), whole()),
        scratch_shapes=[
            part,
            part,
            pltpu.VMEM((bags, width), F32),
            pltpu.VMEM((batch, width), F32),
            pltpu.VMEM((CHUNK, width), F32),
            pltpu.VMEM((CHUNK, width), BF16),
            pltpu.VMEM((shards, width, rows), F32),
            pltpu.SMEM(places.shape, jnp.int32),
            pltpu.SemaphoreType.DMA(()),
        ],
        compiler_params=pltpu.CompilerParams(vmem_limit_bytes=VMEM_LIMIT),
        cost_estimate=pl.CostEstimate(
            flops=2 * 10**9, bytes_accessed=20 * 10**6, transcendentals=0
        ),
        name="dense",
    )(info, places, cross, scaled, head, labels, counted, *begun, *weights)


def splits_evenly(factor, replicas):
    return replicas == 8 and factor.shape[1] == 4 * 128 and factor.shape[0] % 32 == 0


def gather_whole(factors):
    def spot(which):
        def copy(ref, full):
            full[which][...] = ref[...]

        return copy

    return [
        (lax.all_gather(w, "table", axis=0, tiled=True), spot(i)) for i, w in enumerate(factors)
    ]


def gather_blocks(factors, near, corner, after):
    shards = lax.axis_size("table")
    shard_rows = factors[0].shape[0]
    half, lanes = shard_rows // 2, near.shape[2]
    first, second = swap(near, 2), swap(near, 4)
    first, second, corner, after = lax.optimization_barrier((first, second, corner, after))
    corners = [(swap(first[1:, :half], 4), 0), (swap(second[1:, half:], 2), 1)]
    every = tuple(range(1, shards))

    def put(masks, block, core, column, begin, end):
        def copy(ref, full):
            own, here = lax.axis_index("replica"), lax.axis_index("table")
            for i, mask in enumerate(masks):
                start = (here ^ mask) * shard_rows + ((own & 1) ^ core) * half
                at = pl.ds(pl.multiple_of(start, 16), half)
                for which in range(begin, end):
                    full[which][at, column * lanes : (column + 1) * lanes] = ref[
                        i, (which - begin) * half : (which - begin + 1) * half, :
                    ]

        return block, copy

    def put_own(which, masks):
        def copy(ref, full):
            own, here = lax.axis_index("replica"), lax.axis_index("table")
            at = pl.ds(pl.multiple_of(here * shard_rows, 16), shard_rows)
            for column, mask in enumerate(masks):
                columns = pl.ds(pl.multiple_of(((own >> 1) ^ mask) * lanes, lanes), lanes)
                full[which][at, column * lanes : (column + 1) * lanes] = ref[:, columns]

        return factors[which], copy

    early = [put_own(which, (0, 1, 2)) for which in range(2)]
    for column, block in enumerate((near, first, second)):
        early += [put(every, block, 0, column, 0, 2), put(every, swap(block, 1), 1, column, 0, 2)]

    def late(after):
        blocks, after = lax.optimization_barrier(([c[0] for c in corners], after))
        out = [put_own(which, (3,)) for which in range(2)]
        out += [put((1,), corner, 0, 0, 0, 2), put((1,), swap(corner, 1), 1, 0, 0, 2)]
        for block, (_, which) in zip(blocks, corners):
            out.append(put(every[1:], block, 0, 0, which, which + 1))
            out.append(put(every[1:], swap(block, 1), 1, 0, which, which + 1))
        return out, after

    return early, late, after


def reduce_rows(even, odd):
    shards, replicas = lax.axis_size("table"), lax.axis_size("replica")
    kept = even.astype(F32) + swap(odd, 1).astype(F32)
    for masks in mask_stages(replicas)[1:]:
        split = kept.reshape((-1, len(masks) + 1) + kept.shape[1:])
        kept = split[:, 0]
        for i, mask in enumerate(masks):
            kept = kept + swap(split[:, i + 1].astype(BF16), mask).astype(F32)
    kept = kept[0]
    total = kept[0]
    for k in range(1, shards):
        total = total + cross_over(kept[k].astype(BF16), k).astype(F32)
    return total


def finish_kernel(accum, even, odd, update, fresh):
    count, block, width = even.shape
    mine = lax.axis_index("replica")
    for m in range(2 * count):
        own = mine ^ m
        grad = (odd if m % 2 else even)[m // 2]
        square = jnp.sum(grad * grad, axis=1, keepdims=True) * (1.0 / width)
        row = accum[pl.ds(own, 1), :] + row_of(square, block)
        fresh[pl.ds(own, 1), :] = row
        rows = pl.ds(pl.multiple_of(own * block, block), block)
        update[rows, :] = -grad / (jnp.sqrt(column_of(row, block)) + EPSILON)


def finish(accum, even, odd):
    replicas, block = accum.shape
    width = even.shape[2]
    return pl.pallas_call(
        finish_kernel,
        out_shape=(
            jax.ShapeDtypeStruct((replicas * block, width), F32),
            jax.ShapeDtypeStruct((replicas, block), F32),
        ),
        in_specs=[whole()] * 3,
        out_specs=(whole(), whole()),
        compiler_params=pltpu.CompilerParams(vmem_limit_bytes=VMEM_LIMIT),
        name="finish",
    )(accum, even, odd)


def local(
    emb_table,
    row_accum,
    look_rows,
    live_counts,
    bag_order,
    dense_emb,
    labels,
    cross_in,
    cross_out,
    cross_bias,
    head_weight,
):
    shards, replicas = lax.axis_size("table"), lax.axis_size("replica")
    rows = emb_table.shape[0]
    block = rows // replicas
    batch = dense_emb.shape[0]
    factors = (cross_in, cross_out)
    even_split = splits_evenly(cross_in, replicas)

    packed = pack(look_rows, emb_table, shards, replicas)
    parcels = [cross_over(p, k + 1) for k, p in enumerate(packed)]
    bias, head, label_row = (x.reshape(1, -1) for x in (cross_bias, head_weight, labels))
    prepared = ready(live_counts, look_rows, bag_order, dense_emb, head, shards)
    parcels, prepared, blocks = lax.optimization_barrier(
        (parcels, prepared, cut(factors) if even_split else [])
    )
    places, info, own_words, lead = prepared
    far, corner = [], []
    if even_split:
        far = jnp.stack([cross_over(blocks[0], k) for k in range(1, shards)])
        corner = cross_over(blocks[1], 1)[None]
    counted = slots(info, own_words, parcels, bag_order.shape[2], rows, shards, replicas)
    pieces, far, counted, own_rows = replica_gather(
        jnp.stack([p[:block] for p in parcels]), far, counted, split_own(emb_table, replicas)
    )
    crossed = pool(info, places, counted, own_rows, pieces, lead, head)
    rank = cross_in.shape[1]
    if even_split:
        early, late, crossed = gather_blocks(factors, far, corner, crossed)
        rank = rank - 128
    else:
        early, late = gather_whole(factors), None
    begun = first_step(*crossed, bias, head, *zip(*early), rank)
    last = []
    if late:
        last, begun = late(begun)
    logits, even, odd = dense_step(
        info,
        places,
        *crossed,
        head,
        label_row,
        counted,
        begun,
        [block for block, _ in last],
        [copy for _, copy in last],
        shards,
        replicas,
    )
    grad = reduce_rows(even, odd)
    update, accum = finish(row_accum.reshape(replicas, block), *replica_gather(grad)[0])
    return (logits.reshape(-1), update, accum.reshape(-1))


def solution(mesh):
    placed = (
        P("table", None),
        P("table"),
        P("replica", "table", None, None, None),
        P("replica", None, None),
        P("replica", "table", None),
        P(("replica", "table"), None),
        P(("replica", "table")),
        P("table", None),
        P("table", None),
        P(),
        P(),
    )
    return jax.shard_map(
        local,
        mesh=mesh,
        in_specs=placed,
        out_specs=(P(("replica", "table")), P("table", None), P("table")),
        check_vma=False,
    )
```

```python
import functools

import jax
import jax.numpy as jnp
from jax import lax
from jax.experimental import pallas as pl
from jax.experimental.pallas import tpu as pltpu
from jax.sharding import PartitionSpec as P

EPSILON = 1e-08
F32, BF16 = jnp.float32, jnp.bfloat16
LOW = 32
UNROLL = 8
HOT = 4
CHUNK = 256
ID_BITS = 10
VMEM_LIMIT = 28 * 1024 * 1024
PACK_LIMIT = 60 * 1024 * 1024


def swap(array, mask):
    size = lax.axis_size("replica")
    return lax.ppermute(array, "replica", [(i, i ^ mask) for i in range(size)])


def cross_over(array, mask):
    size = lax.axis_size("table")
    return lax.ppermute(array, "table", [(i, i ^ mask) for i in range(size)])


def mask_stages(size):
    stages, bit = [(1,)], 1
    while (1 << bit) < size:
        if (2 << bit) < size:
            stages.append((1 << bit, 2 << bit, 3 << bit))
            bit += 2
        else:
            stages.append((1 << bit,))
            bit += 1
    return stages


def replica_gather(piece, *beside, after=None):
    held = [piece]
    for masks in reversed(mask_stages(lax.axis_size("replica"))[1:]):
        last = held
        if after is not None:
            last, after = lax.optimization_barrier((held, after))
        sent = [[swap(h, mask) for h in (held if mask != masks[-1] else last)] for mask in masks]
        held = [h for group in [held] + sent for h in group]
    held, *beside = lax.optimization_barrier((held, *beside))
    order = sorted(range(len(held)), key=lambda i: gather_masks(lax.axis_size("replica"))[i])
    even = jnp.stack([held[i] for i in order])
    return (even, swap(even, 1)), *beside


def gather_masks(size):
    masks = [0]
    for group in reversed(mask_stages(size)[1:]):
        masks = masks + [m ^ mask for mask in group for m in masks]
    return masks


def whole(space=pltpu.VMEM):
    return pl.BlockSpec(memory_space=space)


def slot_range(info, shards, j):
    source = lax.axis_index("table") ^ j
    start = jnp.int32(0)
    for s in range(shards):
        start = start + jnp.where(s < source, info[0, s], 0)
    return source, start, info[0, source]


def pack_kernel(shards, look_rows, table, *refs):
    parcels, (ids, done) = refs[:-2], refs[-2:]
    width = table.shape[1]
    capacity = look_rows.shape[4]
    lines = -(-capacity // width)
    block = parcels[0].shape[0] - HOT // 2 * lines
    mine, here = lax.axis_index("replica"), lax.axis_index("table")
    rows = table.at[pl.ds(pl.multiple_of(mine * block, block), block), :]
    copies = [
        pltpu.make_async_copy(rows, parcel.at[:block, :], done.at[i])
        for i, parcel in enumerate(parcels)
    ]
    reads = [
        pltpu.make_async_copy(look_rows.at[0, 0, here ^ (i + 1)], ids.at[i], done.at[shards - 1 + i])
        for i in range(shards - 1)
    ]
    for copy in reads + copies:
        copy.start()
    for i, parcel in enumerate(parcels):
        reads[i].wait()
        for pair in range(HOT // 2):
            for q in range(lines):
                line = block + pair * lines + q
                size = min(width, capacity - q * width)
                if size < width:
                    parcel[line : line + 1, :] = jnp.zeros((1, width), F32)
                at = slice(q * width, q * width + size)
                value = (ids[i, 2 * pair : 2 * pair + 1, at] << ID_BITS) | (
                    ids[i, 2 * pair + 1 : 2 * pair + 2, at]
                )
                parcel[line : line + 1, :size] = value.astype(F32)
    for copy in copies:
        copy.wait()


def pack(look_rows, table, shards, replicas):
    rows, width = table.shape
    capacity = look_rows.shape[4]
    lines = HOT // 2 * -(-capacity // width)
    parcel = jax.ShapeDtypeStruct((rows // replicas + lines, width), F32)
    return pl.pallas_call(
        functools.partial(pack_kernel, shards),
        out_shape=[parcel] * (shards - 1),
        in_specs=[whole(pltpu.HBM)] * 2,
        out_specs=[whole()] * (shards - 1),
        scratch_shapes=[
            pltpu.VMEM((shards - 1,) + look_rows.shape[3:], jnp.int32),
            pltpu.SemaphoreType.DMA((2 * shards - 2,)),
        ],
        compiler_params=pltpu.CompilerParams(vmem_limit_bytes=PACK_LIMIT),
        name="pack",
    )(look_rows, table)


def cut_kernel(first, second, near, corner, done):
    half, lanes = near.shape[0] // 2, near.shape[1]
    mine = lax.axis_index("replica")
    copies = []
    for out, mask in ((near, 0), (corner, 3)):
        for i, factor in enumerate((first, second)):
            at = (
                pl.ds(pl.multiple_of((mine & 1) * half, 16), half),
                pl.ds(pl.multiple_of(((mine >> 1) ^ mask) * lanes, lanes), lanes),
            )
            into = out.at[i * half : (i + 1) * half, :]
            copies.append(pltpu.make_async_copy(factor.at[at], into, done.at[len(copies)]))
    for copy in copies:
        copy.start()
    for copy in copies:
        copy.wait()


def cut(factors):
    rows = factors[0].shape[0]
    return pl.pallas_call(
        cut_kernel,
        out_shape=[jax.ShapeDtypeStruct((r, 128), BF16) for r in (rows, rows)],
        in_specs=[whole(pltpu.HBM)] * 2,
        out_specs=[whole()] * 2,
        scratch_shapes=[pltpu.SemaphoreType.DMA((4,))],
        compiler_params=pltpu.CompilerParams(vmem_limit_bytes=PACK_LIMIT),
        name="cut",
    )(*factors)


def quotient(value, divisor, below):
    shift = 19
    factor = (1 << shift) // divisor + 1
    assert below * factor < 1 << 31
    assert all((v * factor) >> shift == v // divisor for v in range(below))
    return lax.shift_right_logical(value * factor, shift)


def split_rows(value):
    high = value.astype(BF16)
    return high, (value - high.astype(F32)).astype(BF16)


def ready_kernel(
    shards, live_counts, look_rows, bag_order, dense, head, places, info, words, lead
):
    batch, width = dense.shape
    capacity = look_rows.shape[4]
    bags = bag_order.shape[2]
    here = lax.axis_index("table")
    order = bag_order[0]
    sample = quotient(order, bags // batch, bags)
    dest = (order - sample * (bags // batch)) * batch + sample
    for q in range(bags // CHUNK):
        one = dest[:, q * CHUNK : q * CHUNK + CHUNK // 2]
        two = dest[:, q * CHUNK + CHUNK // 2 : (q + 1) * CHUNK]
        places[:, q * CHUNK // 2 : (q + 1) * CHUNK // 2] = one | (two << 16)
    lane = lax.broadcasted_iota(jnp.int32, info.shape, 1)
    counts = jnp.zeros(info.shape, jnp.int32)
    for s in range(shards):
        counts = jnp.where(lane == s, live_counts[0, here, s], counts)
    info[...] = counts
    words[...] = jnp.zeros_like(words)
    for pair in range(HOT // 2):
        words[pair : pair + 1, :capacity] = (
            look_rows[0, 0, here, 2 * pair : 2 * pair + 1, :] << ID_BITS
        ) | look_rows[0, 0, here, 2 * pair + 1 : 2 * pair + 2, :]
    lead[:, :width] = dense[...]
    lead[:, width:] = (dense[...].astype(F32) * head[:, :width]).astype(BF16)


def ready(live_counts, look_rows, bag_order, dense, head, shards):
    batch, width = dense.shape
    bags = bag_order.shape[2]
    padded = -(-look_rows.shape[4] // width) * width
    return pl.pallas_call(
        functools.partial(ready_kernel, shards),
        out_shape=[
            jax.ShapeDtypeStruct((1, bags // 2), jnp.int32),
            jax.ShapeDtypeStruct((1, 128), jnp.int32),
            jax.ShapeDtypeStruct((8, padded), jnp.int32),
            jax.ShapeDtypeStruct((batch, 2 * width), BF16),
        ],
        in_specs=[whole(pltpu.SMEM)] + [whole()] * 4,
        out_specs=[whole()] * 4,
        compiler_params=pltpu.CompilerParams(vmem_limit_bytes=VMEM_LIMIT),
        cost_estimate=pl.CostEstimate(flops=1000, bytes_accessed=1000, transcendentals=0),
        name="ready",
    )(live_counts, look_rows, bag_order, dense, head)


def own_kernel(replicas, table, own):
    rows, width = table.shape
    block = rows // replicas
    mine = lax.axis_index("replica")
    for m in range(replicas):
        there = pl.ds(pl.multiple_of((mine ^ m) * block, block), block)
        at = slice(m * block, (m + 1) * block)
        own[at, :width], own[at, width:] = split_rows(table[there, :])


def split_own(table, replicas):
    rows, width = table.shape
    return pl.pallas_call(
        functools.partial(own_kernel, replicas),
        out_shape=jax.ShapeDtypeStruct((rows, 2 * width), BF16),
        in_specs=[whole()],
        out_specs=whole(),
        compiler_params=pltpu.CompilerParams(vmem_limit_bytes=VMEM_LIMIT),
        cost_estimate=pl.CostEstimate(flops=1000, bytes_accessed=1000, transcendentals=0),
        name="split_own",
    )(table)


def slots_kernel(shards, replicas, bags, info, own, *refs):
    parcels, (counted, shifted, words) = refs[: shards - 1], refs[shards - 1 :]
    width = parcels[0].shape[1]
    padded = own.shape[1]
    rows = counted.shape[1]
    block = rows // replicas
    field = (1 << ID_BITS) - 1
    slot = lax.broadcasted_iota(jnp.int32, (8, bags), 1)
    ranges = [slot_range(info, shards, j) for j in range(shards)]
    shifted[...] = jnp.zeros_like(shifted)
    for j, (source, start, live) in enumerate(ranges):
        if j == 0:
            shifted[:, :padded] = own[...]
        else:
            for pair in range(HOT // 2):
                for q in range(padded // width):
                    line = block + pair * (padded // width) + q
                    shifted[pair : pair + 1, q * width : (q + 1) * width] = parcels[j - 1][
                        line : line + 1, :
                    ].astype(jnp.int32)
        moved = pltpu.roll(shifted[...], start, 1)[:, :bags]
        inside = (slot >= start) & (slot < start + live)
        words[...] = jnp.where(inside, moved, words[...] if j else 0)

    flip = lax.axis_index("replica") * block
    low = lax.broadcasted_iota(jnp.int32, (LOW, CHUNK), 0)
    for source, start, live in ranges:

        def pair(q, _, start=start, live=live, source=source):
            at = pl.ds(pl.multiple_of(q * CHUNK, CHUNK), CHUNK)
            place = q * CHUNK + lax.broadcasted_iota(jnp.int32, (1, CHUNK), 1) - start
            inside = (place >= 0) & (place < live)
            lows, highs = [], []
            for h in range(HOT):
                word = words[h // 2 : h // 2 + 1, at]
                row = (lax.shift_right_logical(word, (h % 2) * ID_BITS) & field) ^ flip
                row = jnp.where(inside, row, -1)
                highs.append(lax.shift_right_arithmetic(row, LOW.bit_length() - 1))
                lows.append((low == (row & (LOW - 1))).astype(F32).astype(BF16))
            for b in range(rows // LOW):
                count = None
                for h in range(HOT):
                    hit = (highs[h] == b).astype(F32).astype(BF16)
                    term = lows[h] * hit
                    count = term if count is None else count + term
                counted[q + source, b * LOW : (b + 1) * LOW, :] = count
            return 0

        lax.fori_loop(start // CHUNK, (start + live + CHUNK - 1) // CHUNK, pair, 0)


def slots(info, own, parcels, bags, rows, shards, replicas):
    pairs = bags // CHUNK + shards - 1
    return pl.pallas_call(
        functools.partial(slots_kernel, shards, replicas, bags),
        out_shape=jax.ShapeDtypeStruct((pairs, rows, CHUNK), BF16),
        in_specs=[whole(pltpu.SMEM)] + [whole()] * (1 + len(parcels)),
        out_specs=whole(),
        scratch_shapes=[
            pltpu.VMEM((8, bags + own.shape[1]), jnp.int32),
            pltpu.VMEM((8, bags), jnp.int32),
        ],
        compiler_params=pltpu.CompilerParams(vmem_limit_bytes=VMEM_LIMIT),
        cost_estimate=pl.CostEstimate(flops=1000, bytes_accessed=1000, transcendentals=0),
        name="slots",
    )(info, own, *parcels)


def pool_kernel(
    shards, info, places, counted, own, even, odd, lead, head, cross, scaled, table, sums, pooled
):
    width = lead.shape[1] // 2
    block = even.shape[2]
    batch = lead.shape[0]
    half = CHUNK // 2
    for m in range(2 * even.shape[0]):
        at = slice(m * block, (m + 1) * block)
        for k in range(1, shards):
            value = (odd if m % 2 else even)[m // 2, k - 1]
            table[k - 1, at, :width], table[k - 1, at, width:] = split_rows(value)
    sums[...] = jnp.zeros_like(sums)
    for j in range(shards):
        source, start, live = slot_range(info, shards, j)
        found_in = own if j == 0 else table.at[j - 1]

        def pair(q, _, found_in=found_in, source=source):
            at = pl.ds(pl.multiple_of(q * CHUNK, CHUNK), CHUNK)
            found = lax.dot_general(
                counted[q + source], found_in[...], (((0,), (0,)), ((), ())), preferred_element_type=F32
            )
            sums[at, :] += found[:, :width] + found[:, width:]
            return 0

        lax.fori_loop(start // CHUNK, (start + live + CHUNK - 1) // CHUNK, pair, 0)

    def group(i, _):
        k0 = i * UNROLL
        k0 = k0 + lax.div(k0, half) * half
        for u in range(UNROLL):
            word = places[0, i * UNROLL + u]
            pooled[pl.ds(word & 0xFFFF, 1), :] = sums[pl.ds(k0 + u, 1), :]
            pooled[pl.ds(lax.shift_right_logical(word, 16), 1), :] = sums[pl.ds(k0 + u + half, 1), :]
        return 0

    lax.fori_loop(0, sums.shape[0] // (2 * UNROLL), group, 0)
    cross[:, :width] = lead[:, :width]
    scaled[:, :width] = lead[:, width:]
    for f in range(1, cross.shape[1] // width):
        at = slice(f * width, (f + 1) * width)
        value = pooled[(f - 1) * batch : f * batch, :].astype(BF16)
        cross[:, at] = value
        scaled[:, at] = (value.astype(F32) * head[:, at]).astype(BF16)


def pool(info, places, counted, own, pieces, lead, head):
    rows, width = own.shape[0], own.shape[1] // 2
    bags = 2 * places.shape[1]
    shards = pieces[0].shape[1] + 1
    smem = whole(pltpu.SMEM)
    return pl.pallas_call(
        functools.partial(pool_kernel, shards),
        out_shape=[jax.ShapeDtypeStruct((lead.shape[0], head.shape[1]), BF16)] * 2,
        in_specs=[smem, smem] + [whole()] * 6,
        out_specs=[whole()] * 2,
        scratch_shapes=[
            pltpu.VMEM((shards - 1, rows, 2 * width), BF16),
            pltpu.VMEM((bags, width), F32),
            pltpu.VMEM((bags, width), F32),
        ],
        compiler_params=pltpu.CompilerParams(vmem_limit_bytes=VMEM_LIMIT),
        cost_estimate=pl.CostEstimate(flops=1000, bytes_accessed=1000, transcendentals=0),
        name="pool",
    )(info, places, counted, own, *pieces, lead, head)


def column_of(row, size):
    eye = lax.broadcasted_iota(jnp.int32, (size, size), 0) == lax.broadcasted_iota(
        jnp.int32, (size, size), 1
    )
    return jnp.sum(jnp.where(eye, jnp.broadcast_to(row, (size, size)), 0.0), axis=1, keepdims=True)


def row_of(column, size):
    eye = lax.broadcasted_iota(jnp.int32, (size, size), 0) == lax.broadcasted_iota(
        jnp.int32, (size, size), 1
    )
    return jnp.sum(
        jnp.where(eye, jnp.broadcast_to(column, (size, size)), 0.0), axis=0, keepdims=True
    )


def first_kernel(copies, cross, scaled, bias, head, *refs):
    weights, (grads, logit, full_in, full_out) = refs[: len(copies)], refs[len(copies) :]
    for ref, copy in zip(weights, copies):
        copy(ref, (full_in, full_out))
    add_rank(cross, scaled, head, full_in, full_out, bias, None, grads, logit)


def add_rank(cross, scaled, head, full_in, full_out, bias, before, grads, logit):
    batch, features = cross.shape
    width = logit.shape[1]
    across = (((1,), (1,)), ((), ()))
    hidden = jnp.dot(cross[...], full_in[...], preferred_element_type=F32).astype(BF16)
    back = jnp.dot(scaled[...], full_out[...], preferred_element_type=F32).astype(BF16)
    step = 3 * width if (features // width) % 3 == 0 else width
    total = jnp.zeros((batch, width), F32) if before is None else before[1][...]
    for n in range(features // step):
        at = slice(n * step, (n + 1) * step)
        mixed = lax.dot_general(hidden, full_out[at, :], across, preferred_element_type=F32)
        if bias is not None:
            mixed = mixed + bias[:, at] + 1.0
        gain = head[:, at] * mixed
        term = cross[:, at].astype(F32) * gain
        grad = gain + lax.dot_general(back, full_in[at, :], across, preferred_element_type=F32)
        for p in range(step // width):
            part = slice(p * width, (p + 1) * width)
            total = total + term[:, part]
            f = n * (step // width) + p
            if f > 0:
                rows = slice((f - 1) * batch, f * batch)
                grads[rows, :] = grad[:, part] + (0.0 if before is None else before[0][rows, :])
    logit[...] = total


def first_step(cross, scaled, bias, head, weights, copies, rank):
    batch, features = cross.shape
    width = 128
    return pl.pallas_call(
        functools.partial(first_kernel, copies),
        out_shape=(
            jax.ShapeDtypeStruct((features // width * batch - batch, width), F32),
            jax.ShapeDtypeStruct((batch, width), F32),
        ),
        in_specs=[whole()] * (4 + len(weights)),
        out_specs=(whole(), whole()),
        scratch_shapes=[pltpu.VMEM((features, rank), BF16)] * 2,
        compiler_params=pltpu.CompilerParams(vmem_limit_bytes=VMEM_LIMIT),
        cost_estimate=pl.CostEstimate(
            flops=2 * 10**9, bytes_accessed=20 * 10**6, transcendentals=0
        ),
        name="first",
    )(cross, scaled, bias, head, *weights)


def dense_kernel(shards, replicas, copies, info, places, cross, scaled, head, labels, counted, *refs):
    begun, partial = refs[:2]
    weights = refs[2 : 2 + len(copies)]
    logits, even, odd, full_in, full_out, grads, logit, slots, narrow, total, spots, done = refs[
        2 + len(copies) :
    ]
    batch = cross.shape[0]
    width = slots.shape[1]
    bags = grads.shape[0]
    rows = total.shape[2]
    here = lax.axis_index("table")
    fetch = pltpu.make_async_copy(places, spots, done)
    fetch.start()

    if copies:
        for ref, copy in zip(weights, copies):
            copy(ref, (full_in, full_out))
        add_rank(cross, scaled, head, full_in, full_out, None, (begun, partial), grads, logit)
    else:
        grads[...] = begun[...]
        logit[...] = partial[...]
    sums = jnp.sum(logit[...], axis=1, keepdims=True)
    logits[...] = row_of(sums, batch)
    lean = jax.nn.sigmoid(sums) - column_of(labels[...].astype(F32), batch)
    for f in range(bags // batch):
        at = slice(f * batch, (f + 1) * batch)
        grads[at, :] = (grads[at, :] * lean).astype(BF16).astype(F32)

    half = CHUNK // 2
    chunks = bags // CHUNK

    def gather(q):
        for i in range(half):
            word = spots[0, q * half + i]
            slots[i : i + 1, :] = grads[pl.ds(word & 0xFFFF, 1), :]
            slots[i + half : i + half + 1, :] = grads[pl.ds(lax.shift_right_logical(word, 16), 1), :]

    def shard_of(k):
        end, shard = jnp.int32(0), jnp.int32(0)
        for s in range(shards - 1):
            end = end + info[0, s]
            shard = shard + jnp.where(k >= end, 1, 0)
        return shard

    def add(q, shard):
        place = here ^ shard
        found = lax.dot_general(
            narrow[...], counted[q + shard], (((0,), (1,)), ((), ())), preferred_element_type=F32
        )
        start = slot_range(info, shards, place)[1]
        total[place] = found + jnp.where(start < q * CHUNK, total[place], 0.0)

    fetch.wait()
    gather(0)

    def chunk(q, _):
        narrow[...] = slots[...].astype(BF16)
        shard = shard_of(q * CHUNK)
        add(q, shard)
        gather(jnp.minimum(q + 1, chunks - 1))

        def more(s, _):
            add(q, s)
            return 0

        lax.fori_loop(shard + 1, shard_of((q + 1) * CHUNK - 1) + 1, more, 0)
        return 0

    lax.fori_loop(0, chunks, chunk, 0)
    block = rows // replicas
    for j in range(shards):
        for m in range(replicas):
            sums = total[j, :, m * block : (m + 1) * block].T
            (odd if m % 2 else even)[m // 2, j] = sums.astype(BF16)


def dense_step(
    info, places, cross, scaled, head, labels, counted, begun, weights, copies, shards, replicas
):
    batch, features = cross.shape
    width = 128
    bags = begun[0].shape[0]
    rows = counted.shape[1]
    half = jax.ShapeDtypeStruct((replicas // 2, shards, rows // replicas, width), BF16)
    smem = whole(pltpu.SMEM)
    part = pltpu.VMEM((features, width) if copies else (16, width), BF16)
    return pl.pallas_call(
        functools.partial(dense_kernel, shards, replicas, copies),
        out_shape=(jax.ShapeDtypeStruct((1, batch), F32), half, half),
        in_specs=[smem] + [whole()] * (8 + len(weights)),
        out_specs=(whole(), whole(), whole()),
        scratch_shapes=[
            part,
            part,
            pltpu.VMEM((bags, width), F32),
            pltpu.VMEM((batch, width), F32),
            pltpu.VMEM((CHUNK, width), F32),
            pltpu.VMEM((CHUNK, width), BF16),
            pltpu.VMEM((shards, width, rows), F32),
            pltpu.SMEM(places.shape, jnp.int32),
            pltpu.SemaphoreType.DMA(()),
        ],
        compiler_params=pltpu.CompilerParams(vmem_limit_bytes=VMEM_LIMIT),
        cost_estimate=pl.CostEstimate(
            flops=2 * 10**9, bytes_accessed=20 * 10**6, transcendentals=0
        ),
        name="dense",
    )(info, places, cross, scaled, head, labels, counted, *begun, *weights)


def splits_evenly(factor, replicas):
    return replicas == 8 and factor.shape[1] == 4 * 128 and factor.shape[0] % 32 == 0


def gather_whole(factors):
    def spot(which):
        def copy(ref, full):
            full[which][...] = ref[...]

        return copy

    return [
        (lax.all_gather(w, "table", axis=0, tiled=True), spot(i)) for i, w in enumerate(factors)
    ]


def gather_blocks(factors, near, corner, after):
    shards = lax.axis_size("table")
    shard_rows = factors[0].shape[0]
    half, lanes = shard_rows // 2, near.shape[2]
    first, second = swap(near, 2), swap(near, 4)
    first, second, corner, after = lax.optimization_barrier((first, second, corner, after))
    corners = [(swap(first[1:, :half], 4), 0), (swap(second[1:, half:], 2), 1)]
    every = tuple(range(1, shards))

    def put(masks, block, core, column, begin, end):
        def copy(ref, full):
            own, here = lax.axis_index("replica"), lax.axis_index("table")
            for i, mask in enumerate(masks):
                start = (here ^ mask) * shard_rows + ((own & 1) ^ core) * half
                at = pl.ds(pl.multiple_of(start, 16), half)
                for which in range(begin, end):
                    full[which][at, column * lanes : (column + 1) * lanes] = ref[
                        i, (which - begin) * half : (which - begin + 1) * half, :
                    ]

        return block, copy

    def put_own(which, masks):
        def copy(ref, full):
            own, here = lax.axis_index("replica"), lax.axis_index("table")
            at = pl.ds(pl.multiple_of(here * shard_rows, 16), shard_rows)
            for column, mask in enumerate(masks):
                columns = pl.ds(pl.multiple_of(((own >> 1) ^ mask) * lanes, lanes), lanes)
                full[which][at, column * lanes : (column + 1) * lanes] = ref[:, columns]

        return factors[which], copy

    early = [put_own(which, (0, 1, 2)) for which in range(2)]
    for column, block in enumerate((near, first, second)):
        early += [put(every, block, 0, column, 0, 2), put(every, swap(block, 1), 1, column, 0, 2)]

    def late(after):
        blocks, after = lax.optimization_barrier(([c[0] for c in corners], after))
        out = [put_own(which, (3,)) for which in range(2)]
        out += [put((1,), corner, 0, 0, 0, 2), put((1,), swap(corner, 1), 1, 0, 0, 2)]
        for block, (_, which) in zip(blocks, corners):
            out.append(put(every[1:], block, 0, 0, which, which + 1))
            out.append(put(every[1:], swap(block, 1), 1, 0, which, which + 1))
        return out, after

    return early, late, after


def reduce_rows(even, odd):
    shards, replicas = lax.axis_size("table"), lax.axis_size("replica")
    kept = even.astype(F32) + swap(odd, 1).astype(F32)
    for masks in mask_stages(replicas)[1:]:
        split = kept.reshape((-1, len(masks) + 1) + kept.shape[1:])
        kept = split[:, 0]
        for i, mask in enumerate(masks):
            kept = kept + swap(split[:, i + 1].astype(BF16), mask).astype(F32)
    kept = kept[0]
    total = kept[0]
    for k in range(1, shards):
        total = total + cross_over(kept[k].astype(BF16), k).astype(F32)
    return total


def finish_kernel(accum, even, odd, update, fresh):
    count, block, width = even.shape
    mine = lax.axis_index("replica")
    for m in range(2 * count):
        own = mine ^ m
        grad = (odd if m % 2 else even)[m // 2]
        square = jnp.sum(grad * grad, axis=1, keepdims=True) * (1.0 / width)
        row = accum[pl.ds(own, 1), :] + row_of(square, block)
        fresh[pl.ds(own, 1), :] = row
        rows = pl.ds(pl.multiple_of(own * block, block), block)
        update[rows, :] = -grad / (jnp.sqrt(column_of(row, block)) + EPSILON)


def finish(accum, even, odd):
    replicas, block = accum.shape
    width = even.shape[2]
    return pl.pallas_call(
        finish_kernel,
        out_shape=(
            jax.ShapeDtypeStruct((replicas * block, width), F32),
            jax.ShapeDtypeStruct((replicas, block), F32),
        ),
        in_specs=[whole()] * 3,
        out_specs=(whole(), whole()),
        compiler_params=pltpu.CompilerParams(vmem_limit_bytes=VMEM_LIMIT),
        name="finish",
    )(accum, even, odd)


def local(
    emb_table,
    row_accum,
    look_rows,
    live_counts,
    bag_order,
    dense_emb,
    labels,
    cross_in,
    cross_out,
    cross_bias,
    head_weight,
):
    shards, replicas = lax.axis_size("table"), lax.axis_size("replica")
    rows = emb_table.shape[0]
    block = rows // replicas
    batch = dense_emb.shape[0]
    factors = (cross_in, cross_out)
    even_split = splits_evenly(cross_in, replicas)

    packed = pack(look_rows, emb_table, shards, replicas)
    parcels = [cross_over(p, k + 1) for k, p in enumerate(packed)]
    bias, head, label_row = (x.reshape(1, -1) for x in (cross_bias, head_weight, labels))
    parcels[0], blocks = lax.optimization_barrier(
        (parcels[0], cut(factors) if even_split else [])
    )
    counts, blocks = lax.optimization_barrier((live_counts, blocks))
    prepared = ready(counts, look_rows, bag_order, dense_emb, head, shards)
    places, info, own_words, lead = prepared
    far, corner = [], []
    if even_split:
        far = jnp.stack([cross_over(blocks[0], k) for k in range(1, shards)])
        corner = cross_over(blocks[1], 1)[None]
    counted = slots(info, own_words, parcels, bag_order.shape[2], rows, shards, replicas)
    pieces, far, counted, own_rows = replica_gather(
        jnp.stack([p[:block] for p in parcels]),
        far,
        counted,
        split_own(emb_table, replicas),
        after=prepared,
    )
    crossed = pool(info, places, counted, own_rows, pieces, lead, head)
    rank = cross_in.shape[1]
    if even_split:
        early, late, crossed = gather_blocks(factors, far, corner, crossed)
        rank = rank - 128
    else:
        early, late = gather_whole(factors), None
    begun = first_step(*crossed, bias, head, *zip(*early), rank)
    last = []
    if late:
        last, begun = late(begun)
    logits, even, odd = dense_step(
        info,
        places,
        *crossed,
        head,
        label_row,
        counted,
        begun,
        [block for block, _ in last],
        [copy for _, copy in last],
        shards,
        replicas,
    )
    grad = reduce_rows(even, odd)
    update, accum = finish(row_accum.reshape(replicas, block), *replica_gather(grad)[0])
    return (logits.reshape(-1), update, accum.reshape(-1))


def solution(mesh):
    placed = (
        P("table", None),
        P("table"),
        P("replica", "table", None, None, None),
        P("replica", None, None),
        P("replica", "table", None),
        P(("replica", "table"), None),
        P(("replica", "table")),
        P("table", None),
        P("table", None),
        P(),
        P(),
    )
    return jax.shard_map(
        local,
        mesh=mesh,
        in_specs=placed,
        out_specs=(P(("replica", "table")), P("table", None), P("table")),
        check_vma=False,
    )
```

```python
import functools

import jax
import jax.numpy as jnp
from jax import lax
from jax.experimental import pallas as pl
from jax.experimental.pallas import tpu as pltpu
from jax.sharding import PartitionSpec as P

EPSILON = 1e-08
F32, BF16 = jnp.float32, jnp.bfloat16
LOW = 32
UNROLL = 8
HOT = 4
CHUNK = 256
ID_BITS = 10
VMEM_LIMIT = 28 * 1024 * 1024
PACK_LIMIT = 60 * 1024 * 1024


def swap(array, mask):
    size = lax.axis_size("replica")
    return lax.ppermute(array, "replica", [(i, i ^ mask) for i in range(size)])


def cross_over(array, mask):
    size = lax.axis_size("table")
    return lax.ppermute(array, "table", [(i, i ^ mask) for i in range(size)])


def mask_stages(size):
    stages, bit = [(1,)], 1
    while (1 << bit) < size:
        if (2 << bit) < size:
            stages.append((1 << bit, 2 << bit, 3 << bit))
            bit += 2
        else:
            stages.append((1 << bit,))
            bit += 1
    return stages


def replica_gather(piece, *beside, after=None):
    held = [piece]
    for masks in reversed(mask_stages(lax.axis_size("replica"))[1:]):
        last = held
        if after is not None:
            last, after = lax.optimization_barrier((held, after))
        sent = [[swap(h, mask) for h in (held if mask != masks[-1] else last)] for mask in masks]
        held = [h for group in [held] + sent for h in group]
    held, *beside = lax.optimization_barrier((held, *beside))
    order = sorted(range(len(held)), key=lambda i: gather_masks(lax.axis_size("replica"))[i])
    even = jnp.stack([held[i] for i in order])
    return (even, swap(even, 1)), *beside


def gather_masks(size):
    masks = [0]
    for group in reversed(mask_stages(size)[1:]):
        masks = masks + [m ^ mask for mask in group for m in masks]
    return masks


def whole(space=pltpu.VMEM):
    return pl.BlockSpec(memory_space=space)


def slot_range(info, shards, j):
    source = lax.axis_index("table") ^ j
    start = jnp.int32(0)
    for s in range(shards):
        start = start + jnp.where(s < source, info[0, s], 0)
    return source, start, info[0, source]


def pack_kernel(shards, look_rows, table, *refs):
    parcels, (ids, done) = refs[:-2], refs[-2:]
    width = table.shape[1]
    capacity = look_rows.shape[4]
    lines = -(-capacity // width)
    block = parcels[0].shape[0] - HOT // 2 * lines
    mine, here = lax.axis_index("replica"), lax.axis_index("table")
    rows = table.at[pl.ds(pl.multiple_of(mine * block, block), block), :]
    copies = [
        pltpu.make_async_copy(rows, parcel.at[:block, :], done.at[i])
        for i, parcel in enumerate(parcels)
    ]
    reads = [
        pltpu.make_async_copy(look_rows.at[0, 0, here ^ (i + 1)], ids.at[i], done.at[shards - 1 + i])
        for i in range(shards - 1)
    ]
    for copy in reads + copies:
        copy.start()
    for i, parcel in enumerate(parcels):
        reads[i].wait()
        for pair in range(HOT // 2):
            for q in range(lines):
                line = block + pair * lines + q
                size = min(width, capacity - q * width)
                if size < width:
                    parcel[line : line + 1, :] = jnp.zeros((1, width), F32)
                at = slice(q * width, q * width + size)
                value = (ids[i, 2 * pair : 2 * pair + 1, at] << ID_BITS) | (
                    ids[i, 2 * pair + 1 : 2 * pair + 2, at]
                )
                parcel[line : line + 1, :size] = value.astype(F32)
    for copy in copies:
        copy.wait()


def pack(look_rows, table, shards, replicas):
    rows, width = table.shape
    capacity = look_rows.shape[4]
    lines = HOT // 2 * -(-capacity // width)
    parcel = jax.ShapeDtypeStruct((rows // replicas + lines, width), F32)
    return pl.pallas_call(
        functools.partial(pack_kernel, shards),
        out_shape=[parcel] * (shards - 1),
        in_specs=[whole(pltpu.HBM)] * 2,
        out_specs=[whole()] * (shards - 1),
        scratch_shapes=[
            pltpu.VMEM((shards - 1,) + look_rows.shape[3:], jnp.int32),
            pltpu.SemaphoreType.DMA((2 * shards - 2,)),
        ],
        compiler_params=pltpu.CompilerParams(vmem_limit_bytes=PACK_LIMIT),
        name="pack",
    )(look_rows, table)


def cut_kernel(first, second, near, corner, done):
    half, lanes = near.shape[0] // 2, near.shape[1]
    mine = lax.axis_index("replica")
    copies = []
    for out, mask in ((near, 0), (corner, 3)):
        for i, factor in enumerate((first, second)):
            at = (
                pl.ds(pl.multiple_of((mine & 1) * half, 16), half),
                pl.ds(pl.multiple_of(((mine >> 1) ^ mask) * lanes, lanes), lanes),
            )
            into = out.at[i * half : (i + 1) * half, :]
            copies.append(pltpu.make_async_copy(factor.at[at], into, done.at[len(copies)]))
    for copy in copies:
        copy.start()
    for copy in copies:
        copy.wait()


def cut(factors):
    rows = factors[0].shape[0]
    return pl.pallas_call(
        cut_kernel,
        out_shape=[jax.ShapeDtypeStruct((r, 128), BF16) for r in (rows, rows)],
        in_specs=[whole(pltpu.HBM)] * 2,
        out_specs=[whole()] * 2,
        scratch_shapes=[pltpu.SemaphoreType.DMA((4,))],
        compiler_params=pltpu.CompilerParams(vmem_limit_bytes=PACK_LIMIT),
        name="cut",
    )(*factors)


def quotient(value, divisor, below):
    shift = 19
    factor = (1 << shift) // divisor + 1
    assert below * factor < 1 << 31
    assert all((v * factor) >> shift == v // divisor for v in range(below))
    return lax.shift_right_logical(value * factor, shift)


def split_rows(value):
    high = value.astype(BF16)
    return high, (value - high.astype(F32)).astype(BF16)


def ready_kernel(
    shards, live_counts, look_rows, bag_order, dense, head, places, info, words, lead
):
    batch, width = dense.shape
    capacity = look_rows.shape[4]
    bags = bag_order.shape[2]
    here = lax.axis_index("table")
    order = bag_order[0]
    sample = quotient(order, bags // batch, bags)
    dest = (order - sample * (bags // batch)) * batch + sample
    for q in range(bags // CHUNK):
        one = dest[:, q * CHUNK : q * CHUNK + CHUNK // 2]
        two = dest[:, q * CHUNK + CHUNK // 2 : (q + 1) * CHUNK]
        places[:, q * CHUNK // 2 : (q + 1) * CHUNK // 2] = one | (two << 16)
    lane = lax.broadcasted_iota(jnp.int32, info.shape, 1)
    counts = jnp.zeros(info.shape, jnp.int32)
    for s in range(shards):
        counts = jnp.where(lane == s, live_counts[0, here, s], counts)
    info[...] = counts
    words[...] = jnp.zeros_like(words)
    for pair in range(HOT // 2):
        words[pair : pair + 1, :capacity] = (
            look_rows[0, 0, here, 2 * pair : 2 * pair + 1, :] << ID_BITS
        ) | look_rows[0, 0, here, 2 * pair + 1 : 2 * pair + 2, :]
    lead[:, :width] = dense[...]
    lead[:, width:] = (dense[...].astype(F32) * head[:, :width]).astype(BF16)


def ready(live_counts, look_rows, bag_order, dense, head, shards):
    batch, width = dense.shape
    bags = bag_order.shape[2]
    padded = -(-look_rows.shape[4] // width) * width
    return pl.pallas_call(
        functools.partial(ready_kernel, shards),
        out_shape=[
            jax.ShapeDtypeStruct((1, bags // 2), jnp.int32),
            jax.ShapeDtypeStruct((1, 128), jnp.int32),
            jax.ShapeDtypeStruct((8, padded), jnp.int32),
            jax.ShapeDtypeStruct((batch, 2 * width), BF16),
        ],
        in_specs=[whole(pltpu.SMEM)] + [whole()] * 4,
        out_specs=[whole()] * 4,
        compiler_params=pltpu.CompilerParams(vmem_limit_bytes=VMEM_LIMIT),
        cost_estimate=pl.CostEstimate(flops=1000, bytes_accessed=1000, transcendentals=0),
        name="ready",
    )(live_counts, look_rows, bag_order, dense, head)


def own_kernel(replicas, table, own):
    rows, width = table.shape
    block = rows // replicas
    mine = lax.axis_index("replica")
    for m in range(replicas):
        there = pl.ds(pl.multiple_of((mine ^ m) * block, block), block)
        at = slice(m * block, (m + 1) * block)
        own[at, :width], own[at, width:] = split_rows(table[there, :])


def split_own(table, replicas):
    rows, width = table.shape
    return pl.pallas_call(
        functools.partial(own_kernel, replicas),
        out_shape=jax.ShapeDtypeStruct((rows, 2 * width), BF16),
        in_specs=[whole()],
        out_specs=whole(),
        compiler_params=pltpu.CompilerParams(vmem_limit_bytes=VMEM_LIMIT),
        cost_estimate=pl.CostEstimate(flops=1000, bytes_accessed=1000, transcendentals=0),
        name="split_own",
    )(table)


def slots_kernel(shards, replicas, bags, info, own, *refs):
    parcels, (counted, shifted, words) = refs[: shards - 1], refs[shards - 1 :]
    width = parcels[0].shape[1]
    padded = own.shape[1]
    rows = counted.shape[1]
    block = rows // replicas
    field = (1 << ID_BITS) - 1
    slot = lax.broadcasted_iota(jnp.int32, (8, bags), 1)
    ranges = [slot_range(info, shards, j) for j in range(shards)]
    shifted[...] = jnp.zeros_like(shifted)
    for j, (source, start, live) in enumerate(ranges):
        if j == 0:
            shifted[:, :padded] = own[...]
        else:
            for pair in range(HOT // 2):
                for q in range(padded // width):
                    line = block + pair * (padded // width) + q
                    shifted[pair : pair + 1, q * width : (q + 1) * width] = parcels[j - 1][
                        line : line + 1, :
                    ].astype(jnp.int32)
        moved = pltpu.roll(shifted[...], start, 1)[:, :bags]
        inside = (slot >= start) & (slot < start + live)
        words[...] = jnp.where(inside, moved, words[...] if j else 0)

    flip = lax.axis_index("replica") * block
    low = lax.broadcasted_iota(jnp.int32, (LOW, CHUNK), 0)
    for source, start, live in ranges:

        def pair(q, _, start=start, live=live, source=source):
            at = pl.ds(pl.multiple_of(q * CHUNK, CHUNK), CHUNK)
            place = q * CHUNK + lax.broadcasted_iota(jnp.int32, (1, CHUNK), 1) - start
            inside = (place >= 0) & (place < live)
            lows, highs = [], []
            for h in range(HOT):
                word = words[h // 2 : h // 2 + 1, at]
                row = (lax.shift_right_logical(word, (h % 2) * ID_BITS) & field) ^ flip
                row = jnp.where(inside, row, -1)
                highs.append(lax.shift_right_arithmetic(row, LOW.bit_length() - 1))
                lows.append((low == (row & (LOW - 1))).astype(F32).astype(BF16))
            for b in range(rows // LOW):
                count = None
                for h in range(HOT):
                    hit = (highs[h] == b).astype(F32).astype(BF16)
                    term = lows[h] * hit
                    count = term if count is None else count + term
                counted[q + source, b * LOW : (b + 1) * LOW, :] = count
            return 0

        lax.fori_loop(start // CHUNK, (start + live + CHUNK - 1) // CHUNK, pair, 0)


def slots(info, own, parcels, bags, rows, shards, replicas):
    pairs = bags // CHUNK + shards - 1
    return pl.pallas_call(
        functools.partial(slots_kernel, shards, replicas, bags),
        out_shape=jax.ShapeDtypeStruct((pairs, rows, CHUNK), BF16),
        in_specs=[whole(pltpu.SMEM)] + [whole()] * (1 + len(parcels)),
        out_specs=whole(),
        scratch_shapes=[
            pltpu.VMEM((8, bags + own.shape[1]), jnp.int32),
            pltpu.VMEM((8, bags), jnp.int32),
        ],
        compiler_params=pltpu.CompilerParams(vmem_limit_bytes=VMEM_LIMIT),
        cost_estimate=pl.CostEstimate(flops=1000, bytes_accessed=1000, transcendentals=0),
        name="slots",
    )(info, own, *parcels)


def pool_kernel(
    shards, info, places, counted, own, even, odd, lead, head, cross, scaled, table, sums, pooled
):
    width = lead.shape[1] // 2
    block = even.shape[2]
    batch = lead.shape[0]
    half = CHUNK // 2
    for m in range(2 * even.shape[0]):
        at = slice(m * block, (m + 1) * block)
        for k in range(1, shards):
            value = (odd if m % 2 else even)[m // 2, k - 1]
            table[k - 1, at, :width], table[k - 1, at, width:] = split_rows(value)
    sums[...] = jnp.zeros_like(sums)
    for j in range(shards):
        source, start, live = slot_range(info, shards, j)
        found_in = own if j == 0 else table.at[j - 1]

        def pair(q, _, found_in=found_in, source=source):
            at = pl.ds(pl.multiple_of(q * CHUNK, CHUNK), CHUNK)
            found = lax.dot_general(
                counted[q + source], found_in[...], (((0,), (0,)), ((), ())), preferred_element_type=F32
            )
            sums[at, :] += found[:, :width] + found[:, width:]
            return 0

        lax.fori_loop(start // CHUNK, (start + live + CHUNK - 1) // CHUNK, pair, 0)

    def group(i, _):
        k0 = i * UNROLL
        k0 = k0 + lax.div(k0, half) * half
        for u in range(UNROLL):
            word = places[0, i * UNROLL + u]
            pooled[pl.ds(word & 0xFFFF, 1), :] = sums[pl.ds(k0 + u, 1), :]
            pooled[pl.ds(lax.shift_right_logical(word, 16), 1), :] = sums[pl.ds(k0 + u + half, 1), :]
        return 0

    lax.fori_loop(0, sums.shape[0] // (2 * UNROLL), group, 0)
    cross[:, :width] = lead[:, :width]
    scaled[:, :width] = lead[:, width:]
    for f in range(1, cross.shape[1] // width):
        at = slice(f * width, (f + 1) * width)
        value = pooled[(f - 1) * batch : f * batch, :].astype(BF16)
        cross[:, at] = value
        scaled[:, at] = (value.astype(F32) * head[:, at]).astype(BF16)


def pool(info, places, counted, own, pieces, lead, head):
    rows, width = own.shape[0], own.shape[1] // 2
    bags = 2 * places.shape[1]
    shards = pieces[0].shape[1] + 1
    smem = whole(pltpu.SMEM)
    return pl.pallas_call(
        functools.partial(pool_kernel, shards),
        out_shape=[jax.ShapeDtypeStruct((lead.shape[0], head.shape[1]), BF16)] * 2,
        in_specs=[smem, smem] + [whole()] * 6,
        out_specs=[whole()] * 2,
        scratch_shapes=[
            pltpu.VMEM((shards - 1, rows, 2 * width), BF16),
            pltpu.VMEM((bags, width), F32),
            pltpu.VMEM((bags, width), F32),
        ],
        compiler_params=pltpu.CompilerParams(vmem_limit_bytes=VMEM_LIMIT),
        cost_estimate=pl.CostEstimate(flops=1000, bytes_accessed=1000, transcendentals=0),
        name="pool",
    )(info, places, counted, own, *pieces, lead, head)


def column_of(row, size):
    eye = lax.broadcasted_iota(jnp.int32, (size, size), 0) == lax.broadcasted_iota(
        jnp.int32, (size, size), 1
    )
    return jnp.sum(jnp.where(eye, jnp.broadcast_to(row, (size, size)), 0.0), axis=1, keepdims=True)


def row_of(column, size):
    eye = lax.broadcasted_iota(jnp.int32, (size, size), 0) == lax.broadcasted_iota(
        jnp.int32, (size, size), 1
    )
    return jnp.sum(
        jnp.where(eye, jnp.broadcast_to(column, (size, size)), 0.0), axis=0, keepdims=True
    )


def first_kernel(copies, cross, scaled, bias, head, *refs):
    weights, (grads, logit, full_in, full_out) = refs[: len(copies)], refs[len(copies) :]
    for ref, copy in zip(weights, copies):
        copy(ref, (full_in, full_out))
    add_rank(cross, scaled, head, full_in, full_out, bias, None, grads, logit)


def add_rank(cross, scaled, head, full_in, full_out, bias, before, grads, logit):
    batch, features = cross.shape
    width = logit.shape[1]
    across = (((1,), (1,)), ((), ()))
    hidden = jnp.dot(cross[...], full_in[...], preferred_element_type=F32).astype(BF16)
    back = jnp.dot(scaled[...], full_out[...], preferred_element_type=F32).astype(BF16)
    step = 3 * width if (features // width) % 3 == 0 else width
    total = jnp.zeros((batch, width), F32) if before is None else before[1][...]
    for n in range(features // step):
        at = slice(n * step, (n + 1) * step)
        mixed = lax.dot_general(hidden, full_out[at, :], across, preferred_element_type=F32)
        if bias is not None:
            mixed = mixed + bias[:, at] + 1.0
        gain = head[:, at] * mixed
        term = cross[:, at].astype(F32) * gain
        grad = gain + lax.dot_general(back, full_in[at, :], across, preferred_element_type=F32)
        for p in range(step // width):
            part = slice(p * width, (p + 1) * width)
            total = total + term[:, part]
            f = n * (step // width) + p
            if f > 0:
                rows = slice((f - 1) * batch, f * batch)
                grads[rows, :] = grad[:, part] + (0.0 if before is None else before[0][rows, :])
    logit[...] = total


def first_step(cross, scaled, bias, head, weights, copies, rank):
    batch, features = cross.shape
    width = 128
    return pl.pallas_call(
        functools.partial(first_kernel, copies),
        out_shape=(
            jax.ShapeDtypeStruct((features // width * batch - batch, width), F32),
            jax.ShapeDtypeStruct((batch, width), F32),
        ),
        in_specs=[whole()] * (4 + len(weights)),
        out_specs=(whole(), whole()),
        scratch_shapes=[pltpu.VMEM((features, rank), BF16)] * 2,
        compiler_params=pltpu.CompilerParams(vmem_limit_bytes=VMEM_LIMIT),
        cost_estimate=pl.CostEstimate(
            flops=2 * 10**9, bytes_accessed=20 * 10**6, transcendentals=0
        ),
        name="first",
    )(cross, scaled, bias, head, *weights)


def dense_kernel(shards, replicas, copies, info, places, cross, scaled, head, labels, counted, *refs):
    begun, partial = refs[:2]
    weights = refs[2 : 2 + len(copies)]
    logits, even, odd, full_in, full_out, grads, logit, slots, narrow, total, spots, done = refs[
        2 + len(copies) :
    ]
    batch = cross.shape[0]
    width = slots.shape[1]
    bags = grads.shape[0]
    rows = total.shape[2]
    here = lax.axis_index("table")
    fetch = pltpu.make_async_copy(places, spots, done)
    fetch.start()

    if copies:
        for ref, copy in zip(weights, copies):
            copy(ref, (full_in, full_out))
        add_rank(cross, scaled, head, full_in, full_out, None, (begun, partial), grads, logit)
    else:
        grads[...] = begun[...]
        logit[...] = partial[...]
    sums = jnp.sum(logit[...], axis=1, keepdims=True)
    logits[...] = row_of(sums, batch)
    lean = jax.nn.sigmoid(sums) - column_of(labels[...].astype(F32), batch)
    for f in range(bags // batch):
        at = slice(f * batch, (f + 1) * batch)
        grads[at, :] = (grads[at, :] * lean).astype(BF16).astype(F32)

    half = CHUNK // 2
    chunks = bags // CHUNK

    def gather(q):
        for i in range(half):
            word = spots[0, q * half + i]
            slots[i : i + 1, :] = grads[pl.ds(word & 0xFFFF, 1), :]
            slots[i + half : i + half + 1, :] = grads[pl.ds(lax.shift_right_logical(word, 16), 1), :]

    def shard_of(k):
        end, shard = jnp.int32(0), jnp.int32(0)
        for s in range(shards - 1):
            end = end + info[0, s]
            shard = shard + jnp.where(k >= end, 1, 0)
        return shard

    def add(q, shard):
        place = here ^ shard
        found = lax.dot_general(
            narrow[...], counted[q + shard], (((0,), (1,)), ((), ())), preferred_element_type=F32
        )
        start = slot_range(info, shards, place)[1]
        total[place] = found + jnp.where(start < q * CHUNK, total[place], 0.0)

    fetch.wait()
    gather(0)

    def chunk(q, _):
        narrow[...] = slots[...].astype(BF16)
        shard = shard_of(q * CHUNK)
        add(q, shard)
        gather(jnp.minimum(q + 1, chunks - 1))

        def more(s, _):
            add(q, s)
            return 0

        lax.fori_loop(shard + 1, shard_of((q + 1) * CHUNK - 1) + 1, more, 0)
        return 0

    lax.fori_loop(0, chunks, chunk, 0)
    block = rows // replicas
    for j in range(shards):
        for m in range(replicas):
            sums = total[j, :, m * block : (m + 1) * block].T
            (odd if m % 2 else even)[m // 2, j] = sums.astype(BF16)


def dense_step(
    info, places, cross, scaled, head, labels, counted, begun, weights, copies, shards, replicas
):
    batch, features = cross.shape
    width = 128
    bags = begun[0].shape[0]
    rows = counted.shape[1]
    half = jax.ShapeDtypeStruct((replicas // 2, shards, rows // replicas, width), BF16)
    smem = whole(pltpu.SMEM)
    part = pltpu.VMEM((features, width) if copies else (16, width), BF16)
    return pl.pallas_call(
        functools.partial(dense_kernel, shards, replicas, copies),
        out_shape=(jax.ShapeDtypeStruct((1, batch), F32), half, half),
        in_specs=[smem] + [whole()] * (8 + len(weights)),
        out_specs=(whole(), whole(), whole()),
        scratch_shapes=[
            part,
            part,
            pltpu.VMEM((bags, width), F32),
            pltpu.VMEM((batch, width), F32),
            pltpu.VMEM((CHUNK, width), F32),
            pltpu.VMEM((CHUNK, width), BF16),
            pltpu.VMEM((shards, width, rows), F32),
            pltpu.SMEM(places.shape, jnp.int32),
            pltpu.SemaphoreType.DMA(()),
        ],
        compiler_params=pltpu.CompilerParams(vmem_limit_bytes=VMEM_LIMIT),
        cost_estimate=pl.CostEstimate(
            flops=2 * 10**9, bytes_accessed=20 * 10**6, transcendentals=0
        ),
        name="dense",
    )(info, places, cross, scaled, head, labels, counted, *begun, *weights)


def splits_evenly(factor, replicas):
    return replicas == 8 and factor.shape[1] == 4 * 128 and factor.shape[0] % 32 == 0


def gather_whole(factors):
    def spot(which):
        def copy(ref, full):
            full[which][...] = ref[...]

        return copy

    return [
        (lax.all_gather(w, "table", axis=0, tiled=True), spot(i)) for i, w in enumerate(factors)
    ]


def gather_blocks(factors, near, corner, after):
    shards = lax.axis_size("table")
    shard_rows = factors[0].shape[0]
    half, lanes = shard_rows // 2, near.shape[2]
    first, second = swap(near, 2), swap(near, 4)
    first, second, corner, after = lax.optimization_barrier((first, second, corner, after))
    corners = [(swap(first[1:, :half], 4), 0), (swap(second[1:, half:], 2), 1)]
    every = tuple(range(1, shards))

    def put(masks, block, core, column, begin, end):
        def copy(ref, full):
            own, here = lax.axis_index("replica"), lax.axis_index("table")
            for i, mask in enumerate(masks):
                start = (here ^ mask) * shard_rows + ((own & 1) ^ core) * half
                at = pl.ds(pl.multiple_of(start, 16), half)
                for which in range(begin, end):
                    full[which][at, column * lanes : (column + 1) * lanes] = ref[
                        i, (which - begin) * half : (which - begin + 1) * half, :
                    ]

        return block, copy

    def put_own(which, masks):
        def copy(ref, full):
            own, here = lax.axis_index("replica"), lax.axis_index("table")
            at = pl.ds(pl.multiple_of(here * shard_rows, 16), shard_rows)
            for column, mask in enumerate(masks):
                columns = pl.ds(pl.multiple_of(((own >> 1) ^ mask) * lanes, lanes), lanes)
                full[which][at, column * lanes : (column + 1) * lanes] = ref[:, columns]

        return factors[which], copy

    early = [put_own(which, (0, 1, 2)) for which in range(2)]
    for column, block in enumerate((near, first, second)):
        early += [put(every, block, 0, column, 0, 2), put(every, swap(block, 1), 1, column, 0, 2)]

    def late(after):
        blocks, after = lax.optimization_barrier(([c[0] for c in corners], after))
        out = [put_own(which, (3,)) for which in range(2)]
        out += [put((1,), corner, 0, 0, 0, 2), put((1,), swap(corner, 1), 1, 0, 0, 2)]
        for block, (_, which) in zip(blocks, corners):
            out.append(put(every[1:], block, 0, 0, which, which + 1))
            out.append(put(every[1:], swap(block, 1), 1, 0, which, which + 1))
        return out, after

    return early, late, after


def reduce_rows(even, odd):
    shards, replicas = lax.axis_size("table"), lax.axis_size("replica")
    kept = even.astype(F32) + swap(odd, 1).astype(F32)
    for masks in mask_stages(replicas)[1:]:
        split = kept.reshape((-1, len(masks) + 1) + kept.shape[1:])
        kept = split[:, 0]
        for i, mask in enumerate(masks):
            kept = kept + swap(split[:, i + 1].astype(BF16), mask).astype(F32)
    kept = kept[0]
    total = kept[0]
    for k in range(1, shards):
        total = total + cross_over(kept[k].astype(BF16), k).astype(F32)
    return total


def finish_kernel(accum, even, odd, update, fresh):
    count, block, width = even.shape
    mine = lax.axis_index("replica")
    for m in range(2 * count):
        own = mine ^ m
        grad = (odd if m % 2 else even)[m // 2]
        square = jnp.sum(grad * grad, axis=1, keepdims=True) * (1.0 / width)
        row = accum[pl.ds(own, 1), :] + row_of(square, block)
        fresh[pl.ds(own, 1), :] = row
        rows = pl.ds(pl.multiple_of(own * block, block), block)
        update[rows, :] = -grad / (jnp.sqrt(column_of(row, block)) + EPSILON)


def finish(accum, even, odd):
    replicas, block = accum.shape
    width = even.shape[2]
    return pl.pallas_call(
        finish_kernel,
        out_shape=(
            jax.ShapeDtypeStruct((replicas * block, width), F32),
            jax.ShapeDtypeStruct((replicas, block), F32),
        ),
        in_specs=[whole()] * 3,
        out_specs=(whole(), whole()),
        compiler_params=pltpu.CompilerParams(vmem_limit_bytes=VMEM_LIMIT),
        name="finish",
    )(accum, even, odd)


def local(
    emb_table,
    row_accum,
    look_rows,
    live_counts,
    bag_order,
    dense_emb,
    labels,
    cross_in,
    cross_out,
    cross_bias,
    head_weight,
):
    shards, replicas = lax.axis_size("table"), lax.axis_size("replica")
    rows = emb_table.shape[0]
    block = rows // replicas
    batch = dense_emb.shape[0]
    factors = (cross_in, cross_out)
    even_split = splits_evenly(cross_in, replicas)

    packed = pack(look_rows, emb_table, shards, replicas)
    parcels = [cross_over(p, k + 1) for k, p in enumerate(packed)]
    bias, label_row = cross_bias.reshape(1, -1), labels.reshape(1, -1)
    parcels[0], blocks = lax.optimization_barrier(
        (parcels[0], cut(factors) if even_split else [])
    )
    counts, head, blocks = lax.optimization_barrier((live_counts, head_weight, blocks))
    head = head.reshape(1, -1)
    prepared = ready(counts, look_rows, bag_order, dense_emb, head, shards)
    places, info, own_words, lead = prepared
    far, corner = [], []
    if even_split:
        far = jnp.stack([cross_over(blocks[0], k) for k in range(1, shards)])
        corner = cross_over(blocks[1], 1)[None]
    counted = slots(info, own_words, parcels, bag_order.shape[2], rows, shards, replicas)
    pieces, far, counted = replica_gather(
        jnp.stack([p[:block] for p in parcels]),
        far,
        counted,
        after=prepared,
    )
    own_rows = split_own(emb_table, replicas)
    crossed = pool(info, places, counted, own_rows, pieces, lead, head)
    rank = cross_in.shape[1]
    if even_split:
        early, late, crossed = gather_blocks(factors, far, corner, crossed)
        rank = rank - 128
    else:
        early, late = gather_whole(factors), None
    begun = first_step(*crossed, bias, head, *zip(*early), rank)
    last = []
    if late:
        last, begun = late(begun)
    logits, even, odd = dense_step(
        info,
        places,
        *crossed,
        head,
        label_row,
        counted,
        begun,
        [block for block, _ in last],
        [copy for _, copy in last],
        shards,
        replicas,
    )
    grad = reduce_rows(even, odd)
    update, accum = finish(row_accum.reshape(replicas, block), *replica_gather(grad)[0])
    return (logits.reshape(-1), update, accum.reshape(-1))


def solution(mesh):
    placed = (
        P("table", None),
        P("table"),
        P("replica", "table", None, None, None),
        P("replica", None, None),
        P("replica", "table", None),
        P(("replica", "table"), None),
        P(("replica", "table")),
        P("table", None),
        P("table", None),
        P(),
        P(),
    )
    return jax.shard_map(
        local,
        mesh=mesh,
        in_specs=placed,
        out_specs=(P(("replica", "table")), P("table", None), P("table")),
        check_vma=False,
    )
```
